128 devices in a mesh: tp: 8 (over y, core), dp: 16 (over z, x).
Axes of the slice: x: 4, y: 4, z: 4, core: 2. Of those that a mesh axis runs over, the one named last changes fastest.
Arguments:
- hidden_rows: bfloat16 [16384, 3, 4096], P('dp', None, 'tp'), may hold values from -6 to 6
- target_rows: bfloat16 [16384, 4096], P('dp', 'tp')
- row_counts: int32 [2048], P('dp'), may hold values from 1 to 8, as said below
- seq_slot: int32 [2048], P('dp'), may hold values from 0 to 2047, as said below
- joining_weight: bfloat16 [3, 4096, 4096], P(None, 'tp'), may hold values from -4 to 4
- norm_gain: float32 [4096], replicated, may hold values from 0.1 to 1.9
Outputs:
- seq_loss: float32 [2048], P('dp')
- serving_weight: bfloat16 [3, 4096, 4096], P(None, ('tp', 'dp'))
- column_scale: float32 [4096], replicated
The draws below stay inside these ranges and needn't reach their ends.
Inputs may be any that keep to these rules, and one draw needn't show every extreme that they name: `seq_slot`: the slots form owners of 128 slots each (owner = slot // 128); the requests of replica d for one owner hold exactly that owner's slots d * 8 to d * 8 + 7, each once. `row_counts`: one owner, drawn anew, gets 8 rows from every request of every replica. For every other owner, the requests of one replica with slots d * 8 + 2m and d * 8 + 2m + 1 have counts that sum to 8. So every replica uses exactly 544 rows.
All inputs are finite; a program needn't handle non-finite values. Where the reference program divides by a largest or mean magnitude, that divisor is 1e-20 or more.
Results may differ from the reference program's by a relative error of at most 0.02.
Values may be sent and summed in bfloat16 or wider, within the bound.
A program may use at most 128 MiB of HBM per device.

```python
import jax
import jax.numpy as jnp
from jax import lax

FEAT = 4096
OUT = 4096
REQS = 128
MOST = 8
ROWS = 1024
LIVE = 544
TOTAL_ROWS = 16384
SEQS = 2048
N_DP = 16


def owner_plan(key):
    share = REQS // N_DP
    heavy = jax.random.randint(jax.random.fold_in(key, 11), (), 0, N_DP)
    replica_keys = jax.random.split(jax.random.fold_in(key, 12), N_DP)
    orders = jax.vmap(lambda k: jax.random.permutation(k, REQS))(replica_keys).astype(jnp.int32)
    owner = orders // share
    within = orders % share
    replica = jnp.arange(N_DP, dtype=jnp.int32)[:, None]
    slots = owner * REQS + replica * share + within
    halves = jax.random.randint(jax.random.fold_in(key, 13), (N_DP, N_DP, share // 2), 1, MOST)
    table = jnp.stack([halves, MOST - halves], axis=-1).reshape(N_DP, N_DP * share)
    table_owner = (jnp.arange(N_DP * share, dtype=jnp.int32) // share)[None, :]
    table = jnp.where(table_owner == heavy, MOST, table)
    counts = jnp.take_along_axis(table, orders, axis=1)
    return (slots.reshape(-1).astype(jnp.int32), counts.reshape(-1).astype(jnp.int32))


def draw_seq_slot(key, part):
    return owner_plan(key)[0]


def draw_row_counts(key, part):
    return owner_plan(key)[1]


def draw_target_rows(key, part):
    key = jax.random.fold_in(key, 5)
    base_key, scale_key = jax.random.split(key)
    base = jax.random.normal(base_key, (TOTAL_ROWS, OUT), jnp.float32)
    spread = jnp.exp(jax.random.uniform(scale_key, (TOTAL_ROWS, 1), jnp.float32, jnp.log(0.3), jnp.log(3.0)))
    return jnp.clip(base * spread, -12.0, 12.0).astype(jnp.bfloat16)


def draw_joining_weight(key, part):
    key = jax.random.fold_in(key, 7)
    base_key, rough_key = jax.random.split(key)
    column = jnp.arange(OUT, dtype=jnp.float32) / (OUT - 1)
    rough = jnp.exp(jax.random.uniform(rough_key, (OUT,), jnp.float32, jnp.log(0.7), jnp.log(1.4)))
    base = jnp.clip(jax.random.normal(base_key, (3, FEAT, OUT), jnp.float32), -6.0, 6.0)
    rise = jnp.exp(column * jnp.log(5.0))
    scale = (rise * rough)[None, None, :] / jnp.sqrt(3.0 * FEAT)
    return jnp.clip(base * scale, -4.0, 4.0).astype(jnp.bfloat16)


def block_levels(rng, shape, pieces, low, largest):
    level, own = 1.0, jax.random.fold_in(rng, 6)
    for position, parts in pieces:
        steps = jnp.exp(jax.random.uniform(jax.random.fold_in(own, position), (parts,), jnp.float32, low / len(pieces), largest / len(pieces)))
        level = level * jnp.repeat(steps, shape[position] // parts).reshape([-1 if axis == position else 1 for axis in range(len(shape))])
    return level


def bell_draw(rng, dims, width, reach, cuts=(), kind=jnp.bfloat16):
    loudness = block_levels(rng, dims, cuts, -0.22, 0.18) if cuts else 1.0
    array = jax.random.normal(rng, dims, jnp.float32) * width * loudness
    return jnp.minimum(jnp.maximum(array, -reach), reach).astype(kind)


def setup_inputs(seed: int = 0) -> dict:
    seeds = jax.random.split(jax.random.key(seed), 7)
    hidden_rows = bell_draw(seeds[0], (TOTAL_ROWS, 3, FEAT), 1.0, 6.0, ((0, 16), (2, 8)))
    target_rows = draw_target_rows(jax.random.fold_in(seeds[6], 71), 0)
    row_counts = draw_row_counts(jax.random.fold_in(seeds[6], 71), 0)
    seq_slot = draw_seq_slot(jax.random.fold_in(seeds[6], 71), 0)
    joining_weight = draw_joining_weight(jax.random.fold_in(seeds[6], 71), 0)
    norm_gain = jnp.clip(1.0 + 0.18 * jax.random.normal(seeds[5], (OUT,), jnp.float32), 0.1, 1.9)
    return {"hidden_rows": hidden_rows, "target_rows": target_rows, "row_counts": row_counts, "seq_slot": seq_slot, "joining_weight": joining_weight, "norm_gain": norm_gain}


learn_rate = 1.0

def compact_rows(counts, live_rows, most):
    ends = jnp.cumsum(counts).astype(jnp.int32)
    starts = (ends - counts).astype(jnp.int32)
    places = jnp.arange(live_rows, dtype=jnp.int32)
    request = lax.optimization_barrier(jnp.sum((ends[None, :] <= places[:, None]).astype(jnp.int32), axis=1)).astype(jnp.int32)
    offset = places - starts[request]
    return (request, (request * most + offset).astype(jnp.int32))

def reference(hidden_rows, target_rows, row_counts, seq_slot, joining_weight, norm_gain):
    flat_weight = joining_weight.reshape(3 * FEAT, OUT)
    seq_ids = jnp.arange(SEQS, dtype=jnp.int32)

    def replica(carry, index):
        grad, losses = carry
        counts = lax.dynamic_slice_in_dim(row_counts, index * REQS, REQS)
        slots = lax.dynamic_slice_in_dim(seq_slot, index * REQS, REQS)
        request, source_row = compact_rows(counts, LIVE, MOST)
        block = lax.dynamic_slice_in_dim(hidden_rows, index * ROWS, ROWS)
        inputs = block[source_row].reshape(LIVE, 3 * FEAT)
        wanted = lax.dynamic_slice_in_dim(target_rows, index * ROWS, ROWS)[source_row].astype(jnp.float32)
        joined = jnp.dot(inputs, flat_weight, preferred_element_type=jnp.float32)
        inv_rms = lax.rsqrt(lax.optimization_barrier(jnp.mean(joined * joined, axis=1)) + 1e-05)
        normed = joined * inv_rms[:, None] * norm_gain[None, :]
        err = normed - wanted
        row_loss = lax.optimization_barrier(jnp.mean(err * err, axis=1))
        count_row = counts[request].astype(jnp.float32)
        slot_row = slots[request]
        terms = row_loss / count_row
        partial_value = lax.optimization_barrier(jnp.sum(jnp.where(slot_row[:, None] == seq_ids[None, :], terms[:, None], 0.0), axis=0))
        d_normed = err * (2.0 / (OUT * count_row))[:, None]
        inner = lax.optimization_barrier(jnp.sum(norm_gain[None, :] * d_normed * joined, axis=1))
        d_joined = (inv_rms[:, None] * norm_gain[None, :] * d_normed - joined * (inv_rms ** 3 * inner / OUT)[:, None]).astype(jnp.bfloat16)
        term = lax.dot_general(inputs, d_joined, (((0,), (0,)), ((), ())), preferred_element_type=jnp.float32)
        term = lax.optimization_barrier(term.astype(jnp.bfloat16)).astype(jnp.float32)
        return ((grad + term, losses + partial_value), None)
    start = (jnp.zeros((3 * FEAT, OUT), jnp.float32), jnp.zeros((SEQS,), jnp.float32))
    (grad, losses), _ = lax.scan(replica, start, jnp.arange(N_DP, dtype=jnp.int32))
    updated = flat_weight.astype(jnp.float32) - learn_rate * grad
    column_scale = lax.optimization_barrier(jnp.max(jnp.abs(updated), axis=0)) + 1e-06
    serving_weight = (updated / column_scale[None, :]).astype(jnp.bfloat16).reshape(3, FEAT, OUT)
    return (losses, serving_weight, column_scale)
```

```python
import jax
import jax.numpy as jnp
from jax import lax
from jax.sharding import PartitionSpec as P

learn_rate = 1.0


def compact_plan(row_counts, slot_rows, live):
    requests = row_counts.shape[0]
    most = slot_rows // requests
    count_row = jnp.repeat(row_counts, most)
    used = jnp.arange(slot_rows, dtype=jnp.int32) % most < count_row
    rank = jnp.cumsum(used.astype(jnp.int32)) - 1
    places = jnp.arange(live, dtype=jnp.int32)
    picked = (rank[None, :] == places[:, None]) & used[None, :]
    return count_row, picked


def shards(hidden_rows, target_rows, row_counts, seq_slot, joining_weight, norm_gain):
    n_dp = lax.axis_size("dp")
    dp_index = lax.axis_index("dp")
    tp_index = lax.axis_index("tp")
    requests = row_counts.shape[0]
    slot_rows = hidden_rows.shape[0]
    most = slot_rows // requests
    feat_local = hidden_rows.shape[2]
    out_local = target_rows.shape[1]
    out_cols = joining_weight.shape[2]
    sub_rows = feat_local // n_dp
    live = (n_dp - 1) * (requests // n_dp // 2) * most + (requests // n_dp) * most
    count_row, picked = compact_plan(row_counts, slot_rows, live)
    chosen = picked.astype(jnp.bfloat16)
    inputs = [
        jnp.dot(chosen, hidden_rows[:, l, :], preferred_element_type=jnp.float32).astype(jnp.bfloat16)
        for l in range(3)
    ]
    wanted = jnp.dot(chosen, target_rows, preferred_element_type=jnp.float32)
    count_live = jnp.sum(jnp.where(picked, count_row[None, :], 0), axis=1).astype(jnp.float32)
    flat_inputs = jnp.concatenate(inputs, axis=1)
    flat_weight = joining_weight.reshape(3 * feat_local, out_cols)
    partial_joined = jnp.dot(flat_inputs, flat_weight, preferred_element_type=jnp.float32)
    joined = lax.psum_scatter(
        partial_joined.astype(jnp.bfloat16), "tp", scatter_dimension=1, tiled=True
    ).astype(jnp.float32)
    gain = lax.dynamic_slice_in_dim(norm_gain, tp_index * out_local, out_local)[None, :]
    scaled = joined * gain
    sums = lax.psum(
        jnp.stack(
            [
                jnp.sum(joined * joined, axis=1),
                jnp.sum(scaled * scaled, axis=1),
                jnp.sum(scaled * wanted, axis=1),
                jnp.sum(wanted * wanted, axis=1),
            ]
        ),
        "tp",
    )
    inv_rms = lax.rsqrt(sums[0] / out_cols + 1e-05)
    row_weight = 2.0 / (out_cols * count_live)
    row_loss = (inv_rms * inv_rms * sums[1] - 2.0 * inv_rms * sums[2] + sums[3]) / out_cols
    inner = row_weight * (inv_rms * sums[1] - sums[2])
    err = scaled * inv_rms[:, None] - wanted
    d_joined = (
        (inv_rms * row_weight)[:, None] * gain * err
        - joined * (inv_rms**3 * inner / out_cols)[:, None]
    ).astype(jnp.bfloat16)
    grad_rows_full = lax.all_gather(d_joined, "tp", axis=1, tiled=True)
    slot_loss = jnp.sum(jnp.where(picked, row_loss[:, None], 0.0), axis=0)
    request_loss = jnp.sum(slot_loss.reshape(requests, most), axis=1) / row_counts.astype(jnp.float32)
    all_slots = jnp.arange(requests * n_dp, dtype=jnp.int32)
    spread = jnp.sum(jnp.where(all_slots[:, None] == seq_slot[None, :], request_loss[None, :], 0.0), axis=1)
    block_rows = 3 * sub_rows
    split = jnp.stack([part.reshape(live, n_dp, sub_rows) for part in inputs], axis=2)
    split = split.reshape(live, n_dp * block_rows)
    grad_mine = lax.psum_scatter(
        lax.dot_general(
            split, grad_rows_full, (((0,), (0,)), ((), ())), preferred_element_type=jnp.float32
        ).astype(jnp.bfloat16),
        "dp",
        scatter_dimension=0,
        tiled=True,
    ).astype(jnp.float32)
    seq_loss = lax.psum_scatter(spread, "dp", scatter_dimension=0, tiled=True)
    weight_mine = lax.dynamic_slice_in_dim(joining_weight, dp_index * sub_rows, sub_rows, 1)
    updated = weight_mine.reshape(block_rows, out_cols).astype(jnp.float32) - learn_rate * grad_mine
    largest = lax.pmax(jnp.max(jnp.abs(updated), axis=0), ("tp", "dp"))
    column_scale = largest + 1e-06
    serving_weight = (
        (updated / column_scale[None, :]).astype(jnp.bfloat16).reshape(3, sub_rows, out_cols)
    )
    return (seq_loss, serving_weight, column_scale)


def solution(mesh):
    placed = (P("dp", None, "tp"), P("dp", "tp"), P("dp"), P("dp"), P(None, "tp", None), P())
    return jax.shard_map(
        shards,
        mesh=mesh,
        in_specs=placed,
        out_specs=(P("dp"), P(None, ("tp", "dp"), None), P()),
        check_vma=False,
    )
```

```python
import jax
import jax.numpy as jnp
from jax import lax
from jax.experimental import pallas as pl
from jax.experimental.pallas import tpu as pltpu
from jax.sharding import PartitionSpec as P

learn_rate = 1.0

F32, BF16, I32 = jnp.float32, jnp.bfloat16, jnp.int32
EXACT = lax.Precision.HIGHEST
REQS, MOST, SLOTS, LIVE = 128, 8, 1024, 544
HALF = LIVE // 2
PAD = 640
ALL = 4 * LIVE
BLOCK, PART = 512, 256
FEATS = 384
OUT = 4096
ROWS_OUT = 96
CHUNK = 32


def iota(shape, dim):
    return lax.broadcasted_iota(I32, shape, dim)


def names():
    out = [f"x{j}" for j in (1, 2, 3)] + [f"c{i}" for i in range(4)]
    out += ["h+", "h-", "f+", "f-"] + [f"s{j}" for j in range(1, 8)]
    for h in "zy":
        for s in "+-":
            out += [f"{h}1{s}", f"{h}1f{s}"]
            out += [f"{h}2{s}{b}" for b in range(4)] + [f"{h}2f{s}{b}" for b in range(4)]
    out += [f"d{h}{b}" for h in range(2) for b in range(4)]
    out += [f"g{h}{b}{o}{j}" for h in range(2) for b in range(4) for o in range(2) for j in (1, 2, 3)]
    out += [f"m{j}" for j in range(1, 8)] + [f"n{j}" for j in range(1, 16)]
    return {name: i for i, name in enumerate(out)}


IDS = names()
STEP = (0, 3, 1, 2)


def kernel(
    hid_hbm, tgt_hbm, counts_ref, slots_ref, w_hbm, gain_ref,
    loss_ref, serve_ref, scale_ref,
    hid, tgt, wv, pick, xc, wanted, csend, crecv, part, hrecv, frecv, xg, xgt, df, gs, gr, upd,
    owner, cntr, stc, str_, stat, mx, mxr, dpr, sprd, lsem, ss, rs,
):
    t = lax.axis_index("tp")
    d = lax.axis_index("dp")
    y, c = t // 2, t % 2
    z, x = d // 4, d % 4
    sent = []

    def at(y=y, c=c, z=z, x=x):
        return {"tp": (y % 4) * 2 + c, "dp": (z % 4) * 4 + x % 4}

    sibling = at(c=1 - c)

    def send(name, src, dst, device):
        i = IDS[name]
        copy = pltpu.make_async_remote_copy(
            src_ref=src, dst_ref=dst, send_sem=ss.at[i], recv_sem=rs.at[i],
            device_id=device, device_id_type=pl.DeviceIdType.MESH,
        )
        copy.start()
        sent.append(copy)

    def got(name, ref):
        i = IDS[name]
        pltpu.make_async_remote_copy(
            src_ref=ref, dst_ref=ref, send_sem=ss.at[i], recv_sem=rs.at[i],
            device_id=sibling, device_id_type=pl.DeviceIdType.MESH,
        ).wait_recv()

    loads = [
        pltpu.make_async_copy(hid_hbm, hid, lsem.at[0]),
        pltpu.make_async_copy(tgt_hbm, tgt, lsem.at[1]),
    ]
    for zz in range(4):
        for l in range(3):
            loads.append(
                pltpu.make_async_copy(
                    w_hbm.at[l, pl.ds(zz * 128, 128)],
                    wv.at[pl.ds(zz * FEATS + l * 128, 128)],
                    lsem.at[2 + zz * 3 + l],
                )
            )
    for load in loads:
        load.start()
    barrier = pltpu.get_barrier_semaphore()
    for j in range(1, 8):
        pl.semaphore_signal(
            barrier, inc=1, device_id={"tp": (t + j) % 8, "dp": d}, device_id_type=pl.DeviceIdType.MESH
        )
    for j in range(1, 16):
        pl.semaphore_signal(
            barrier, inc=1, device_id={"tp": t, "dp": (d + j) % 16}, device_id_type=pl.DeviceIdType.MESH
        )

    counts = counts_ref[...].astype(F32)
    counts8 = jnp.broadcast_to(counts, (8, REQS))
    expand = (iota((REQS, SLOTS), 1) // MOST == iota((REQS, SLOTS), 0)).astype(F32)
    before = (iota((REQS, REQS), 0) < iota((REQS, REQS), 1)).astype(F32)
    start8 = jnp.dot(counts8, before, precision=EXACT, preferred_element_type=F32)
    count_slot = jnp.dot(counts8, expand, precision=EXACT, preferred_element_type=F32)
    start_slot = jnp.dot(start8, expand, precision=EXACT, preferred_element_type=F32)
    inside = iota((8, SLOTS), 1) % MOST
    rank8 = (start_slot + 0.5).astype(I32) + inside
    rank8 = jnp.where(inside < (count_slot + 0.5).astype(I32), rank8, -1)
    rank = rank8[0:1, :]
    cntr[...] = jnp.ones_like(cntr)

    @pl.loop(0, LIVE // 272)
    def _(i):
        rows = pl.ds(pl.multiple_of(i * 272, 16), 272)
        hit = iota((272, SLOTS), 0) + i * 272 == rank
        pick[rows, :] = jnp.where(hit, 1.0, 0.0).astype(BF16)

    for load in loads[:2]:
        load.wait()

    @pl.loop(0, LIVE // 272)
    def _(i):
        rows = pl.ds(pl.multiple_of(i * 272, 16), 272)
        chosen = pick[rows, :]
        for l in range(3):
            got_rows = jnp.dot(chosen, hid[l], preferred_element_type=F32).astype(BF16)
            for zz in range(4):
                xc[rows, zz * FEATS + l * 128 : zz * FEATS + (l + 1) * 128] = got_rows[
                    :, zz * 128 : (zz + 1) * 128
                ]
        wanted[rows, :] = jnp.dot(chosen, tgt[...], preferred_element_type=F32).astype(BF16)
        owner[rows, :] = lax.dot_general(
            chosen, expand.astype(BF16), (((1,), (1,)), ((), ())), preferred_element_type=F32
        )

    cntr[:, 0:LIVE] = lax.dot_general(
        count_slot.astype(BF16), pick[...], (((1,), (1,)), ((), ())), preferred_element_type=F32
    )
    pl.semaphore_wait(barrier, 22)

    def feats(zz):
        return pl.ds(pl.multiple_of((zz % 4) * FEATS, 128), FEATS)

    def rows_of(zz):
        return pl.ds(pl.multiple_of((zz % 4) * LIVE, 16), LIVE)

    for j in (1, 2, 3):
        send(f"x{j}", xc.at[:, feats(z + j)], xg.at[rows_of(z), :], at(z=z + j))
    own_copy = pltpu.make_async_copy(xc.at[:, feats(z)], xg.at[rows_of(z), :], lsem.at[14])
    own_copy.start()
    for load in loads[2:]:
        load.wait()

    def forward(yy, core, dst):
        column = ((yy % 4) * 2 + core) * BLOCK

        @pl.loop(0, 2)
        def _(i):
            cols = pl.ds(pl.multiple_of(column + i * PART, PART), PART)
            dst[:, pl.ds(pl.multiple_of(i * PART, PART), PART)] = jnp.dot(
                xc[...], wv[:, cols], preferred_element_type=F32
            ).astype(dst.dtype)

    def to_sibling(i, step):
        forward(y + step, 1 - c, csend.at[i])
        send(f"c{i}", csend.at[i], crecv.at[i], sibling)

    ysend = [hid.at[i, pl.ds(0, LIVE)] for i in range(3)]
    up, down = at(y=y + 1), at(y=y + 3)
    top, low = pl.ds(0, HALF), pl.ds(HALF, HALF)
    to_sibling(0, 2)
    forward(y + 2, c, part.at[0])
    got("c0", crecv.at[0])
    ysend[0][...] = (part[0] + crecv[0].astype(F32)).astype(BF16)
    send("h+", ysend[0].at[top], hrecv.at[0], up)
    send("h-", ysend[0].at[low], hrecv.at[1], down)
    to_sibling(1, 1)
    forward(y + 1, c, part.at[1])
    to_sibling(2, 3)
    forward(y + 3, c, part.at[2])
    got("c1", crecv.at[1])
    got("c2", crecv.at[2])
    got("h+", hrecv.at[0])
    ysend[1][top, :] = (part[1, top, :] + crecv[1, top, :].astype(F32) + hrecv[0].astype(F32)).astype(BF16)
    ysend[1][low, :] = (part[1, low, :] + crecv[1, low, :].astype(F32)).astype(BF16)
    send("f+", ysend[1], frecv.at[0], up)
    got("h-", hrecv.at[1])
    ysend[2][top, :] = (part[2, top, :] + crecv[2, top, :].astype(F32)).astype(BF16)
    ysend[2][low, :] = (part[2, low, :] + crecv[2, low, :].astype(F32) + hrecv[1].astype(F32)).astype(BF16)
    send("f-", ysend[2], frecv.at[1], down)
    to_sibling(3, 0)
    forward(y, c, part.at[0])

    own_copy.wait()
    for j in (1, 2, 3):
        got(f"x{j}", xg.at[rows_of(z + 4 - j), :])

    @pl.loop(0, ALL // 128)
    def _(k):
        places = pl.ds(pl.multiple_of(k * 128, 128), 128)
        turned = xg[places, :].T
        for xx in range(4):
            for l in range(3):
                xgt[xx * ROWS_OUT + l * 32 : xx * ROWS_OUT + (l + 1) * 32, places] = turned[
                    l * 128 + xx * 32 : l * 128 + (xx + 1) * 32, :
                ]

    got("c3", crecv.at[3])
    got("f+", frecv.at[0])
    got("f-", frecv.at[1])
    gain = gain_ref[pl.ds(t, 1), :]
    stc[...] = jnp.zeros_like(stc)
    lane = iota((CHUNK, 128), 1)

    @pl.loop(0, LIVE // CHUNK)
    def _(i):
        rows = pl.ds(pl.multiple_of(i * CHUNK, CHUNK), CHUNK)
        joined = part[0, rows, :] + crecv[3, rows, :].astype(F32)
        joined = joined + (frecv[0, rows, :].astype(F32) + frecv[1, rows, :].astype(F32))
        part[0, rows, :] = joined
        goal = wanted[rows, :].astype(F32)
        scaled = joined * gain
        sums = [joined * joined, scaled * scaled, scaled * goal, goal * goal]
        row = jnp.zeros((CHUNK, 128), F32)
        for k, term in enumerate(sums):
            row = jnp.where(lane == k, jnp.sum(term, axis=1, keepdims=True), row)
        stc[rows, :] = row

    turned = stc[...].T
    stat[pl.ds(t, 1)] = turned[None, 0:8, :]
    for j in range(1, 8):
        send(f"s{j}", stat.at[t], stat.at[t], {"tp": (t + j) % 8, "dp": d})
    for j in range(1, 8):
        got(f"s{j}", stat.at[(t + 8 - j) % 8])
    total = stat[0]
    for j in range(1, 8):
        total = total + stat[j]
    inv_rms = lax.rsqrt(total[0:1] / OUT + 1e-05)
    weight_row = 2.0 / (OUT * cntr[0:1, :])
    row_loss = (inv_rms * inv_rms * total[1:2] - 2.0 * inv_rms * total[2:3] + total[3:4]) / OUT
    inner = weight_row * (inv_rms * total[1:2] - total[2:3])
    str_[...] = jnp.zeros_like(str_)
    str_[0:1, :] = inv_rms
    str_[1:2, :] = inv_rms * weight_row
    str_[2:3, :] = inv_rms * inv_rms * inv_rms * inner / OUT
    str_[3:4, :] = row_loss
    stc[...] = str_[...].T

    @pl.loop(0, LIVE // CHUNK)
    def _(i):
        rows = pl.ds(pl.multiple_of(i * CHUNK, CHUNK), CHUNK)
        there = pl.ds(pl.multiple_of(z * LIVE + i * CHUNK, CHUNK), CHUNK)
        joined = part[0, rows, :]
        stats = stc[rows, :]
        err = joined * stats[:, 0:1] * gain - wanted[rows, :].astype(F32)
        value = (stats[:, 1:2] * gain * err - joined * stats[:, 2:3]).astype(BF16)
        df[0, t, there, :] = value[:, 0:PART]
        df[1, t, there, :] = value[:, PART:BLOCK]

    def block(h, yy, zz, half=None):
        start, size = (0, LIVE) if half is None else (half * HALF, HALF)
        rows = pl.ds(pl.multiple_of((zz % 4) * LIVE + start, 16), size)
        return df.at[h, (yy % 4) * 2 + c, rows, :]

    def first(h, step, half=None):
        return block(0, y, z + step, half) if h == "z" else block(1, y + step, z, half)

    def second(h, b, step, half=None):
        if h == "z":
            return block(0, y + step, z + STEP[b], half)
        return block(1, y + STEP[b], z + step, half)

    def along(axis, step):
        return at(z=z + step) if axis == "z" else at(y=y + step)

    other = {"z": "y", "y": "z"}

    def put(name, ref, device):
        send(name, ref, ref, device)

    def spread_second(h, b):
        ref = second(h, b, 0)
        put(f"{h}2+{b}", ref, along(other[h], 1))
        put(f"{h}2-{b}", ref, along(other[h], 3))

    def pass_first(h):
        got(f"{h}1+", first(h, 3))
        put(f"{h}1f+", first(h, 3, 0), along(h, 1))
        got(f"{h}1-", first(h, 1))
        put(f"{h}1f-", first(h, 1, 1), along(h, 3))

    def end_first(h):
        got(f"{h}1f+", first(h, 2, 0))
        got(f"{h}1f-", first(h, 2, 1))

    def pass_second(h, b):
        got(f"{h}2+{b}", second(h, b, 3))
        put(f"{h}2f+{b}", second(h, b, 3, 0), along(other[h], 1))
        got(f"{h}2-{b}", second(h, b, 1))
        put(f"{h}2f-{b}", second(h, b, 1, 1), along(other[h], 3))

    def end_second(h, b):
        got(f"{h}2f+{b}", second(h, b, 2, 0))
        got(f"{h}2f-{b}", second(h, b, 2, 1))

    def whole(h, b, core):
        return df.at[h, ((y + STEP[b]) % 4) * 2 + core]

    def share(h, b):
        put(f"d{h}{b}", whole(h, b, c), sibling)

    def columns(h, b, o):
        core = c if o == 0 else 1 - c
        return (((y + STEP[b]) % 4) * 2 + core) * BLOCK + h * PART

    def grad(h, b, o):
        if o == 1:
            got(f"d{h}{b}", whole(h, b, 1 - c))
        cols = pl.ds(pl.multiple_of(columns(h, b, o), PART), PART)
        core = c if o == 0 else 1 - c
        gs[:, cols] = jnp.dot(
            xgt[...], df[h, ((y + STEP[b]) % 4) * 2 + core], preferred_element_type=F32
        ).astype(BF16)
        for j in (1, 2, 3):
            rows = pl.ds(pl.multiple_of(((x + j) % 4) * ROWS_OUT, 32), ROWS_OUT)
            send(f"g{h}{b}{o}{j}", gs.at[rows, cols], gr.at[j - 1, :, cols], at(x=x + j))

    def finish(h, b, o):
        column = columns(h, b, o)
        cols = pl.ds(pl.multiple_of(column, PART), PART)
        for j in (1, 2, 3):
            got(f"g{h}{b}{o}{j}", gr.at[j - 1, :, cols])
        largest = jnp.zeros((1, PART), F32)
        for l in range(3):
            mine = pl.ds(pl.multiple_of(x * ROWS_OUT + l * 32, 32), 32)
            there = pl.ds(pl.multiple_of(z * FEATS + l * 128 + x * 32, 32), 32)
            here = pl.ds(l * 32, 32)
            total = gs[mine, cols].astype(F32)
            for j in range(3):
                total = total + gr[j, here, cols].astype(F32)
            new = wv[there, cols].astype(F32) - learn_rate * total
            upd[here, cols] = new
            largest = jnp.maximum(largest, jnp.max(jnp.abs(new), axis=0, keepdims=True))
        for k in range(PART // 128):
            mx[pl.ds(column // 128 + k, 1), :] = largest[:, k * 128 : (k + 1) * 128]

    for h in "zy":
        put(f"{h}1+", first(h, 0), along(h, 1))
        put(f"{h}1-", first(h, 0), along(h, 3))
    for h in "zy":
        spread_second(h, 0)

    loss_rows = stc[0:LIVE, 3:4] * owner[...]
    request_loss = jnp.sum(loss_rows, axis=0, keepdims=True) / counts
    slots = slots_ref[...]
    places = slots // REQS * 8 + slots % REQS - d * 8
    hit = places == iota((REQS, REQS), 0)
    by_place = jnp.sum(jnp.where(hit, request_loss, 0.0), axis=1, keepdims=True)
    eye = iota((REQS, REQS), 0) == iota((REQS, REQS), 1)
    by_place = jnp.sum(jnp.where(eye, by_place, 0.0), axis=0, keepdims=True)
    dpr[pl.ds(d, 1), 32:40, :] = jnp.broadcast_to(by_place[None], (1, 8, 128))

    for h in "zy":
        pass_first(h)
        spread_second(h, 1)
        spread_second(h, 2)
    for h in "zy":
        end_first(h)
        spread_second(h, 3)
    share(0, 0)
    grad(0, 0, 0)
    pass_second("z", 0)
    pass_second("y", 0)
    grad(0, 0, 1)
    end_second("y", 0)
    share(1, 0)
    grad(1, 0, 0)
    pass_second("z", 1)
    pass_second("y", 1)
    grad(1, 0, 1)
    end_second("y", 1)
    share(1, 1)
    grad(1, 1, 0)
    pass_second("z", 2)
    pass_second("y", 2)
    grad(1, 1, 1)
    finish(0, 0, 0)
    finish(0, 0, 1)
    end_second("y", 2)
    share(1, 2)
    grad(1, 2, 0)
    finish(1, 0, 0)
    finish(1, 0, 1)
    pass_second("z", 3)
    share(0, 1)
    share(0, 2)
    pass_second("y", 3)
    grad(1, 2, 1)
    grad(0, 1, 0)
    grad(0, 2, 0)
    grad(0, 1, 1)
    grad(0, 2, 1)
    finish(1, 1, 0)
    finish(1, 1, 1)
    for b in range(4):
        end_second("z", b)
    share(0, 3)
    end_second("y", 3)
    share(1, 3)
    grad(0, 3, 0)
    grad(1, 3, 0)
    grad(0, 3, 1)
    grad(1, 3, 1)
    for h, b in ((1, 2), (0, 1), (0, 2), (0, 3), (1, 3)):
        finish(h, b, 0)
        finish(h, b, 1)

    for j in range(1, 8):
        send(f"m{j}", mx, mxr.at[j - 1], {"tp": (t + j) % 8, "dp": d})
    most = mx[...]
    for j in range(1, 8):
        got(f"m{j}", mxr.at[j - 1])
        most = jnp.maximum(most, mxr[j - 1])
    dpr[pl.ds(d, 1), 0:32, :] = most[None]
    for j in range(1, 16):
        send(f"n{j}", dpr.at[d], dpr.at[d], {"tp": t, "dp": (d + j) % 16})
    for j in range(1, 16):
        got(f"n{j}", dpr.at[(d + 16 - j) % 16])
    for j in range(16):
        most = jnp.maximum(most, dpr[j, 0:32, :])
        sprd[j * 8 : (j + 1) * 8, :] = dpr[j, 32:40, :]
    scale = most + 1e-06
    scale_ref[...] = scale
    for k in range(OUT // 128):
        cols = slice(k * 128, (k + 1) * 128)
        for l in range(3):
            serve_ref[l, :, cols] = (upd[l * 32 : (l + 1) * 32, cols] / scale[k : k + 1, :]).astype(BF16)
    lanes = iota((REQS, REQS), 1) == d * 8 + iota((REQS, REQS), 0) % 8
    mine = jnp.sum(jnp.where(lanes, sprd[...], 0.0), axis=1, keepdims=True)
    loss_ref[...] = jnp.sum(jnp.where(eye, mine, 0.0), axis=0, keepdims=True)
    for copy in sent:
        copy.wait_send()


def shards(hidden_rows, target_rows, row_counts, seq_slot, joining_weight, norm_gain):
    any_spec = pl.BlockSpec(memory_space=pl.ANY)
    vmem = pl.BlockSpec(memory_space=pltpu.VMEM)
    n = len(IDS)
    loss, serve, scale = pl.pallas_call(
        kernel,
        out_shape=(
            jax.ShapeDtypeStruct((1, REQS), F32),
            jax.ShapeDtypeStruct((3, 32, OUT), BF16),
            jax.ShapeDtypeStruct((32, 128), F32),
        ),
        in_specs=[any_spec, any_spec, vmem, vmem, any_spec, vmem],
        out_specs=(vmem, vmem, vmem),
        scratch_shapes=[
            pltpu.VMEM((3, SLOTS, BLOCK), BF16),
            pltpu.VMEM((SLOTS, BLOCK), BF16),
            pltpu.VMEM((4 * FEATS, OUT), BF16),
            pltpu.VMEM((LIVE, SLOTS), BF16),
            pltpu.VMEM((LIVE, 4 * FEATS), BF16),
            pltpu.VMEM((LIVE, BLOCK), BF16),
            pltpu.VMEM((4, LIVE, BLOCK), BF16),
            pltpu.VMEM((4, LIVE, BLOCK), BF16),
            pltpu.VMEM((3, LIVE, BLOCK), F32),
            pltpu.VMEM((2, HALF, BLOCK), BF16),
            pltpu.VMEM((2, LIVE, BLOCK), BF16),
            pltpu.VMEM((ALL, FEATS), BF16),
            pltpu.VMEM((FEATS, ALL), BF16),
            pltpu.VMEM((2, 8, ALL, PART), BF16),
            pltpu.VMEM((FEATS, OUT), BF16),
            pltpu.VMEM((3, ROWS_OUT, OUT), BF16),
            pltpu.VMEM((ROWS_OUT, OUT), F32),
            pltpu.VMEM((LIVE, REQS), F32),
            pltpu.VMEM((8, PAD), F32),
            pltpu.VMEM((PAD, 128), F32),
            pltpu.VMEM((128, PAD), F32),
            pltpu.VMEM((8, 8, PAD), F32),
            pltpu.VMEM((32, 128), F32),
            pltpu.VMEM((7, 32, 128), F32),
            pltpu.VMEM((16, 40, 128), F32),
            pltpu.VMEM((REQS, 128), F32),
            pltpu.SemaphoreType.DMA((15,)),
            pltpu.SemaphoreType.DMA((n,)),
            pltpu.SemaphoreType.DMA((n,)),
        ],
        compiler_params=pltpu.CompilerParams(
            collective_id=0, has_side_effects=True, vmem_limit_bytes=64 * 2**20 - 2**18
        ),
        name="joining_step",
    )(
        jnp.transpose(hidden_rows, (1, 0, 2)),
        target_rows,
        row_counts.reshape(1, REQS),
        seq_slot.reshape(1, REQS),
        joining_weight,
        norm_gain.reshape(8, BLOCK),
    )
    return loss.reshape(REQS), serve, scale.reshape(OUT)


def solution(mesh):
    placed = (P("dp", None, "tp"), P("dp", "tp"), P("dp"), P("dp"), P(None, "tp", None), P())
    return jax.shard_map(
        shards,
        mesh=mesh,
        in_specs=placed,
        out_specs=(P("dp"), P(None, ("tp", "dp"), None), P()),
        check_vma=False,
    )
```

```python
import jax
import jax.numpy as jnp
from jax import lax
from jax.experimental import pallas as pl
from jax.experimental.pallas import tpu as pltpu
from jax.sharding import PartitionSpec as P

learn_rate = 1.0

F32, BF16, I32 = jnp.float32, jnp.bfloat16, jnp.int32
EXACT = lax.Precision.HIGHEST
REQS, MOST, SLOTS, LIVE = 128, 8, 1024, 544
HALF = LIVE // 2
PAD = 640
ALL = 4 * LIVE
BLOCK, PART = 512, 256
FEATS = 384
OUT = 4096
ROWS_OUT = 96
CHUNK = 32


def iota(shape, dim):
    return lax.broadcasted_iota(I32, shape, dim)


def names():
    out = [f"x{h}{j}" for h in range(2) for j in (1, 2, 3)] + [f"c{i}" for i in range(4)]
    out += ["h+", "h-", "f+a", "f+b", "f-a", "f-b"] + [f"s{j}" for j in range(1, 8)]
    for h in range(2):
        out += [f"{k}{h}{s}" for k in ("y", "yf") for s in "+-"]
        out += [f"{k}{h}{b}{s}" for k in ("a", "af") for b in range(4) for s in "+-"]
        out += [f"v{h}{j}" for j in (1, 2, 3)] + [f"d{h}{b}" for b in range(4)]
        out += [f"g{h}{b}{o}{j}" for b in range(4) for o in range(2) for j in (1, 2, 3)]
    out += [f"m{j}" for j in range(1, 8)] + [f"n{j}" for j in range(1, 16)]
    return {name: i for i, name in enumerate(out)}


IDS = names()
STEP = (0, 3, 1, 2)
ALONG = ((0, 2, 3), (0, 1, 3))
WHOLE = (1, 2)
TURN = (1, 3)


def kernel(
    hid_hbm, tgt_hbm, counts_ref, slots_ref, w_hbm, gain_ref,
    upd, small_ref,
    hid, tgt, wv, pick, perm, xc, xcb, wanted, crecv, part, hrecv, frecv, xg, xgt, df, gs, gr,
    owner, stc, str_, stat, mx, mxr, dpr, sprd, lsem, ss, rs,
):
    t = lax.axis_index("tp")
    d = lax.axis_index("dp")
    y, c = t // 2, t % 2
    z, x = d // 4, d % 4
    sent = []

    def at(y=y, c=c, z=z, x=x):
        return {"tp": (y % 4) * 2 + c, "dp": (z % 4) * 4 + x % 4}

    sibling = at(c=1 - c)

    def send(name, src, dst, device):
        i = IDS[name]
        copy = pltpu.make_async_remote_copy(
            src_ref=src, dst_ref=dst, send_sem=ss.at[i], recv_sem=rs.at[i],
            device_id=device, device_id_type=pl.DeviceIdType.MESH,
        )
        copy.start()
        sent.append(copy)

    def got(name, ref):
        i = IDS[name]
        pltpu.make_async_remote_copy(
            src_ref=ref, dst_ref=ref, send_sem=ss.at[i], recv_sem=rs.at[i],
            device_id=sibling, device_id_type=pl.DeviceIdType.MESH,
        ).wait_recv()

    loads = [pltpu.make_async_copy(hid_hbm.at[l], hid.at[l], lsem.at[l]) for l in range(3)]
    loads.append(pltpu.make_async_copy(tgt_hbm, tgt, lsem.at[3]))
    weights = []
    for zz in range(4):
        for l in range(3):
            weights.append(
                pltpu.make_async_copy(
                    w_hbm.at[l, pl.ds(zz * 128, 128)],
                    wv.at[pl.ds(zz * FEATS + l * 128, 128)],
                    lsem.at[4 + zz * 3 + l],
                )
            )
    for load in loads:
        load.start()
    barrier = pltpu.get_barrier_semaphore()
    for j in range(1, 8):
        pl.semaphore_signal(
            barrier, inc=1, device_id={"tp": (t + j) % 8, "dp": d}, device_id_type=pl.DeviceIdType.MESH
        )
    for j in range(1, 16):
        pl.semaphore_signal(
            barrier, inc=1, device_id={"tp": t, "dp": (d + j) % 16}, device_id_type=pl.DeviceIdType.MESH
        )

    counts = counts_ref[...].astype(F32)
    counts8 = jnp.broadcast_to(counts, (8, REQS))
    expand = (iota((REQS, SLOTS), 1) // MOST == iota((REQS, SLOTS), 0)).astype(F32)
    before = (iota((REQS, REQS), 0) < iota((REQS, REQS), 1)).astype(F32)
    start8 = jnp.dot(counts8, before, precision=EXACT, preferred_element_type=F32)
    count_slot = jnp.dot(counts8, expand, precision=EXACT, preferred_element_type=F32)
    start_slot = jnp.dot(start8, expand, precision=EXACT, preferred_element_type=F32)
    inside = iota((8, SLOTS), 1) % MOST
    rank8 = (start_slot + 0.5).astype(I32) + inside
    rank8 = jnp.where(inside < (count_slot + 0.5).astype(I32), rank8, -1)
    rank = rank8[0:1, :]

    @pl.loop(0, LIVE // 272)
    def _(i):
        rows = pl.ds(pl.multiple_of(i * 272, 16), 272)
        hit = iota((272, SLOTS), 0) + i * 272 == rank
        pick[rows, :] = jnp.where(hit, 1.0, 0.0).astype(BF16)

    place = iota((BLOCK, BLOCK), 1)
    source = place // 32 % 4 * 128 + place // 128 * 32 + place % 32
    perm[...] = (iota((BLOCK, BLOCK), 0) == source).astype(F32).astype(BF16)

    for load in loads:
        load.wait()
    for load in weights:
        load.start()

    @pl.loop(0, LIVE // 272)
    def _(i):
        rows = pl.ds(pl.multiple_of(i * 272, 16), 272)
        chosen = pick[rows, :]
        for l in range(3):
            got_rows = jnp.dot(chosen, hid[l], preferred_element_type=F32).astype(BF16)
            swapped = jnp.dot(got_rows, perm[...], preferred_element_type=F32).astype(BF16)
            for q in range(4):
                cols = slice(q * FEATS + l * 128, q * FEATS + (l + 1) * 128)
                xc[rows, cols] = got_rows[:, q * 128 : (q + 1) * 128]
                xcb[rows, cols] = swapped[:, q * 128 : (q + 1) * 128]

    pl.semaphore_wait(barrier, 22)

    def feats(q):
        return pl.ds(pl.multiple_of((q % 4) * FEATS, 128), FEATS)

    def rows_of(q):
        return pl.ds(pl.multiple_of((q % 4) * LIVE, 16), LIVE)

    me = (z, x)

    def axis(h, step):
        return at(z=z + step) if h == 0 else at(x=x + step)

    own_copies = []
    for h, kept in enumerate((xc, xcb)):
        for j in (1, 2, 3):
            send(f"x{h}{j}", kept.at[:, feats(me[h] + j)], xg.at[h, rows_of(me[h]), :], axis(h, j))
        own_copies.append(
            pltpu.make_async_copy(kept.at[:, feats(me[h])], xg.at[h, rows_of(me[h]), :], lsem.at[16 + h])
        )
        own_copies[h].start()

    turned_expand = (iota((SLOTS, REQS), 0) // MOST == iota((SLOTS, REQS), 1)).astype(F32).astype(BF16)

    @pl.loop(0, LIVE // 272)
    def _(i):
        rows = pl.ds(pl.multiple_of(i * 272, 16), 272)
        chosen = pick[rows, :]
        wanted[rows, :] = jnp.dot(chosen, tgt[...], preferred_element_type=F32).astype(BF16)
        owner[rows, :] = jnp.dot(chosen, turned_expand, preferred_element_type=F32)

    for load in weights:
        load.wait()

    def forward(yy, core, dst):
        column = ((yy % 4) * 2 + core) * BLOCK

        @pl.loop(0, 2)
        def _(i):
            cols = pl.ds(pl.multiple_of(column + i * PART, PART), PART)
            dst[:, pl.ds(pl.multiple_of(i * PART, PART), PART)] = jnp.dot(
                xc[...], wv[:, cols], preferred_element_type=F32
            ).astype(dst.dtype)

    csend = [pick.at[:, 0:BLOCK], pick.at[:, BLOCK : 2 * BLOCK], tgt.at[pl.ds(0, LIVE)], pick.at[:, 0:BLOCK]]

    def to_sibling(i, step):
        forward(y + step, 1 - c, csend[i])
        send(f"c{i}", csend[i], crecv.at[i], sibling)

    ysend = [hid.at[i, pl.ds(0, LIVE)] for i in range(3)]
    up, down = at(y=y + 1), at(y=y + 3)
    top, low = pl.ds(0, HALF), pl.ds(HALF, HALF)
    to_sibling(0, 2)
    first_sent = sent.pop()
    forward(y + 2, c, part.at[0])
    got("c0", crecv.at[0])
    ysend[0][...] = (part[0] + crecv[0].astype(F32)).astype(BF16)
    send("h+", ysend[0].at[top], hrecv.at[0], up)
    send("h-", ysend[0].at[low], hrecv.at[1], down)
    to_sibling(1, 1)
    forward(y + 1, c, part.at[1])
    got("c1", crecv.at[1])
    ysend[1][low, :] = (part[1, low, :] + crecv[1, low, :].astype(F32)).astype(BF16)
    send("f+a", ysend[1].at[low], frecv.at[0, low], up)
    to_sibling(2, 3)
    forward(y + 3, c, part.at[2])
    got("c2", crecv.at[2])
    ysend[2][top, :] = (part[2, top, :] + crecv[2, top, :].astype(F32)).astype(BF16)
    send("f-a", ysend[2].at[top], frecv.at[1, top], down)
    got("h+", hrecv.at[0])
    ysend[1][top, :] = (part[1, top, :] + crecv[1, top, :].astype(F32) + hrecv[0].astype(F32)).astype(BF16)
    send("f+b", ysend[1].at[top], frecv.at[0, top], up)
    got("h-", hrecv.at[1])
    ysend[2][low, :] = (part[2, low, :] + crecv[2, low, :].astype(F32) + hrecv[1].astype(F32)).astype(BF16)
    send("f-b", ysend[2].at[low], frecv.at[1, low], down)
    first_sent.wait_send()
    to_sibling(3, 0)
    forward(y, c, part.at[0])

    for h in range(2):
        own_copies[h].wait()
        for j in (1, 2, 3):
            got(f"x{h}{j}", xg.at[h, rows_of(me[h] + 4 - j), :])

        @pl.loop(0, ALL // 128)
        def _(k):
            places = pl.ds(pl.multiple_of(k * 128, 128), 128)
            turned = xg[h, places, :].T
            for q in range(4):
                for l in range(3):
                    xgt[h, q * ROWS_OUT + l * 32 : q * ROWS_OUT + (l + 1) * 32, places] = turned[
                        l * 128 + q * 32 : l * 128 + (q + 1) * 32, :
                    ]

    got("c3", crecv.at[3])
    got("f+a", frecv.at[0, low])
    got("f-a", frecv.at[1, top])
    got("f+b", frecv.at[0, top])
    got("f-b", frecv.at[1, low])
    gains = gain_ref[pl.ds(t * 4, 4), :]
    gain = jnp.concatenate([gains[k : k + 1, :] for k in range(4)], axis=1)
    stc[...] = jnp.zeros_like(stc)
    lane = iota((CHUNK, 128), 1)

    @pl.loop(0, LIVE // CHUNK)
    def _(i):
        rows = pl.ds(pl.multiple_of(i * CHUNK, CHUNK), CHUNK)
        joined = part[0, rows, :] + crecv[3, rows, :].astype(F32)
        joined = joined + (frecv[0, rows, :].astype(F32) + frecv[1, rows, :].astype(F32))
        part[0, rows, :] = joined
        goal = wanted[rows, :].astype(F32)
        scaled = joined * gain
        sums = [joined * joined, scaled * scaled, scaled * goal, goal * goal]
        row = jnp.zeros((CHUNK, 128), F32)
        for k, term in enumerate(sums):
            row = jnp.where(lane == k, jnp.sum(term, axis=1, keepdims=True), row)
        count = jnp.sum(owner[rows, :] * counts, axis=1, keepdims=True)
        stc[rows, :] = jnp.where(lane == 4, count, row)

    turned = stc[...].T
    count_row = jnp.maximum(turned[4:5, :], 1.0)
    stat[pl.ds(t, 1)] = turned[None, 0:8, :]
    for j in range(1, 8):
        send(f"s{j}", stat.at[t], stat.at[t], {"tp": (t + j) % 8, "dp": d})
    for j in range(1, 8):
        got(f"s{j}", stat.at[(t + 8 - j) % 8])
    total = stat[0]
    for j in range(1, 8):
        total = total + stat[j]
    inv_rms = lax.rsqrt(total[0:1] / OUT + 1e-05)
    weight_row = 2.0 / (OUT * count_row)
    row_loss = (inv_rms * inv_rms * total[1:2] - 2.0 * inv_rms * total[2:3] + total[3:4]) / OUT
    inner = weight_row * (inv_rms * total[1:2] - total[2:3])
    str_[...] = jnp.zeros_like(str_)
    str_[0:1, :] = inv_rms
    str_[1:2, :] = inv_rms * weight_row
    str_[2:3, :] = inv_rms * inv_rms * inv_rms * inner / OUT
    str_[3:4, :] = row_loss
    stc[...] = str_[...].T

    @pl.loop(0, LIVE // CHUNK)
    def _(i):
        rows = pl.ds(pl.multiple_of(i * CHUNK, CHUNK), CHUNK)
        joined = part[0, rows, :]
        stats = stc[rows, :]
        err = joined * stats[:, 0:1] * gain - wanted[rows, :].astype(F32)
        value = (stats[:, 1:2] * gain * err - joined * stats[:, 2:3]).astype(BF16)
        for h in range(2):
            there = pl.ds(pl.multiple_of(me[h] * LIVE + i * CHUNK, CHUNK), CHUNK)
            df[h, t, there, :] = value[:, h * PART : (h + 1) * PART]

    def block(h, yy, place, half=None):
        start, size = (0, LIVE) if half is None else (half * HALF, HALF)
        rows = pl.ds(pl.multiple_of((place % 4) * LIVE + start, 16), size)
        return df.at[h, (yy % 4) * 2 + c, rows, :]

    def put(name, ref, device):
        send(name, ref, ref, device)

    def put_y(h):
        put(f"y{h}+", block(h, y, me[h]), up)
        put(f"y{h}-", block(h, y, me[h]), down)

    def pass_y(h):
        got(f"y{h}+", block(h, y + 3, me[h]))
        put(f"yf{h}+", block(h, y + 3, me[h], 0), up)
        got(f"y{h}-", block(h, y + 1, me[h]))
        put(f"yf{h}-", block(h, y + 1, me[h], 1), down)

    def end_y(h):
        got(f"yf{h}+", block(h, y + 2, me[h], 0))
        got(f"yf{h}-", block(h, y + 2, me[h], 1))

    def put_axis(h, b):
        put(f"a{h}{b}+", block(h, y + STEP[b], me[h]), axis(h, 1))
        put(f"a{h}{b}-", block(h, y + STEP[b], me[h]), axis(h, 3))

    def pass_axis(h, b):
        got(f"a{h}{b}+", block(h, y + STEP[b], me[h] + 3))
        put(f"af{h}{b}+", block(h, y + STEP[b], me[h] + 3, 0), axis(h, 1))
        got(f"a{h}{b}-", block(h, y + STEP[b], me[h] + 1))
        put(f"af{h}{b}-", block(h, y + STEP[b], me[h] + 1, 1), axis(h, 3))

    def end_axis(h, b):
        got(f"af{h}{b}+", block(h, y + STEP[b], me[h] + 2, 0))
        got(f"af{h}{b}-", block(h, y + STEP[b], me[h] + 2, 1))

    def put_whole(h):
        for j in (1, 3, 2):
            put(f"v{h}{j}", block(h, y, me[h] + j), at(y=y + TURN[h]))

    def end_whole(h):
        for j in (1, 3, 2):
            got(f"v{h}{j}", block(h, y + 4 - TURN[h], me[h] + j))

    def whole(h, b, core):
        return df.at[h, ((y + STEP[b]) % 4) * 2 + core]

    def share(h, b):
        put(f"d{h}{b}", whole(h, b, c), sibling)

    def block_of(b, o):
        return ((y + STEP[b]) % 4) * 2 + (c if o == 0 else 1 - c)

    def across(h, step):
        return axis(1 - h, step)

    def grad(h, b, o):
        if o == 1:
            got(f"d{h}{b}", whole(h, b, 1 - c))
        cols = pl.ds(pl.multiple_of(block_of(b, o) * PART, PART), PART)
        gs[h, :, cols] = jnp.dot(xgt[h], df[h, block_of(b, o)], preferred_element_type=F32).astype(BF16)
        for j in (2, 1, 3):
            rows = pl.ds(pl.multiple_of(((me[1 - h] + j) % 4) * ROWS_OUT, 32), ROWS_OUT)
            send(f"g{h}{b}{o}{j}", gs.at[h, rows, cols], gr.at[h, j - 1, :, cols], across(h, j))

    def finish(h, b, o):
        column = block_of(b, o) * BLOCK + h * PART
        cols = pl.ds(pl.multiple_of(block_of(b, o) * PART, PART), PART)
        wide = pl.ds(pl.multiple_of(column, PART), PART)
        for j in (1, 2, 3):
            got(f"g{h}{b}{o}{j}", gr.at[h, j - 1, :, cols])
        largest = jnp.zeros((1, PART), F32)
        for l in range(3):
            mine = pl.ds(pl.multiple_of(me[1 - h] * ROWS_OUT + l * 32, 32), 32)
            there = pl.ds(pl.multiple_of(z * FEATS + l * 128 + x * 32, 32), 32)
            here = pl.ds(l * 32, 32)
            total = gs[h, mine, cols].astype(F32)
            for j in range(3):
                total = total + gr[h, j, here, cols].astype(F32)
            new = wv[there, wide].astype(F32) - learn_rate * total
            upd[l, :, wide] = new
            largest = jnp.maximum(largest, jnp.max(jnp.abs(new), axis=0, keepdims=True))
        for k in range(PART // 128):
            mx[pl.ds(column // 128 + k, 1), :] = largest[:, k * 128 : (k + 1) * 128]

    for h in range(2):
        put_y(h)
        put_axis(h, 0)

    loss_rows = stc[0:LIVE, 3:4] * owner[...]
    request_loss = jnp.sum(loss_rows, axis=0, keepdims=True) / counts
    slots = slots_ref[...]
    places = slots // REQS * 8 + slots % REQS - d * 8
    hit = places == iota((REQS, REQS), 0)
    by_place = jnp.sum(jnp.where(hit, request_loss, 0.0), axis=1, keepdims=True)
    eye = iota((REQS, REQS), 0) == iota((REQS, REQS), 1)
    by_place = jnp.sum(jnp.where(eye, by_place, 0.0), axis=0, keepdims=True)
    dpr[pl.ds(d, 1), 32:40, :] = jnp.broadcast_to(by_place[None], (1, 8, 128))

    for h in range(2):
        pass_axis(h, 0)
    for h in range(2):
        pass_y(h)
        put_axis(h, ALONG[h][1])
    for h in range(2):
        end_axis(h, 0)
        share(h, 0)
        put_whole(h)
    for h in range(2):
        grad(h, 0, 0)
    for h in range(2):
        end_y(h)
        put_axis(h, 3)
    for h in range(2):
        grad(h, 0, 1)
    for h in range(2):
        pass_axis(h, ALONG[h][1])
    for h in range(2):
        end_axis(h, ALONG[h][1])
        share(h, ALONG[h][1])
        grad(h, ALONG[h][1], 0)
    for h in range(2):
        grad(h, ALONG[h][1], 1)
    for h in range(2):
        pass_axis(h, 3)
    for h in range(2):
        finish(h, 0, 0)
        finish(h, 0, 1)
    for h in range(2):
        end_whole(h)
        share(h, WHOLE[h])
        grad(h, WHOLE[h], 0)
    for h in range(2):
        end_axis(h, 3)
        share(h, 3)
        grad(h, WHOLE[h], 1)
        grad(h, 3, 0)
    for h in range(2):
        grad(h, 3, 1)
    for h in range(2):
        for o in range(2):
            finish(h, ALONG[h][1], o)
    for h in range(2):
        for o in range(2):
            finish(h, WHOLE[h], o)
    for h in range(2):
        for o in range(2):
            finish(h, 3, o)

    for j in range(1, 8):
        send(f"m{j}", mx, mxr.at[j - 1], {"tp": (t + j) % 8, "dp": d})
    most = mx[...]
    for j in range(1, 8):
        got(f"m{j}", mxr.at[j - 1])
        most = jnp.maximum(most, mxr[j - 1])
    dpr[pl.ds(d, 1), 0:32, :] = most[None]
    for j in range(1, 16):
        send(f"n{j}", dpr.at[d], dpr.at[d], {"tp": t, "dp": (d + j) % 16})
    for j in range(1, 16):
        got(f"n{j}", dpr.at[(d + 16 - j) % 16])
    for j in range(16):
        most = jnp.maximum(most, dpr[j, 0:32, :])
        sprd[j * 8 : (j + 1) * 8, :] = dpr[j, 32:40, :]
    small_ref[0:32, :] = most + 1e-06
    lanes = iota((REQS, REQS), 1) == d * 8 + iota((REQS, REQS), 0) % 8
    mine = jnp.sum(jnp.where(lanes, sprd[...], 0.0), axis=1, keepdims=True)
    loss = jnp.sum(jnp.where(eye, mine, 0.0), axis=0, keepdims=True)
    small_ref[32:40, :] = jnp.broadcast_to(loss, (8, 128))
    for copy in sent:
        copy.wait_send()


def scaled(upd, small, loss_ref, serve_ref, scale_ref):
    scale_ref[...] = small[0:32, :]
    loss_ref[...] = small[32:33, :]
    for k in range(OUT // 128):
        cols = slice(k * 128, (k + 1) * 128)
        serve_ref[:, :, cols] = (upd[:, :, cols] / small[k : k + 1, :][None]).astype(BF16)


def shards(hidden_rows, target_rows, row_counts, seq_slot, joining_weight, norm_gain):
    any_spec = pl.BlockSpec(memory_space=pl.ANY)
    vmem = pl.BlockSpec(memory_space=pltpu.VMEM)
    n = len(IDS)
    upd, small = pl.pallas_call(
        kernel,
        out_shape=(
            jax.ShapeDtypeStruct((3, 32, OUT), F32),
            jax.ShapeDtypeStruct((40, 128), F32),
        ),
        in_specs=[any_spec, any_spec, vmem, vmem, any_spec, vmem],
        out_specs=(vmem, vmem),
        scratch_shapes=[
            pltpu.VMEM((3, SLOTS, BLOCK), BF16),
            pltpu.VMEM((SLOTS, BLOCK), BF16),
            pltpu.VMEM((4 * FEATS, OUT), BF16),
            pltpu.VMEM((LIVE, SLOTS), BF16),
            pltpu.VMEM((BLOCK, BLOCK), BF16),
            pltpu.VMEM((LIVE, 4 * FEATS), BF16),
            pltpu.VMEM((LIVE, 4 * FEATS), BF16),
            pltpu.VMEM((LIVE, BLOCK), BF16),
            pltpu.VMEM((4, LIVE, BLOCK), BF16),
            pltpu.VMEM((3, LIVE, BLOCK), F32),
            pltpu.VMEM((2, HALF, BLOCK), BF16),
            pltpu.VMEM((2, LIVE, BLOCK), BF16),
            pltpu.VMEM((2, ALL, FEATS), BF16),
            pltpu.VMEM((2, FEATS, ALL), BF16),
            pltpu.VMEM((2, 8, ALL, PART), BF16),
            pltpu.VMEM((2, FEATS, 8 * PART), BF16),
            pltpu.VMEM((2, 3, ROWS_OUT, 8 * PART), BF16),
            pltpu.VMEM((LIVE, REQS), F32),
            pltpu.VMEM((PAD, 128), F32),
            pltpu.VMEM((128, PAD), F32),
            pltpu.VMEM((8, 8, PAD), F32),
            pltpu.VMEM((32, 128), F32),
            pltpu.VMEM((7, 32, 128), F32),
            pltpu.VMEM((16, 40, 128), F32),
            pltpu.VMEM((REQS, 128), F32),
            pltpu.SemaphoreType.DMA((18,)),
            pltpu.SemaphoreType.DMA((n,)),
            pltpu.SemaphoreType.DMA((n,)),
        ],
        compiler_params=pltpu.CompilerParams(
            collective_id=0, has_side_effects=True, vmem_limit_bytes=64 * 2**20 - 2**18
        ),
        name="joining_step",
    )(
        jnp.transpose(hidden_rows, (1, 0, 2)),
        target_rows,
        row_counts.reshape(1, REQS),
        seq_slot.reshape(1, REQS),
        joining_weight,
        norm_gain.reshape(32, 128),
    )
    loss, serve, scale = pl.pallas_call(
        scaled,
        out_shape=(
            jax.ShapeDtypeStruct((1, REQS), F32),
            jax.ShapeDtypeStruct((3, 32, OUT), BF16),
            jax.ShapeDtypeStruct((32, 128), F32),
        ),
        in_specs=[vmem, vmem],
        out_specs=(vmem, vmem, vmem),
        name="scaled",
    )(upd, small)
    return loss.reshape(REQS), serve, scale.reshape(OUT)


def solution(mesh):
    placed = (P("dp", None, "tp"), P("dp", "tp"), P("dp"), P("dp"), P(None, "tp", None), P())
    return jax.shard_map(
        shards,
        mesh=mesh,
        in_specs=placed,
        out_specs=(P("dp"), P(None, ("tp", "dp"), None), P()),
        check_vma=False,
    )
```

```python
import jax
import jax.numpy as jnp
from jax import lax
from jax.experimental import pallas as pl
from jax.experimental.pallas import tpu as pltpu
from jax.sharding import PartitionSpec as P

learn_rate = 1.0

F32, BF16, I32 = jnp.float32, jnp.bfloat16, jnp.int32
EXACT = lax.Precision.HIGHEST
REQS, MOST, SLOTS, LIVE = 128, 8, 1024, 544
HALF = LIVE // 2
PAD = 640
ALL = 4 * LIVE
BLOCK, PART = 512, 256
FEATS = 384
OUT = 4096
ROWS_OUT = 96
CHUNK = 32


def iota(shape, dim):
    return lax.broadcasted_iota(I32, shape, dim)


def names():
    out = [f"x{h}{j}" for h in range(2) for j in (1, 2, 3)] + [f"c{i}" for i in range(4)]
    out += ["c0b", "h+", "h-", "f+a", "f+b", "f-a", "f-b"] + [f"s{j}" for j in range(1, 8)]
    for h in range(2):
        out += [f"{k}{h}{s}" for k in ("y", "yf") for s in "+-"]
        out += [f"{k}{h}{b}{s}" for k in ("a", "af") for b in range(4) for s in "+-"]
        out += [f"v{h}{j}" for j in (1, 2, 3)] + [f"d{h}{b}{k}" for b in range(4) for k in range(4)]
        out += [f"g{h}{b}{o}{j}" for b in range(4) for o in range(2) for j in (1, 2, 3)]
    out += [f"m{j}" for j in range(1, 8)] + [f"n{j}" for j in range(1, 16)]
    return {name: i for i, name in enumerate(out)}


IDS = names()
STEP = (0, 3, 1, 2)
ALONG = ((0, 2, 3), (0, 1, 3))
WHOLE = (1, 2)
TURN = (1, 3)


def kernel(
    hid_hbm, tgt_hbm, counts_ref, slots_ref, w_hbm, gain_ref,
    upd, small_ref,
    hid, tgt, wv, pick, perm, xc, xcb, wanted, crecv, part, hrecv, frecv, xg, xgt, df, gs, gr,
    owner, stc, str_, stat, mx, mxr, dpr, sprd, lsem, ss, rs,
):
    t = lax.axis_index("tp")
    d = lax.axis_index("dp")
    y, c = t // 2, t % 2
    z, x = d // 4, d % 4
    sent = {}

    def at(y=y, c=c, z=z, x=x):
        return {"tp": (y % 4) * 2 + c, "dp": (z % 4) * 4 + x % 4}

    sibling = at(c=1 - c)

    def send(name, src, dst, device):
        i = IDS[name]
        copy = pltpu.make_async_remote_copy(
            src_ref=src, dst_ref=dst, send_sem=ss.at[i], recv_sem=rs.at[i],
            device_id=device, device_id_type=pl.DeviceIdType.MESH,
        )
        copy.start()
        sent[name] = copy

    def settle(*which):
        for name in which or tuple(sent):
            sent.pop(name).wait_send()

    def got(name, ref):
        i = IDS[name]
        pltpu.make_async_remote_copy(
            src_ref=ref, dst_ref=ref, send_sem=ss.at[i], recv_sem=rs.at[i],
            device_id=sibling, device_id_type=pl.DeviceIdType.MESH,
        ).wait_recv()

    loads = [pltpu.make_async_copy(hid_hbm.at[l], hid.at[l], lsem.at[l]) for l in range(3)]
    loads.append(pltpu.make_async_copy(tgt_hbm, tgt, lsem.at[3]))
    weights = []
    for zz in range(4):
        for l in range(3):
            weights.append(
                pltpu.make_async_copy(
                    w_hbm.at[l, pl.ds(zz * 128, 128)],
                    wv.at[pl.ds(zz * FEATS + l * 128, 128)],
                    lsem.at[4 + zz * 3 + l],
                )
            )
    for load in loads[:3]:
        load.start()
    barrier = pltpu.get_barrier_semaphore()
    for j in range(1, 8):
        pl.semaphore_signal(
            barrier, inc=1, device_id={"tp": (t + j) % 8, "dp": d}, device_id_type=pl.DeviceIdType.MESH
        )
    for j in range(1, 16):
        pl.semaphore_signal(
            barrier, inc=1, device_id={"tp": t, "dp": (d + j) % 16}, device_id_type=pl.DeviceIdType.MESH
        )

    counts = counts_ref[...].astype(F32)
    counts8 = jnp.broadcast_to(counts, (8, REQS))
    expand = (iota((REQS, SLOTS), 1) >> 3 == iota((REQS, SLOTS), 0)).astype(F32)
    before = (iota((REQS, REQS), 0) < iota((REQS, REQS), 1)).astype(F32)
    start8 = jnp.dot(counts8, before, precision=EXACT, preferred_element_type=F32)
    count_slot = jnp.dot(counts8, expand, precision=EXACT, preferred_element_type=F32)
    start_slot = jnp.dot(start8, expand, precision=EXACT, preferred_element_type=F32)
    inside = iota((8, SLOTS), 1) & 7
    rank8 = (start_slot + 0.5).astype(I32) + inside
    rank8 = jnp.where(inside < (count_slot + 0.5).astype(I32), rank8, -1)
    rank = rank8[0:1, :]

    @pl.loop(0, LIVE // 272)
    def _(i):
        rows = pl.ds(pl.multiple_of(i * 272, 16), 272)
        hit = iota((272, SLOTS), 0) + i * 272 == rank
        pick[rows, :] = jnp.where(hit, 1.0, 0.0).astype(BF16)

    for load in loads[:3]:
        load.wait()
    loads[3].start()
    for load in weights:
        load.start()

    @pl.loop(0, LIVE // 272)
    def _(i):
        rows = pl.ds(pl.multiple_of(i * 272, 16), 272)
        chosen = pick[rows, :]
        for l in range(3):
            got_rows = jnp.dot(chosen, hid[l], preferred_element_type=F32).astype(BF16)
            for q in range(4):
                cols = slice(q * FEATS + l * 128, q * FEATS + (l + 1) * 128)
                xc[rows, cols] = got_rows[:, q * 128 : (q + 1) * 128]

    pl.semaphore_wait(barrier, 22)

    def feats(q):
        return pl.ds(pl.multiple_of((q % 4) * FEATS, 128), FEATS)

    def rows_of(q):
        return pl.ds(pl.multiple_of((q % 4) * LIVE, 16), LIVE)

    me = (z, x)

    def axis(h, step):
        return at(z=z + step) if h == 0 else at(x=x + step)

    own_copies = []

    def exchange(h, kept):
        for j in (1, 2, 3):
            send(f"x{h}{j}", kept.at[:, feats(me[h] + j)], xg.at[h, rows_of(me[h]), :], axis(h, j))
        own_copies.append(
            pltpu.make_async_copy(kept.at[:, feats(me[h])], xg.at[h, rows_of(me[h]), :], lsem.at[16 + h])
        )
        own_copies[h].start()

    exchange(0, xc)
    for load in weights:
        load.wait()

    def forward(yy, core, dst, rows=slice(None)):
        column = ((yy % 4) * 2 + core) * BLOCK

        @pl.loop(0, 2)
        def _(i):
            cols = pl.ds(pl.multiple_of(column + i * PART, PART), PART)
            dst[rows, pl.ds(pl.multiple_of(i * PART, PART), PART)] = jnp.dot(
                xc[rows, :], wv[:, cols], preferred_element_type=F32
            ).astype(dst.dtype)

    csend = [xcb.at[:, i * BLOCK : (i + 1) * BLOCK] for i in range(3)] + [hid.at[2, pl.ds(0, LIVE)]]
    ysend = [hid.at[i, pl.ds(0, LIVE)] for i in range(2)]
    yhalf = [hid.at[i, pl.ds(LIVE, HALF)] for i in range(2)]

    def to_sibling(i, step):
        forward(y + step, 1 - c, csend[i])
        send(f"c{i}", csend[i], crecv.at[i], sibling)

    up, down = at(y=y + 1), at(y=y + 3)
    top, low = pl.ds(0, HALF), pl.ds(HALF, HALF)
    for rows, name in ((top, "c0"), (low, "c0b")):
        forward(y + 2, 1 - c, csend[0], rows)
        send(name, csend[0].at[rows], crecv.at[0, rows], sibling)
        forward(y + 2, c, part.at[0], rows)
    for k, (rows, name, there, device) in enumerate(((top, "c0", "h+", up), (low, "c0b", "h-", down))):
        got(name, crecv.at[0, rows])
        yhalf[k][...] = (part[0, rows, :] + crecv[0, rows, :].astype(F32)).astype(BF16)
        send(there, yhalf[k], hrecv.at[k], device)
    to_sibling(1, 1)
    forward(y + 1, c, part.at[1])
    got("c1", crecv.at[1])
    ysend[0][low, :] = (part[1, low, :] + crecv[1, low, :].astype(F32)).astype(BF16)
    send("f+a", ysend[0].at[low], frecv.at[0, low], up)
    to_sibling(2, 3)
    forward(y + 3, c, part.at[2])
    got("c2", crecv.at[2])
    ysend[1][top, :] = (part[2, top, :] + crecv[2, top, :].astype(F32)).astype(BF16)
    send("f-a", ysend[1].at[top], frecv.at[1, top], down)

    place = iota((BLOCK, BLOCK), 1)
    source = ((place >> 5) & 3) * 128 + (place >> 7) * 32 + (place & 31)
    perm[...] = (iota((BLOCK, BLOCK), 0) == source).astype(F32).astype(BF16)

    settle("c0", "c0b", "c1", "c2")

    @pl.loop(0, LIVE // 272)
    def _(i):
        rows = pl.ds(pl.multiple_of(i * 272, 16), 272)
        for l in range(3):
            whole_rows = jnp.concatenate(
                [xc[rows, q * FEATS + l * 128 : q * FEATS + (l + 1) * 128] for q in range(4)], axis=1
            )
            swapped = jnp.dot(whole_rows, perm[...], preferred_element_type=F32).astype(BF16)
            for q in range(4):
                xcb[rows, q * FEATS + l * 128 : q * FEATS + (l + 1) * 128] = swapped[:, q * 128 : (q + 1) * 128]

    exchange(1, xcb)
    got("h+", hrecv.at[0])
    ysend[0][top, :] = (part[1, top, :] + crecv[1, top, :].astype(F32) + hrecv[0].astype(F32)).astype(BF16)
    send("f+b", ysend[0].at[top], frecv.at[0, top], up)
    got("h-", hrecv.at[1])
    ysend[1][low, :] = (part[2, low, :] + crecv[2, low, :].astype(F32) + hrecv[1].astype(F32)).astype(BF16)
    send("f-b", ysend[1].at[low], frecv.at[1, low], down)
    to_sibling(3, 0)
    forward(y, c, part.at[0])
    turned_expand = (iota((SLOTS, REQS), 0) >> 3 == iota((SLOTS, REQS), 1)).astype(F32).astype(BF16)
    loads[3].wait()

    @pl.loop(0, LIVE // 272)
    def _(i):
        rows = pl.ds(pl.multiple_of(i * 272, 16), 272)
        chosen = pick[rows, :]
        wanted[rows, :] = jnp.dot(chosen, tgt[...], preferred_element_type=F32).astype(BF16)
        owner[rows, :] = jnp.dot(chosen, turned_expand, preferred_element_type=F32)


    for h in range(2):
        own_copies[h].wait()
        for j in (1, 2, 3):
            got(f"x{h}{j}", xg.at[h, rows_of(me[h] + 4 - j), :])

        @pl.loop(0, ALL // 128)
        def _(k):
            places = pl.ds(pl.multiple_of(k * 128, 128), 128)
            turned = xg[h, places, :].T
            for q in range(4):
                for l in range(3):
                    xgt[h, q * ROWS_OUT + l * 32 : q * ROWS_OUT + (l + 1) * 32, places] = turned[
                        l * 128 + q * 32 : l * 128 + (q + 1) * 32, :
                    ]

    got("c3", crecv.at[3])
    got("f+a", frecv.at[0, low])
    got("f-a", frecv.at[1, top])
    got("f+b", frecv.at[0, top])
    got("f-b", frecv.at[1, low])
    gains = gain_ref[pl.ds(t * 4, 4), :]
    gain = jnp.concatenate([gains[k : k + 1, :] for k in range(4)], axis=1)
    stc[...] = jnp.zeros_like(stc)
    lane = iota((CHUNK, 128), 1)

    @pl.loop(0, LIVE // CHUNK)
    def _(i):
        rows = pl.ds(pl.multiple_of(i * CHUNK, CHUNK), CHUNK)
        joined = part[0, rows, :] + crecv[3, rows, :].astype(F32)
        joined = joined + (frecv[0, rows, :].astype(F32) + frecv[1, rows, :].astype(F32))
        part[0, rows, :] = joined
        goal = wanted[rows, :].astype(F32)
        scaled = joined * gain
        sums = [joined * joined, scaled * scaled, scaled * goal, goal * goal]
        row = jnp.zeros((CHUNK, 128), F32)
        for k, term in enumerate(sums):
            row = jnp.where(lane == k, jnp.sum(term, axis=1, keepdims=True), row)
        count = jnp.sum(owner[rows, :] * counts, axis=1, keepdims=True)
        stc[rows, :] = jnp.where(lane == 4, count, row)

    turned = stc[...].T
    count_row = jnp.maximum(turned[4:5, :], 1.0)
    stat[pl.ds(t, 1)] = turned[None, 0:8, :]
    for j in range(1, 8):
        send(f"s{j}", stat.at[t], stat.at[t], {"tp": (t + j) % 8, "dp": d})
    for j in range(1, 8):
        got(f"s{j}", stat.at[(t + 8 - j) % 8])
    total = stat[0]
    for j in range(1, 8):
        total = total + stat[j]
    inv_rms = lax.rsqrt(total[0:1] / OUT + 1e-05)
    weight_row = 2.0 / (OUT * count_row)
    row_loss = (inv_rms * inv_rms * total[1:2] - 2.0 * inv_rms * total[2:3] + total[3:4]) / OUT
    inner = weight_row * (inv_rms * total[1:2] - total[2:3])
    str_[...] = jnp.zeros_like(str_)
    str_[0:1, :] = inv_rms
    str_[1:2, :] = inv_rms * weight_row
    str_[2:3, :] = inv_rms * inv_rms * inv_rms * inner / OUT
    str_[3:4, :] = row_loss
    stc[...] = str_[...].T

    @pl.loop(0, LIVE // CHUNK)
    def _(i):
        rows = pl.ds(pl.multiple_of(i * CHUNK, CHUNK), CHUNK)
        joined = part[0, rows, :]
        stats = stc[rows, :]
        err = joined * stats[:, 0:1] * gain - wanted[rows, :].astype(F32)
        value = (stats[:, 1:2] * gain * err - joined * stats[:, 2:3]).astype(BF16)
        for h in range(2):
            there = pl.ds(pl.multiple_of(me[h] * LIVE + i * CHUNK, CHUNK), CHUNK)
            df[h, t, there, :] = value[:, h * PART : (h + 1) * PART]

    def block(h, yy, place, half=None):
        start, size = (0, LIVE) if half is None else (half * HALF, HALF)
        rows = pl.ds(pl.multiple_of((place % 4) * LIVE + start, 16), size)
        return df.at[h, (yy % 4) * 2 + c, rows, :]

    def put(name, ref, device):
        send(name, ref, ref, device)

    def put_y(h):
        put(f"y{h}+", block(h, y, me[h]), up)
        put(f"y{h}-", block(h, y, me[h]), down)

    def pass_y(h):
        got(f"y{h}+", block(h, y + 3, me[h]))
        put(f"yf{h}+", block(h, y + 3, me[h], 0), up)
        got(f"y{h}-", block(h, y + 1, me[h]))
        put(f"yf{h}-", block(h, y + 1, me[h], 1), down)

    def end_y(h):
        got(f"yf{h}+", block(h, y + 2, me[h], 0))
        got(f"yf{h}-", block(h, y + 2, me[h], 1))

    def put_axis(h, b):
        put(f"a{h}{b}+", block(h, y + STEP[b], me[h]), axis(h, 1))
        put(f"a{h}{b}-", block(h, y + STEP[b], me[h]), axis(h, 3))

    def pass_axis(h, b):
        got(f"a{h}{b}+", block(h, y + STEP[b], me[h] + 3))
        put(f"af{h}{b}+", block(h, y + STEP[b], me[h] + 3, 0), axis(h, 1))
        got(f"a{h}{b}-", block(h, y + STEP[b], me[h] + 1))
        put(f"af{h}{b}-", block(h, y + STEP[b], me[h] + 1, 1), axis(h, 3))

        share(h, b, 0, 1, 3)

    def end_axis(h, b):
        got(f"af{h}{b}+", block(h, y + STEP[b], me[h] + 2, 0))
        got(f"af{h}{b}-", block(h, y + STEP[b], me[h] + 2, 1))
        share(h, b, 2)

    def put_whole(h):
        for j in (1, 3, 2):
            put(f"v{h}{j}", block(h, y, me[h] + j), at(y=y + TURN[h]))

    def end_whole(h):
        for j in (1, 3, 2):
            got(f"v{h}{j}", block(h, y + 4 - TURN[h], me[h] + j))
            share(h, WHOLE[h], j)

    def share(h, b, *steps):
        for k in steps:
            put(f"d{h}{b}{k}", block(h, y + STEP[b], me[h] + k), sibling)

    def shared(h, b):
        for k in range(4):
            rows = rows_of(me[h] + k)
            got(f"d{h}{b}{k}", df.at[h, block_of(b, 1), rows, :])

    def block_of(b, o):
        return ((y + STEP[b]) % 4) * 2 + (c if o == 0 else 1 - c)

    def across(h, step):
        return axis(1 - h, step)

    def grad(h, b, o):
        if o == 1:
            shared(h, b)
        cols = pl.ds(pl.multiple_of(block_of(b, o) * PART, PART), PART)
        gs[h, :, cols] = jnp.dot(xgt[h], df[h, block_of(b, o)], preferred_element_type=F32).astype(BF16)
        for j in (2, 1, 3):
            rows = pl.ds(pl.multiple_of(((me[1 - h] + j) % 4) * ROWS_OUT, 32), ROWS_OUT)
            send(f"g{h}{b}{o}{j}", gs.at[h, rows, cols], gr.at[h, j - 1, :, cols], across(h, j))

    def finish(h, b, o):
        column = block_of(b, o) * BLOCK + h * PART
        cols = pl.ds(pl.multiple_of(block_of(b, o) * PART, PART), PART)
        wide = pl.ds(pl.multiple_of(column, PART), PART)
        for j in (1, 2, 3):
            got(f"g{h}{b}{o}{j}", gr.at[h, j - 1, :, cols])
        largest = jnp.zeros((1, PART), F32)
        for l in range(3):
            mine = pl.ds(pl.multiple_of(me[1 - h] * ROWS_OUT + l * 32, 32), 32)
            there = pl.ds(pl.multiple_of(z * FEATS + l * 128 + x * 32, 32), 32)
            here = pl.ds(l * 32, 32)
            total = gs[h, mine, cols].astype(F32)
            for j in range(3):
                total = total + gr[h, j, here, cols].astype(F32)
            new = wv[there, wide].astype(F32) - learn_rate * total
            upd[l, :, wide] = new
            largest = jnp.maximum(largest, jnp.max(jnp.abs(new), axis=0, keepdims=True))
        for k in range(PART // 128):
            mx[pl.ds(column // 128 + k, 1), :] = largest[:, k * 128 : (k + 1) * 128]

    early = tuple(sent)
    for h in range(2):
        put_y(h)
        put_axis(h, 0)

    loss_rows = stc[0:LIVE, 3:4] * owner[...]
    request_loss = jnp.sum(loss_rows, axis=0, keepdims=True) / counts
    slots = slots_ref[...]
    places = (slots >> 7) * 8 + (slots & 127) - d * 8
    hit = places == iota((REQS, REQS), 0)
    by_place = jnp.sum(jnp.where(hit, request_loss, 0.0), axis=1, keepdims=True)
    eye = iota((REQS, REQS), 0) == iota((REQS, REQS), 1)
    by_place = jnp.sum(jnp.where(eye, by_place, 0.0), axis=0, keepdims=True)
    dpr[pl.ds(d, 1), 32:40, :] = jnp.broadcast_to(by_place[None], (1, 8, 128))

    settle(*early)
    for h in range(2):
        pass_axis(h, 0)
    for h in range(2):
        pass_y(h)
        put_axis(h, ALONG[h][1])
    for h in range(2):
        end_axis(h, 0)
        grad(h, 0, 0)
    for h in range(2):
        end_y(h)
        put_axis(h, 3)
        put_whole(h)
    for h in range(2):
        share(h, WHOLE[h], 0)
        grad(h, 0, 1)
    for h in range(2):
        pass_axis(h, ALONG[h][1])
    for h in range(2):
        end_axis(h, ALONG[h][1])
        grad(h, ALONG[h][1], 0)
    for h in range(2):
        grad(h, ALONG[h][1], 1)
    for h in range(2):
        pass_axis(h, 3)
    for h in range(2):
        finish(h, 0, 0)
        finish(h, 0, 1)
    for h in range(2):
        end_axis(h, 3)
        grad(h, 3, 0)
    for h in range(2):
        grad(h, 3, 1)
    for h in range(2):
        for o in range(2):
            finish(h, ALONG[h][1], o)
    for h in range(2):
        end_whole(h)
        grad(h, WHOLE[h], 0)
    for h in range(2):
        grad(h, WHOLE[h], 1)
    settle(*(name for name in tuple(sent) if name[0] != "g"))
    for h in range(2):
        for o in range(2):
            finish(h, 3, o)
    for h in range(2):
        for o in range(2):
            finish(h, WHOLE[h], o)

    for j in range(1, 8):
        send(f"m{j}", mx, mxr.at[j - 1], {"tp": (t + j) % 8, "dp": d})
    settle(*(name for name in tuple(sent) if name[0] == "g"))
    most = mx[...]
    for j in range(1, 8):
        got(f"m{j}", mxr.at[j - 1])
        most = jnp.maximum(most, mxr[j - 1])
    dpr[pl.ds(d, 1), 0:32, :] = most[None]
    for j in range(1, 16):
        send(f"n{j}", dpr.at[d], dpr.at[d], {"tp": t, "dp": (d + j) % 16})
    for j in range(1, 16):
        got(f"n{j}", dpr.at[(d + 16 - j) % 16])
    for j in range(16):
        most = jnp.maximum(most, dpr[j, 0:32, :])
        sprd[j * 8 : (j + 1) * 8, :] = dpr[j, 32:40, :]
    small_ref[0:32, :] = most + 1e-06
    lanes = iota((REQS, REQS), 1) == d * 8 + (iota((REQS, REQS), 0) & 7)
    mine = jnp.sum(jnp.where(lanes, sprd[...], 0.0), axis=1, keepdims=True)
    loss = jnp.sum(jnp.where(eye, mine, 0.0), axis=0, keepdims=True)
    small_ref[32:40, :] = jnp.broadcast_to(loss, (8, 128))
    settle()


def scaled(upd, small, loss_ref, serve_ref, scale_ref):
    scale_ref[...] = small[0:32, :]
    loss_ref[...] = small[32:33, :]
    for k in range(OUT // 128):
        cols = slice(k * 128, (k + 1) * 128)
        serve_ref[:, :, cols] = (upd[:, :, cols] / small[k : k + 1, :][None]).astype(BF16)


def shards(hidden_rows, target_rows, row_counts, seq_slot, joining_weight, norm_gain):
    any_spec = pl.BlockSpec(memory_space=pl.ANY)
    vmem = pl.BlockSpec(memory_space=pltpu.VMEM)
    n = len(IDS)
    upd, small = pl.pallas_call(
        kernel,
        out_shape=(
            jax.ShapeDtypeStruct((3, 32, OUT), F32),
            jax.ShapeDtypeStruct((40, 128), F32),
        ),
        in_specs=[any_spec, any_spec, vmem, vmem, any_spec, vmem],
        out_specs=(vmem, vmem),
        scratch_shapes=[
            pltpu.VMEM((3, SLOTS, BLOCK), BF16),
            pltpu.VMEM((SLOTS, BLOCK), BF16),
            pltpu.VMEM((4 * FEATS, OUT), BF16),
            pltpu.VMEM((LIVE, SLOTS), BF16),
            pltpu.VMEM((BLOCK, BLOCK), BF16),
            pltpu.VMEM((LIVE, 4 * FEATS), BF16),
            pltpu.VMEM((LIVE, 4 * FEATS), BF16),
            pltpu.VMEM((LIVE, BLOCK), BF16),
            pltpu.VMEM((4, LIVE, BLOCK), BF16),
            pltpu.VMEM((3, LIVE, BLOCK), F32),
            pltpu.VMEM((2, HALF, BLOCK), BF16),
            pltpu.VMEM((2, LIVE, BLOCK), BF16),
            pltpu.VMEM((2, ALL, FEATS), BF16),
            pltpu.VMEM((2, FEATS, ALL), BF16),
            pltpu.VMEM((2, 8, ALL, PART), BF16),
            pltpu.VMEM((2, FEATS, 8 * PART), BF16),
            pltpu.VMEM((2, 3, ROWS_OUT, 8 * PART), BF16),
            pltpu.VMEM((LIVE, REQS), F32),
            pltpu.VMEM((PAD, 128), F32),
            pltpu.VMEM((128, PAD), F32),
            pltpu.VMEM((8, 8, PAD), F32),
            pltpu.VMEM((32, 128), F32),
            pltpu.VMEM((7, 32, 128), F32),
            pltpu.VMEM((16, 40, 128), F32),
            pltpu.VMEM((REQS, 128), F32),
            pltpu.SemaphoreType.DMA((18,)),
            pltpu.SemaphoreType.DMA((n,)),
            pltpu.SemaphoreType.DMA((n,)),
        ],
        compiler_params=pltpu.CompilerParams(
            collective_id=0, has_side_effects=True, vmem_limit_bytes=64 * 2**20 - 2**18
        ),
        name="joining_step",
    )(
        jnp.transpose(hidden_rows, (1, 0, 2)),
        target_rows,
        row_counts.reshape(1, REQS),
        seq_slot.reshape(1, REQS),
        joining_weight,
        norm_gain.reshape(32, 128),
    )
    loss, serve, scale = pl.pallas_call(
        scaled,
        out_shape=(
            jax.ShapeDtypeStruct((1, REQS), F32),
            jax.ShapeDtypeStruct((3, 32, OUT), BF16),
            jax.ShapeDtypeStruct((32, 128), F32),
        ),
        in_specs=[vmem, vmem],
        out_specs=(vmem, vmem, vmem),
        name="scaled",
    )(upd, small)
    return loss.reshape(REQS), serve, scale.reshape(OUT)


def solution(mesh):
    placed = (P("dp", None, "tp"), P("dp", "tp"), P("dp"), P("dp"), P(None, "tp", None), P())
    return jax.shard_map(
        shards,
        mesh=mesh,
        in_specs=placed,
        out_specs=(P("dp"), P(None, ("tp", "dp"), None), P()),
        check_vma=False,
    )
```

```python
import jax
import jax.numpy as jnp
from jax import lax
from jax.experimental import pallas as pl
from jax.experimental.pallas import tpu as pltpu
from jax.sharding import PartitionSpec as P

learn_rate = 1.0

F32, BF16, I32 = jnp.float32, jnp.bfloat16, jnp.int32
EXACT = lax.Precision.HIGHEST
REQS, MOST, SLOTS, LIVE = 128, 8, 1024, 544
HALF = LIVE // 2
PAD = 640
ALL = 4 * LIVE
BLOCK, PART = 512, 256
FEATS = 384
OUT = 4096
ROWS_OUT = 96
CHUNK = 32


def iota(shape, dim):
    return lax.broadcasted_iota(I32, shape, dim)


def names():
    out = [f"x{h}{j}" for h in range(2) for j in (1, 2, 3)] + [f"c{i}" for i in range(4)]
    out += ["c0b", "h+", "h-", "f+a", "f+b", "f-a", "f-b"] + [f"s{j}" for j in range(1, 8)]
    for h in range(2):
        out += [f"{k}{h}{s}" for k in ("y", "yf", "e") for s in "+-"]
        out += [f"{k}{h}{b}{s}" for k in ("a", "af") for b in range(4) for s in "+-"]
        out += [f"v{h}{j}" for j in (1, 2, 3)] + [f"d{h}{b}{k}" for b in range(4) for k in range(4)]
        out += [f"g{h}{b}{o}{j}" for b in range(4) for o in range(2) for j in (1, 2, 3)]
    out += [f"m{j}" for j in range(1, 8)] + [f"n{j}" for j in range(1, 16)]
    return {name: i for i, name in enumerate(out)}


IDS = names()
STEP = (0, 3, 1, 2)
ALONG = ((0, 2, 3), (0, 1, 3))
WHOLE = (1, 2)
TURN = (1, 3)


def kernel(
    hid_hbm, tgt_hbm, counts_ref, slots_ref, w_hbm, gain_ref,
    upd, small_ref,
    hid, tgt, wv, pick, perm, xc, xcb, wanted, crecv, part, hrecv, frecv, xg, xgt, df, gs, gr,
    owner, stc, str_, stat, mx, mxr, dpr, sprd, lsem, ss, rs,
):
    t = lax.axis_index("tp")
    d = lax.axis_index("dp")
    y, c = t // 2, t % 2
    z, x = d // 4, d % 4
    sent = {}

    def at(y=y, c=c, z=z, x=x):
        return {"tp": (y % 4) * 2 + c, "dp": (z % 4) * 4 + x % 4}

    sibling = at(c=1 - c)

    def send(name, src, dst, device):
        i = IDS[name]
        copy = pltpu.make_async_remote_copy(
            src_ref=src, dst_ref=dst, send_sem=ss.at[i], recv_sem=rs.at[i],
            device_id=device, device_id_type=pl.DeviceIdType.MESH,
        )
        copy.start()
        sent[name] = copy

    def settle(*which):
        for name in which or tuple(sent):
            sent.pop(name).wait_send()

    def got(name, ref):
        i = IDS[name]
        pltpu.make_async_remote_copy(
            src_ref=ref, dst_ref=ref, send_sem=ss.at[i], recv_sem=rs.at[i],
            device_id=sibling, device_id_type=pl.DeviceIdType.MESH,
        ).wait_recv()

    loads = [pltpu.make_async_copy(hid_hbm.at[l], hid.at[l], lsem.at[l]) for l in range(3)]
    loads.append(pltpu.make_async_copy(tgt_hbm, tgt, lsem.at[3]))
    weights = []
    for zz in range(4):
        for l in range(3):
            weights.append(
                pltpu.make_async_copy(
                    w_hbm.at[l, pl.ds(zz * 128, 128)],
                    wv.at[pl.ds(zz * FEATS + l * 128, 128)],
                    lsem.at[4 + zz * 3 + l],
                )
            )
    for load in loads[:3]:
        load.start()
    barrier = pltpu.get_barrier_semaphore()
    for j in range(1, 8):
        pl.semaphore_signal(
            barrier, inc=1, device_id={"tp": (t + j) % 8, "dp": d}, device_id_type=pl.DeviceIdType.MESH
        )
    for j in range(1, 16):
        pl.semaphore_signal(
            barrier, inc=1, device_id={"tp": t, "dp": (d + j) % 16}, device_id_type=pl.DeviceIdType.MESH
        )

    counts = counts_ref[...].astype(F32)
    counts8 = jnp.broadcast_to(counts, (8, REQS))
    expand = (iota((REQS, SLOTS), 1) >> 3 == iota((REQS, SLOTS), 0)).astype(F32)
    before = (iota((REQS, REQS), 0) < iota((REQS, REQS), 1)).astype(F32)
    start8 = jnp.dot(counts8, before, precision=EXACT, preferred_element_type=F32)
    count_slot = jnp.dot(counts8, expand, precision=EXACT, preferred_element_type=F32)
    start_slot = jnp.dot(start8, expand, precision=EXACT, preferred_element_type=F32)
    inside = iota((8, SLOTS), 1) & 7
    rank8 = (start_slot + 0.5).astype(I32) + inside
    rank8 = jnp.where(inside < (count_slot + 0.5).astype(I32), rank8, -1)
    rank = rank8[0:1, :]

    @pl.loop(0, LIVE // 272)
    def _(i):
        rows = pl.ds(pl.multiple_of(i * 272, 16), 272)
        hit = iota((272, SLOTS), 0) + i * 272 == rank
        pick[rows, :] = jnp.where(hit, 1.0, 0.0).astype(BF16)

    for load in loads[:3]:
        load.wait()
    loads[3].start()
    for load in weights:
        load.start()

    @pl.loop(0, LIVE // 272)
    def _(i):
        rows = pl.ds(pl.multiple_of(i * 272, 16), 272)
        chosen = pick[rows, :]
        for l in range(3):
            got_rows = jnp.dot(chosen, hid[l], preferred_element_type=F32).astype(BF16)
            for q in range(4):
                cols = slice(q * FEATS + l * 128, q * FEATS + (l + 1) * 128)
                xc[rows, cols] = got_rows[:, q * 128 : (q + 1) * 128]

    pl.semaphore_wait(barrier, 22)

    def feats(q):
        return pl.ds(pl.multiple_of((q % 4) * FEATS, 128), FEATS)

    def rows_of(q):
        return pl.ds(pl.multiple_of((q % 4) * LIVE, 16), LIVE)

    me = (z, x)

    def axis(h, step):
        return at(z=z + step) if h == 0 else at(x=x + step)

    own_copies = []

    def exchange(h, kept):
        for j in (1, 2, 3):
            send(f"x{h}{j}", kept.at[:, feats(me[h] + j)], xg.at[h, rows_of(me[h]), :], axis(h, j))
        own_copies.append(
            pltpu.make_async_copy(kept.at[:, feats(me[h])], xg.at[h, rows_of(me[h]), :], lsem.at[16 + h])
        )
        own_copies[h].start()

    exchange(0, xc)
    for load in weights:
        load.wait()

    def forward(yy, core, dst, rows=slice(None)):
        column = ((yy % 4) * 2 + core) * BLOCK

        @pl.loop(0, 2)
        def _(i):
            cols = pl.ds(pl.multiple_of(column + i * PART, PART), PART)
            dst[rows, pl.ds(pl.multiple_of(i * PART, PART), PART)] = jnp.dot(
                xc[rows, :], wv[:, cols], preferred_element_type=F32
            ).astype(dst.dtype)

    csend = [xcb.at[:, i * BLOCK : (i + 1) * BLOCK] for i in range(3)] + [hid.at[2, pl.ds(0, LIVE)]]
    ysend = [hid.at[i, pl.ds(0, LIVE)] for i in range(2)]
    yhalf = [hid.at[i, pl.ds(LIVE, HALF)] for i in range(2)]

    def to_sibling(i, step):
        forward(y + step, 1 - c, csend[i])
        send(f"c{i}", csend[i], crecv.at[i], sibling)

    up, down = at(y=y + 1), at(y=y + 3)
    top, low = pl.ds(0, HALF), pl.ds(HALF, HALF)
    for rows, name in ((top, "c0"), (low, "c0b")):
        forward(y + 2, 1 - c, csend[0], rows)
        send(name, csend[0].at[rows], crecv.at[0, rows], sibling)
        forward(y + 2, c, part.at[0], rows)
    for k, (rows, name, there, device) in enumerate(((top, "c0", "h+", up), (low, "c0b", "h-", down))):
        got(name, crecv.at[0, rows])
        yhalf[k][...] = (part[0, rows, :] + crecv[0, rows, :].astype(F32)).astype(BF16)
        send(there, yhalf[k], hrecv.at[k], device)
    to_sibling(1, 1)
    forward(y + 1, c, part.at[1])
    got("c1", crecv.at[1])
    ysend[0][low, :] = (part[1, low, :] + crecv[1, low, :].astype(F32)).astype(BF16)
    send("f+a", ysend[0].at[low], frecv.at[0, low], up)
    to_sibling(2, 3)
    forward(y + 3, c, part.at[2])
    got("c2", crecv.at[2])
    ysend[1][top, :] = (part[2, top, :] + crecv[2, top, :].astype(F32)).astype(BF16)
    send("f-a", ysend[1].at[top], frecv.at[1, top], down)

    place = iota((BLOCK, BLOCK), 1)
    source = ((place >> 5) & 3) * 128 + (place >> 7) * 32 + (place & 31)
    perm[...] = (iota((BLOCK, BLOCK), 0) == source).astype(F32).astype(BF16)

    settle("c0", "c0b", "c1", "c2")

    @pl.loop(0, LIVE // 272)
    def _(i):
        rows = pl.ds(pl.multiple_of(i * 272, 16), 272)
        for l in range(3):
            whole_rows = jnp.concatenate(
                [xc[rows, q * FEATS + l * 128 : q * FEATS + (l + 1) * 128] for q in range(4)], axis=1
            )
            swapped = jnp.dot(whole_rows, perm[...], preferred_element_type=F32).astype(BF16)
            for q in range(4):
                xcb[rows, q * FEATS + l * 128 : q * FEATS + (l + 1) * 128] = swapped[:, q * 128 : (q + 1) * 128]

    exchange(1, xcb)
    got("h+", hrecv.at[0])
    ysend[0][top, :] = (part[1, top, :] + crecv[1, top, :].astype(F32) + hrecv[0].astype(F32)).astype(BF16)
    send("f+b", ysend[0].at[top], frecv.at[0, top], up)
    got("h-", hrecv.at[1])
    ysend[1][low, :] = (part[2, low, :] + crecv[2, low, :].astype(F32) + hrecv[1].astype(F32)).astype(BF16)
    send("f-b", ysend[1].at[low], frecv.at[1, low], down)
    to_sibling(3, 0)
    forward(y, c, part.at[0])
    turned_expand = (iota((SLOTS, REQS), 0) >> 3 == iota((SLOTS, REQS), 1)).astype(F32).astype(BF16)
    loads[3].wait()

    @pl.loop(0, LIVE // 272)
    def _(i):
        rows = pl.ds(pl.multiple_of(i * 272, 16), 272)
        chosen = pick[rows, :]
        wanted[rows, :] = jnp.dot(chosen, tgt[...], preferred_element_type=F32).astype(BF16)
        owner[rows, :] = jnp.dot(chosen, turned_expand, preferred_element_type=F32)


    got("c3", crecv.at[3])
    got("f+a", frecv.at[0, low])
    got("f-a", frecv.at[1, top])
    got("f+b", frecv.at[0, top])
    got("f-b", frecv.at[1, low])
    gains = gain_ref[pl.ds(t * 4, 4), :]
    gain = jnp.concatenate([gains[k : k + 1, :] for k in range(4)], axis=1)
    stc[...] = jnp.zeros_like(stc)
    lane = iota((CHUNK, 128), 1)

    @pl.loop(0, LIVE // CHUNK)
    def _(i):
        rows = pl.ds(pl.multiple_of(i * CHUNK, CHUNK), CHUNK)
        joined = part[0, rows, :] + crecv[3, rows, :].astype(F32)
        joined = joined + (frecv[0, rows, :].astype(F32) + frecv[1, rows, :].astype(F32))
        part[0, rows, :] = joined
        goal = wanted[rows, :].astype(F32)
        scaled = joined * gain
        sums = [joined * joined, scaled * scaled, scaled * goal, goal * goal]
        row = jnp.zeros((CHUNK, 128), F32)
        for k, term in enumerate(sums):
            row = jnp.where(lane == k, jnp.sum(term, axis=1, keepdims=True), row)
        count = jnp.sum(owner[rows, :] * counts, axis=1, keepdims=True)
        stc[rows, :] = jnp.where(lane == 4, count, row)

    turned = stc[...].T
    count_row = jnp.maximum(turned[4:5, :], 1.0)
    stat[pl.ds(t, 1)] = turned[None, 0:8, :]
    for j in range(1, 8):
        send(f"s{j}", stat.at[t], stat.at[t], {"tp": (t + j) % 8, "dp": d})
    for j in range(1, 8):
        got(f"s{j}", stat.at[(t + 8 - j) % 8])
    total = stat[0]
    for j in range(1, 8):
        total = total + stat[j]
    inv_rms = lax.rsqrt(total[0:1] / OUT + 1e-05)
    weight_row = 2.0 / (OUT * count_row)
    row_loss = (inv_rms * inv_rms * total[1:2] - 2.0 * inv_rms * total[2:3] + total[3:4]) / OUT
    inner = weight_row * (inv_rms * total[1:2] - total[2:3])
    str_[...] = jnp.zeros_like(str_)
    str_[0:1, :] = inv_rms
    str_[1:2, :] = inv_rms * weight_row
    str_[2:3, :] = inv_rms * inv_rms * inv_rms * inner / OUT
    str_[3:4, :] = row_loss
    stc[...] = str_[...].T

    @pl.loop(0, LIVE // CHUNK)
    def _(i):
        rows = pl.ds(pl.multiple_of(i * CHUNK, CHUNK), CHUNK)
        joined = part[0, rows, :]
        stats = stc[rows, :]
        err = joined * stats[:, 0:1] * gain - wanted[rows, :].astype(F32)
        value = (stats[:, 1:2] * gain * err - joined * stats[:, 2:3]).astype(BF16)
        for h in range(2):
            there = pl.ds(pl.multiple_of(me[h] * LIVE + i * CHUNK, CHUNK), CHUNK)
            df[h, t, there, :] = value[:, h * PART : (h + 1) * PART]

    def block(h, yy, place, half=None):
        start, size = (0, LIVE) if half is None else (half * HALF, HALF)
        rows = pl.ds(pl.multiple_of((place % 4) * LIVE + start, 16), size)
        return df.at[h, (yy % 4) * 2 + c, rows, :]

    def put(name, ref, device):
        send(name, ref, ref, device)

    up_first = (False, True)
    early_half = (1, 0)

    def put_y(h, second):
        if up_first[h] != second:
            put(f"y{h}+", block(h, y, me[h]), up)
        else:
            put(f"y{h}-", block(h, y, me[h]), down)

    def pass_y(h, second):
        if up_first[h] != second:
            got(f"y{h}+", block(h, y + 3, me[h]))
            put(f"yf{h}+", block(h, y + 3, me[h], 0), up)
        else:
            got(f"y{h}-", block(h, y + 1, me[h]))
            put(f"yf{h}-", block(h, y + 1, me[h], 1), down)

    def end_y(h, half):
        got(f"yf{h}" + "+-"[half], block(h, y + 2, me[h], half))

    def put_far(h, half):
        name = "e" if half == early_half[h] else "a"
        last = "" if name == "e" else "3"
        put(f"{name}{h}{last}+", block(h, y + 2, me[h], half), axis(h, 1))
        put(f"{name}{h}{last}-", block(h, y + 2, me[h], half), axis(h, 3))

    def pass_far(h):
        half = early_half[h]
        got(f"e{h}+", block(h, y + 2, me[h] + 3, half))
        put(f"af{h}3+", block(h, y + 2, me[h] + 3, half), axis(h, 1))
        got(f"e{h}-", block(h, y + 2, me[h] + 1, half))
        half = 1 - half
        got(f"a{h}3-", block(h, y + 2, me[h] + 1, half))
        put(f"af{h}3-", block(h, y + 2, me[h] + 1, half), axis(h, 3))
        got(f"a{h}3+", block(h, y + 2, me[h] + 3, half))
        share(h, 3, 0, 1, 3)

    def end_far(h):
        got(f"af{h}3+", block(h, y + 2, me[h] + 2, early_half[h]))
        got(f"af{h}3-", block(h, y + 2, me[h] + 2, 1 - early_half[h]))
        share(h, 3, 2)

    def put_axis(h, b):
        put(f"a{h}{b}+", block(h, y + STEP[b], me[h]), axis(h, 1))
        put(f"a{h}{b}-", block(h, y + STEP[b], me[h]), axis(h, 3))

    def pass_axis(h, b):
        got(f"a{h}{b}+", block(h, y + STEP[b], me[h] + 3))
        put(f"af{h}{b}+", block(h, y + STEP[b], me[h] + 3, 0), axis(h, 1))
        got(f"a{h}{b}-", block(h, y + STEP[b], me[h] + 1))
        put(f"af{h}{b}-", block(h, y + STEP[b], me[h] + 1, 1), axis(h, 3))

        share(h, b, 0, 1, 3)

    def end_axis(h, b):
        got(f"af{h}{b}+", block(h, y + STEP[b], me[h] + 2, 0))
        got(f"af{h}{b}-", block(h, y + STEP[b], me[h] + 2, 1))
        share(h, b, 2)

    def put_whole(h, *steps):
        for j in steps:
            put(f"v{h}{j}", block(h, y, me[h] + j), at(y=y + TURN[h]))

    def end_whole(h):
        for j in (1, 3, 2):
            got(f"v{h}{j}", block(h, y + 4 - TURN[h], me[h] + j))
            share(h, WHOLE[h], j)

    def share(h, b, *steps):
        for k in steps:
            put(f"d{h}{b}{k}", block(h, y + STEP[b], me[h] + k), sibling)

    def shared(h, b):
        for k in range(4):
            rows = rows_of(me[h] + k)
            got(f"d{h}{b}{k}", df.at[h, block_of(b, 1), rows, :])

    def block_of(b, o):
        return ((y + STEP[b]) % 4) * 2 + (c if o == 0 else 1 - c)

    def across(h, step):
        return axis(1 - h, step)

    def grad(h, b, o):
        if o == 1:
            shared(h, b)
        cols = pl.ds(pl.multiple_of(block_of(b, o) * PART, PART), PART)
        gs[h, :, cols] = jnp.dot(xgt[h], df[h, block_of(b, o)], preferred_element_type=F32).astype(BF16)
        for j in (2, 1, 3):
            rows = pl.ds(pl.multiple_of(((me[1 - h] + j) % 4) * ROWS_OUT, 32), ROWS_OUT)
            send(f"g{h}{b}{o}{j}", gs.at[h, rows, cols], gr.at[h, j - 1, :, cols], across(h, j))

    def finish(h, b, o):
        column = block_of(b, o) * BLOCK + h * PART
        cols = pl.ds(pl.multiple_of(block_of(b, o) * PART, PART), PART)
        wide = pl.ds(pl.multiple_of(column, PART), PART)
        for j in (1, 2, 3):
            got(f"g{h}{b}{o}{j}", gr.at[h, j - 1, :, cols])
        largest = jnp.zeros((1, PART), F32)
        for l in range(3):
            mine = pl.ds(pl.multiple_of(me[1 - h] * ROWS_OUT + l * 32, 32), 32)
            there = pl.ds(pl.multiple_of(z * FEATS + l * 128 + x * 32, 32), 32)
            here = pl.ds(l * 32, 32)
            total = gs[h, mine, cols].astype(F32)
            for j in range(3):
                total = total + gr[h, j, here, cols].astype(F32)
            new = wv[there, wide].astype(F32) - learn_rate * total
            upd[l, :, wide] = new
            largest = jnp.maximum(largest, jnp.max(jnp.abs(new), axis=0, keepdims=True))
        for k in range(PART // 128):
            mx[pl.ds(column // 128 + k, 1), :] = largest[:, k * 128 : (k + 1) * 128]

    early = tuple(sent)
    for h in range(2):
        put_y(h, False)
        put_axis(h, 0)

    loss_rows = stc[0:LIVE, 3:4] * owner[...]
    request_loss = jnp.sum(loss_rows, axis=0, keepdims=True) / counts
    slots = slots_ref[...]
    places = (slots >> 7) * 8 + (slots & 127) - d * 8
    hit = places == iota((REQS, REQS), 0)
    by_place = jnp.sum(jnp.where(hit, request_loss, 0.0), axis=1, keepdims=True)
    eye = iota((REQS, REQS), 0) == iota((REQS, REQS), 1)
    by_place = jnp.sum(jnp.where(eye, by_place, 0.0), axis=0, keepdims=True)
    dpr[pl.ds(d, 1), 32:40, :] = jnp.broadcast_to(by_place[None], (1, 8, 128))

    settle(*early)
    for h in range(2):
        own_copies[h].wait()
        for j in (1, 2, 3):
            got(f"x{h}{j}", xg.at[h, rows_of(me[h] + 4 - j), :])

        @pl.loop(0, ALL // 128)
        def _(k):
            places = pl.ds(pl.multiple_of(k * 128, 128), 128)
            turned = xg[h, places, :].T
            for q in range(4):
                for l in range(3):
                    xgt[h, q * ROWS_OUT + l * 32 : q * ROWS_OUT + (l + 1) * 32, places] = turned[
                        l * 128 + q * 32 : l * 128 + (q + 1) * 32, :
                    ]

    for h in range(2):
        pass_axis(h, 0)
    for h in range(2):
        pass_y(h, False)
        put_axis(h, ALONG[h][1])
    for h in range(2):
        put_y(h, True)
    for h in range(2):
        end_axis(h, 0)
        grad(h, 0, 0)
    for h in range(2):
        end_y(h, early_half[h])
        put_far(h, early_half[h])
    for h in range(2):
        pass_y(h, True)
        put_whole(h, 1)
        share(h, WHOLE[h], 0)
    for h in range(2):
        grad(h, 0, 1)
    for h in range(2):
        pass_axis(h, ALONG[h][1])
    for h in range(2):
        end_y(h, 1 - early_half[h])
        put_far(h, 1 - early_half[h])
        put_whole(h, 3, 2)
    for h in range(2):
        end_axis(h, ALONG[h][1])
        grad(h, ALONG[h][1], 0)
    for h in range(2):
        grad(h, ALONG[h][1], 1)
    for h in range(2):
        pass_far(h)
    for h in range(2):
        finish(h, 0, 0)
        finish(h, 0, 1)
    for h in range(2):
        end_far(h)
        grad(h, 3, 0)
    for h in range(2):
        grad(h, 3, 1)
    for h in range(2):
        for o in range(2):
            finish(h, ALONG[h][1], o)
    for h in range(2):
        end_whole(h)
        grad(h, WHOLE[h], 0)
    for h in range(2):
        grad(h, WHOLE[h], 1)
    settle(*(name for name in tuple(sent) if name[0] != "g"))
    for h in range(2):
        for o in range(2):
            finish(h, 3, o)
    for h in range(2):
        for o in range(2):
            finish(h, WHOLE[h], o)

    for j in range(1, 8):
        send(f"m{j}", mx, mxr.at[j - 1], {"tp": (t + j) % 8, "dp": d})
    settle(*(name for name in tuple(sent) if name[0] == "g"))
    most = mx[...]
    for j in range(1, 8):
        got(f"m{j}", mxr.at[j - 1])
        most = jnp.maximum(most, mxr[j - 1])
    dpr[pl.ds(d, 1), 0:32, :] = most[None]
    for j in range(1, 16):
        send(f"n{j}", dpr.at[d], dpr.at[d], {"tp": t, "dp": (d + j) % 16})
    for j in range(1, 16):
        got(f"n{j}", dpr.at[(d + 16 - j) % 16])
    for j in range(16):
        most = jnp.maximum(most, dpr[j, 0:32, :])
        sprd[j * 8 : (j + 1) * 8, :] = dpr[j, 32:40, :]
    small_ref[0:32, :] = most + 1e-06
    lanes = iota((REQS, REQS), 1) == d * 8 + (iota((REQS, REQS), 0) & 7)
    mine = jnp.sum(jnp.where(lanes, sprd[...], 0.0), axis=1, keepdims=True)
    loss = jnp.sum(jnp.where(eye, mine, 0.0), axis=0, keepdims=True)
    small_ref[32:40, :] = jnp.broadcast_to(loss, (8, 128))
    settle()


def scaled(upd, small, loss_ref, serve_ref, scale_ref):
    scale_ref[...] = small[0:32, :]
    loss_ref[...] = small[32:33, :]
    for k in range(OUT // 128):
        cols = slice(k * 128, (k + 1) * 128)
        serve_ref[:, :, cols] = (upd[:, :, cols] / small[k : k + 1, :][None]).astype(BF16)


def shards(hidden_rows, target_rows, row_counts, seq_slot, joining_weight, norm_gain):
    any_spec = pl.BlockSpec(memory_space=pl.ANY)
    vmem = pl.BlockSpec(memory_space=pltpu.VMEM)
    n = len(IDS)
    upd, small = pl.pallas_call(
        kernel,
        out_shape=(
            jax.ShapeDtypeStruct((3, 32, OUT), F32),
            jax.ShapeDtypeStruct((40, 128), F32),
        ),
        in_specs=[any_spec, any_spec, vmem, vmem, any_spec, vmem],
        out_specs=(vmem, vmem),
        scratch_shapes=[
            pltpu.VMEM((3, SLOTS, BLOCK), BF16),
            pltpu.VMEM((SLOTS, BLOCK), BF16),
            pltpu.VMEM((4 * FEATS, OUT), BF16),
            pltpu.VMEM((LIVE, SLOTS), BF16),
            pltpu.VMEM((BLOCK, BLOCK), BF16),
            pltpu.VMEM((LIVE, 4 * FEATS), BF16),
            pltpu.VMEM((LIVE, 4 * FEATS), BF16),
            pltpu.VMEM((LIVE, BLOCK), BF16),
            pltpu.VMEM((4, LIVE, BLOCK), BF16),
            pltpu.VMEM((3, LIVE, BLOCK), F32),
            pltpu.VMEM((2, HALF, BLOCK), BF16),
            pltpu.VMEM((2, LIVE, BLOCK), BF16),
            pltpu.VMEM((2, ALL, FEATS), BF16),
            pltpu.VMEM((2, FEATS, ALL), BF16),
            pltpu.VMEM((2, 8, ALL, PART), BF16),
            pltpu.VMEM((2, FEATS, 8 * PART), BF16),
            pltpu.VMEM((2, 3, ROWS_OUT, 8 * PART), BF16),
            pltpu.VMEM((LIVE, REQS), F32),
            pltpu.VMEM((PAD, 128), F32),
            pltpu.VMEM((128, PAD), F32),
            pltpu.VMEM((8, 8, PAD), F32),
            pltpu.VMEM((32, 128), F32),
            pltpu.VMEM((7, 32, 128), F32),
            pltpu.VMEM((16, 40, 128), F32),
            pltpu.VMEM((REQS, 128), F32),
            pltpu.SemaphoreType.DMA((18,)),
            pltpu.SemaphoreType.DMA((n,)),
            pltpu.SemaphoreType.DMA((n,)),
        ],
        compiler_params=pltpu.CompilerParams(
            collective_id=0, has_side_effects=True, vmem_limit_bytes=64 * 2**20 - 2**18
        ),
        name="joining_step",
    )(
        jnp.transpose(hidden_rows, (1, 0, 2)),
        target_rows,
        row_counts.reshape(1, REQS),
        seq_slot.reshape(1, REQS),
        joining_weight,
        norm_gain.reshape(32, 128),
    )
    loss, serve, scale = pl.pallas_call(
        scaled,
        out_shape=(
            jax.ShapeDtypeStruct((1, REQS), F32),
            jax.ShapeDtypeStruct((3, 32, OUT), BF16),
            jax.ShapeDtypeStruct((32, 128), F32),
        ),
        in_specs=[vmem, vmem],
        out_specs=(vmem, vmem, vmem),
        name="scaled",
    )(upd, small)
    return loss.reshape(REQS), serve, scale.reshape(OUT)


def solution(mesh):
    placed = (P("dp", None, "tp"), P("dp", "tp"), P("dp"), P("dp"), P(None, "tp", None), P())
    return jax.shard_map(
        shards,
        mesh=mesh,
        in_specs=placed,
        out_specs=(P("dp"), P(None, ("tp", "dp"), None), P()),
        check_vma=False,
    )
```

```python
import jax
import jax.numpy as jnp
from jax import lax
from jax.experimental import pallas as pl
from jax.experimental.pallas import tpu as pltpu
from jax.sharding import PartitionSpec as P

learn_rate = 1.0

F32, BF16, I32 = jnp.float32, jnp.bfloat16, jnp.int32
EXACT = lax.Precision.HIGHEST
REQS, MOST, SLOTS, LIVE = 128, 8, 1024, 544
HALF = LIVE // 2
PAD = 640
ALL = 4 * LIVE
BLOCK, PART = 512, 256
FEATS = 384
OUT = 4096
ROWS_OUT = 96
CHUNK = 32


def iota(shape, dim):
    return lax.broadcasted_iota(I32, shape, dim)


def names():
    out = [f"x{h}{j}" for h in range(2) for j in (1, 2, 3)] + [f"c{i}" for i in range(4)]
    out += ["c0b", "h+", "h-", "f+a", "f+b", "f-a", "f-b"] + [f"s{j}" for j in range(1, 8)]
    for h in range(2):
        out += [f"{k}{h}{s}" for k in ("y", "yf", "e") for s in "+-"]
        out += [f"{k}{h}{b}{s}" for k in ("a", "af") for b in range(4) for s in "+-"]
        out += [f"v{h}{j}" for j in (1, 2, 3)] + [f"d{h}{b}{k}" for b in range(4) for k in range(4)]
        out += [f"g{h}{b}{o}{j}" for b in range(4) for o in range(2) for j in (1, 2, 3)]
    out += [f"m{j}" for j in range(1, 8)] + [f"{k}{j}" for k in "no" for j in range(1, 16)]
    return {name: i for i, name in enumerate(out)}


IDS = names()
STEP = (0, 3, 1, 2)
ALONG = ((0, 2, 3), (0, 1, 3))
WHOLE = (1, 2)
TURN = (1, 3)


def kernel(
    hid_hbm, tgt_hbm, counts_ref, slots_ref, w_hbm, gain_ref,
    upd, small_ref,
    hid, tgt, wv, pick, perm, xc, xcb, wanted, crecv, part, hrecv, frecv, xg, xgt, df, gs, gr,
    owner, stc, str_, stat, mxp, mx, mxr, dpr, dpl, sprd, lsem, ss, rs,
):
    t = lax.axis_index("tp")
    d = lax.axis_index("dp")
    y, c = t // 2, t % 2
    z, x = d // 4, d % 4
    sent = {}

    def at(y=y, c=c, z=z, x=x):
        return {"tp": (y % 4) * 2 + c, "dp": (z % 4) * 4 + x % 4}

    sibling = at(c=1 - c)

    def send(name, src, dst, device):
        i = IDS[name]
        copy = pltpu.make_async_remote_copy(
            src_ref=src, dst_ref=dst, send_sem=ss.at[i], recv_sem=rs.at[i],
            device_id=device, device_id_type=pl.DeviceIdType.MESH,
        )
        copy.start()
        sent[name] = copy

    def settle(*which):
        for name in which or tuple(sent):
            sent.pop(name).wait_send()

    def got(name, ref):
        i = IDS[name]
        pltpu.make_async_remote_copy(
            src_ref=ref, dst_ref=ref, send_sem=ss.at[i], recv_sem=rs.at[i],
            device_id=sibling, device_id_type=pl.DeviceIdType.MESH,
        ).wait_recv()

    loads = [pltpu.make_async_copy(hid_hbm.at[l], hid.at[l], lsem.at[l]) for l in range(3)]
    loads.append(pltpu.make_async_copy(tgt_hbm, tgt, lsem.at[3]))
    weights = []
    for zz in range(4):
        for l in range(3):
            weights.append(
                pltpu.make_async_copy(
                    w_hbm.at[l, pl.ds(zz * 128, 128)],
                    wv.at[pl.ds(zz * FEATS + l * 128, 128)],
                    lsem.at[4 + zz * 3 + l],
                )
            )
    for load in loads[:3]:
        load.start()
    barrier = pltpu.get_barrier_semaphore()
    for j in range(1, 8):
        pl.semaphore_signal(
            barrier, inc=1, device_id={"tp": (t + j) % 8, "dp": d}, device_id_type=pl.DeviceIdType.MESH
        )
    for j in range(1, 16):
        pl.semaphore_signal(
            barrier, inc=1, device_id={"tp": t, "dp": (d + j) % 16}, device_id_type=pl.DeviceIdType.MESH
        )

    counts = counts_ref[...].astype(F32)
    counts8 = jnp.broadcast_to(counts, (8, REQS))
    expand = (iota((REQS, SLOTS), 1) >> 3 == iota((REQS, SLOTS), 0)).astype(F32)
    before = (iota((REQS, REQS), 0) < iota((REQS, REQS), 1)).astype(F32)
    start8 = jnp.dot(counts8, before, precision=EXACT, preferred_element_type=F32)
    count_slot = jnp.dot(counts8, expand, precision=EXACT, preferred_element_type=F32)
    start_slot = jnp.dot(start8, expand, precision=EXACT, preferred_element_type=F32)
    inside = iota((8, SLOTS), 1) & 7
    rank8 = (start_slot + 0.5).astype(I32) + inside
    rank8 = jnp.where(inside < (count_slot + 0.5).astype(I32), rank8, -1)
    rank = rank8[0:1, :]

    @pl.loop(0, LIVE // 272)
    def _(i):
        rows = pl.ds(pl.multiple_of(i * 272, 16), 272)
        hit = iota((272, SLOTS), 0) + i * 272 == rank
        pick[rows, :] = jnp.where(hit, 1.0, 0.0).astype(BF16)

    for load in loads[:3]:
        load.wait()
    loads[3].start()
    for load in weights:
        load.start()

    @pl.loop(0, LIVE // 272)
    def _(i):
        rows = pl.ds(pl.multiple_of(i * 272, 16), 272)
        chosen = pick[rows, :]
        for l in range(3):
            got_rows = jnp.dot(chosen, hid[l], preferred_element_type=F32).astype(BF16)
            for q in range(4):
                cols = slice(q * FEATS + l * 128, q * FEATS + (l + 1) * 128)
                xc[rows, cols] = got_rows[:, q * 128 : (q + 1) * 128]

    pl.semaphore_wait(barrier, 22)

    def feats(q):
        return pl.ds(pl.multiple_of((q % 4) * FEATS, 128), FEATS)

    def rows_of(q):
        return pl.ds(pl.multiple_of((q % 4) * LIVE, 16), LIVE)

    me = (z, x)

    def axis(h, step):
        return at(z=z + step) if h == 0 else at(x=x + step)

    own_copies = []

    def exchange(h, kept):
        for j in (1, 2, 3):
            send(f"x{h}{j}", kept.at[:, feats(me[h] + j)], xg.at[h, rows_of(me[h]), :], axis(h, j))
        own_copies.append(
            pltpu.make_async_copy(kept.at[:, feats(me[h])], xg.at[h, rows_of(me[h]), :], lsem.at[16 + h])
        )
        own_copies[h].start()

    exchange(0, xc)
    for load in weights:
        load.wait()

    def forward(yy, core, dst, rows=slice(None)):
        column = ((yy % 4) * 2 + core) * BLOCK

        @pl.loop(0, 2)
        def _(i):
            cols = pl.ds(pl.multiple_of(column + i * PART, PART), PART)
            dst[rows, pl.ds(pl.multiple_of(i * PART, PART), PART)] = jnp.dot(
                xc[rows, :], wv[:, cols], preferred_element_type=F32
            ).astype(dst.dtype)

    csend = [xcb.at[:, 0:BLOCK], hid.at[2, pl.ds(0, LIVE)], wanted, hid.at[2, pl.ds(0, LIVE)]]
    ysend = [hid.at[i, pl.ds(0, LIVE)] for i in range(2)]
    yhalf = [hid.at[i, pl.ds(LIVE, HALF)] for i in range(2)]

    def to_sibling(i, step):
        forward(y + step, 1 - c, csend[i])
        send(f"c{i}", csend[i], crecv.at[i], sibling)

    up, down = at(y=y + 1), at(y=y + 3)
    top, low = pl.ds(0, HALF), pl.ds(HALF, HALF)
    for rows, name in ((top, "c0"), (low, "c0b")):
        forward(y + 2, 1 - c, csend[0], rows)
        send(name, csend[0].at[rows], crecv.at[0, rows], sibling)
        forward(y + 2, c, part.at[0], rows)
    for k, (rows, name, there, device) in enumerate(((top, "c0", "h+", up), (low, "c0b", "h-", down))):
        got(name, crecv.at[0, rows])
        yhalf[k][...] = (part[0, rows, :] + crecv[0, rows, :].astype(F32)).astype(BF16)
        send(there, yhalf[k], hrecv.at[k], device)

    place = iota((BLOCK, BLOCK), 1)
    source = ((place >> 5) & 3) * 128 + (place >> 7) * 32 + (place & 31)
    perm[...] = (iota((BLOCK, BLOCK), 0) == source).astype(F32).astype(BF16)

    settle("c0", "c0b")

    @pl.loop(0, LIVE // 272)
    def _(i):
        rows = pl.ds(pl.multiple_of(i * 272, 16), 272)
        for l in range(3):
            whole_rows = jnp.concatenate(
                [xc[rows, q * FEATS + l * 128 : q * FEATS + (l + 1) * 128] for q in range(4)], axis=1
            )
            swapped = jnp.dot(whole_rows, perm[...], preferred_element_type=F32).astype(BF16)
            for q in range(4):
                xcb[rows, q * FEATS + l * 128 : q * FEATS + (l + 1) * 128] = swapped[:, q * 128 : (q + 1) * 128]

    exchange(1, xcb)
    to_sibling(1, 1)
    forward(y + 1, c, part.at[1])
    got("c1", crecv.at[1])
    ysend[0][low, :] = (part[1, low, :] + crecv[1, low, :].astype(F32)).astype(BF16)
    send("f+a", ysend[0].at[low], frecv.at[0, low], up)
    to_sibling(2, 3)
    forward(y + 3, c, part.at[2])
    got("c2", crecv.at[2])
    ysend[1][top, :] = (part[2, top, :] + crecv[2, top, :].astype(F32)).astype(BF16)
    send("f-a", ysend[1].at[top], frecv.at[1, top], down)
    got("h+", hrecv.at[0])
    ysend[0][top, :] = (part[1, top, :] + crecv[1, top, :].astype(F32) + hrecv[0].astype(F32)).astype(BF16)
    send("f+b", ysend[0].at[top], frecv.at[0, top], up)
    got("h-", hrecv.at[1])
    ysend[1][low, :] = (part[2, low, :] + crecv[2, low, :].astype(F32) + hrecv[1].astype(F32)).astype(BF16)
    send("f-b", ysend[1].at[low], frecv.at[1, low], down)
    settle("c1", "c2")
    to_sibling(3, 0)
    forward(y, c, part.at[0])
    turned_expand = (iota((SLOTS, REQS), 0) >> 3 == iota((SLOTS, REQS), 1)).astype(F32).astype(BF16)
    loads[3].wait()

    @pl.loop(0, LIVE // 272)
    def _(i):
        rows = pl.ds(pl.multiple_of(i * 272, 16), 272)
        chosen = pick[rows, :]
        wanted[rows, :] = jnp.dot(chosen, tgt[...], preferred_element_type=F32).astype(BF16)
        owner[rows, :] = jnp.dot(chosen, turned_expand, preferred_element_type=F32)


    got("c3", crecv.at[3])
    got("f+a", frecv.at[0, low])
    got("f-a", frecv.at[1, top])
    got("f+b", frecv.at[0, top])
    got("f-b", frecv.at[1, low])
    gains = gain_ref[pl.ds(t * 4, 4), :]
    gain = jnp.concatenate([gains[k : k + 1, :] for k in range(4)], axis=1)
    stc[...] = jnp.zeros_like(stc)
    lane = iota((CHUNK, 128), 1)

    @pl.loop(0, LIVE // CHUNK)
    def _(i):
        rows = pl.ds(pl.multiple_of(i * CHUNK, CHUNK), CHUNK)
        joined = part[0, rows, :] + crecv[3, rows, :].astype(F32)
        joined = joined + (frecv[0, rows, :].astype(F32) + frecv[1, rows, :].astype(F32))
        part[0, rows, :] = joined
        goal = wanted[rows, :].astype(F32)
        scaled = joined * gain
        sums = [joined * joined, scaled * scaled, scaled * goal, goal * goal]
        row = jnp.zeros((CHUNK, 128), F32)
        for k, term in enumerate(sums):
            row = jnp.where(lane == k, jnp.sum(term, axis=1, keepdims=True), row)
        count = jnp.sum(owner[rows, :] * counts, axis=1, keepdims=True)
        stc[rows, :] = jnp.where(lane == 4, count, row)

    turned = stc[...].T
    count_row = jnp.maximum(turned[4:5, :], 1.0)
    stat[pl.ds(t, 1)] = turned[None, 0:8, :]
    for j in range(1, 8):
        send(f"s{j}", stat.at[t], stat.at[t], {"tp": (t + j) % 8, "dp": d})
    for j in range(1, 8):
        got(f"s{j}", stat.at[(t + 8 - j) % 8])
    total = stat[0]
    for j in range(1, 8):
        total = total + stat[j]
    inv_rms = lax.rsqrt(total[0:1] / OUT + 1e-05)
    weight_row = 2.0 / (OUT * count_row)
    row_loss = (inv_rms * inv_rms * total[1:2] - 2.0 * inv_rms * total[2:3] + total[3:4]) / OUT
    inner = weight_row * (inv_rms * total[1:2] - total[2:3])
    str_[...] = jnp.zeros_like(str_)
    str_[0:1, :] = inv_rms
    str_[1:2, :] = inv_rms * weight_row
    str_[2:3, :] = inv_rms * inv_rms * inv_rms * inner / OUT
    str_[3:4, :] = row_loss
    stc[...] = str_[...].T

    @pl.loop(0, LIVE // CHUNK)
    def _(i):
        rows = pl.ds(pl.multiple_of(i * CHUNK, CHUNK), CHUNK)
        joined = part[0, rows, :]
        stats = stc[rows, :]
        err = joined * stats[:, 0:1] * gain - wanted[rows, :].astype(F32)
        value = (stats[:, 1:2] * gain * err - joined * stats[:, 2:3]).astype(BF16)
        for h in range(2):
            there = pl.ds(pl.multiple_of(me[h] * LIVE + i * CHUNK, CHUNK), CHUNK)
            df[h, t, there, :] = value[:, h * PART : (h + 1) * PART]

    def block(h, yy, place, half=None):
        start, size = (0, LIVE) if half is None else (half * HALF, HALF)
        rows = pl.ds(pl.multiple_of((place % 4) * LIVE + start, 16), size)
        return df.at[h, (yy % 4) * 2 + c, rows, :]

    def put(name, ref, device):
        send(name, ref, ref, device)

    up_first = (False, True)
    early_half = (1, 0)

    def put_y(h, second):
        if up_first[h] != second:
            put(f"y{h}+", block(h, y, me[h]), up)
        else:
            put(f"y{h}-", block(h, y, me[h]), down)

    def pass_y(h, second):
        if up_first[h] != second:
            got(f"y{h}+", block(h, y + 3, me[h]))
            put(f"yf{h}+", block(h, y + 3, me[h], 0), up)
        else:
            got(f"y{h}-", block(h, y + 1, me[h]))
            put(f"yf{h}-", block(h, y + 1, me[h], 1), down)

    def end_y(h, half):
        got(f"yf{h}" + "+-"[half], block(h, y + 2, me[h], half))

    def put_far(h, half):
        name = "e" if half == early_half[h] else "a"
        last = "" if name == "e" else "3"
        put(f"{name}{h}{last}+", block(h, y + 2, me[h], half), axis(h, 1))
        put(f"{name}{h}{last}-", block(h, y + 2, me[h], half), axis(h, 3))

    def pass_far(h):
        half = early_half[h]
        got(f"e{h}+", block(h, y + 2, me[h] + 3, half))
        put(f"af{h}3+", block(h, y + 2, me[h] + 3, half), axis(h, 1))
        got(f"e{h}-", block(h, y + 2, me[h] + 1, half))
        half = 1 - half
        got(f"a{h}3-", block(h, y + 2, me[h] + 1, half))
        put(f"af{h}3-", block(h, y + 2, me[h] + 1, half), axis(h, 3))
        got(f"a{h}3+", block(h, y + 2, me[h] + 3, half))
        share(h, 3, 0, 1, 3)

    def end_far(h):
        got(f"af{h}3+", block(h, y + 2, me[h] + 2, early_half[h]))
        got(f"af{h}3-", block(h, y + 2, me[h] + 2, 1 - early_half[h]))
        share(h, 3, 2)

    def put_axis(h, b):
        put(f"a{h}{b}+", block(h, y + STEP[b], me[h]), axis(h, 1))
        put(f"a{h}{b}-", block(h, y + STEP[b], me[h]), axis(h, 3))

    def pass_axis(h, b):
        got(f"a{h}{b}+", block(h, y + STEP[b], me[h] + 3))
        put(f"af{h}{b}+", block(h, y + STEP[b], me[h] + 3, 0), axis(h, 1))
        got(f"a{h}{b}-", block(h, y + STEP[b], me[h] + 1))
        put(f"af{h}{b}-", block(h, y + STEP[b], me[h] + 1, 1), axis(h, 3))

        share(h, b, 0, 1, 3)

    def end_axis(h, b):
        got(f"af{h}{b}+", block(h, y + STEP[b], me[h] + 2, 0))
        got(f"af{h}{b}-", block(h, y + STEP[b], me[h] + 2, 1))
        share(h, b, 2)

    def put_whole(h, *steps):
        for j in steps:
            put(f"v{h}{j}", block(h, y, me[h] + j), at(y=y + TURN[h]))

    def end_whole(h):
        for j in (1, 3, 2):
            got(f"v{h}{j}", block(h, y + 4 - TURN[h], me[h] + j))
            share(h, WHOLE[h], j)

    def share(h, b, *steps):
        for k in steps:
            put(f"d{h}{b}{k}", block(h, y + STEP[b], me[h] + k), sibling)

    def shared(h, b):
        for k in range(4):
            rows = rows_of(me[h] + k)
            got(f"d{h}{b}{k}", df.at[h, block_of(b, 1), rows, :])

    def block_of(b, o):
        return ((y + STEP[b]) % 4) * 2 + (c if o == 0 else 1 - c)

    def across(h, step):
        return axis(1 - h, step)

    def grad(h, b, o):
        if o == 1:
            shared(h, b)
        cols = pl.ds(pl.multiple_of(block_of(b, o) * PART, PART), PART)
        gs[h, :, cols] = jnp.dot(xgt[h], df[h, block_of(b, o)], preferred_element_type=F32).astype(BF16)
        for j in (2, 1, 3):
            rows = pl.ds(pl.multiple_of(((me[1 - h] + j) % 4) * ROWS_OUT, 32), ROWS_OUT)
            send(f"g{h}{b}{o}{j}", gs.at[h, rows, cols], gr.at[h, j - 1, :, cols], across(h, j))

    turns = [(0, ALONG[h][1], 3, WHOLE[h]) for h in range(2)]

    def finish(h, b, o):
        column = block_of(b, o) * BLOCK + h * PART
        cols = pl.ds(pl.multiple_of(block_of(b, o) * PART, PART), PART)
        wide = pl.ds(pl.multiple_of(column, PART), PART)
        for j in (1, 2, 3):
            got(f"g{h}{b}{o}{j}", gr.at[h, j - 1, :, cols])
        largest = jnp.zeros((1, PART), F32)
        for l in range(3):
            mine = pl.ds(pl.multiple_of(me[1 - h] * ROWS_OUT + l * 32, 32), 32)
            there = pl.ds(pl.multiple_of(z * FEATS + l * 128 + x * 32, 32), 32)
            here = pl.ds(l * 32, 32)
            total = gs[h, mine, cols].astype(F32)
            for j in range(3):
                total = total + gr[h, j, here, cols].astype(F32)
            new = wv[there, wide].astype(F32) - learn_rate * total
            upd[l, :, wide] = new
            largest = jnp.maximum(largest, jnp.max(jnp.abs(new), axis=0, keepdims=True))
        for k in range(PART // 128):
            row = h * 4 + o * 2 + k
            mxp[turns[h].index(b), row : row + 1, :] = largest[:, k * 128 : (k + 1) * 128]

    early = tuple(sent)
    for h in range(2):
        put_y(h, False)
        put_axis(h, 0)

    loss_rows = stc[0:LIVE, 3:4] * owner[...]
    request_loss = jnp.sum(loss_rows, axis=0, keepdims=True) / counts
    slots = slots_ref[...]
    places = (slots >> 7) * 8 + (slots & 127) - d * 8
    hit = places == iota((REQS, REQS), 0)
    by_place = jnp.sum(jnp.where(hit, request_loss, 0.0), axis=1, keepdims=True)
    eye = iota((REQS, REQS), 0) == iota((REQS, REQS), 1)
    by_place = jnp.sum(jnp.where(eye, by_place, 0.0), axis=0, keepdims=True)
    dpr[pl.ds(d, 1), 16:24, :] = jnp.broadcast_to(by_place[None], (1, 8, 128))

    settle(*early)
    for h in range(2):
        own_copies[h].wait()
        for j in (1, 2, 3):
            got(f"x{h}{j}", xg.at[h, rows_of(me[h] + 4 - j), :])

        @pl.loop(0, ALL // 128)
        def _(k):
            places = pl.ds(pl.multiple_of(k * 128, 128), 128)
            turned = xg[h, places, :].T
            for q in range(4):
                for l in range(3):
                    xgt[h, q * ROWS_OUT + l * 32 : q * ROWS_OUT + (l + 1) * 32, places] = turned[
                        l * 128 + q * 32 : l * 128 + (q + 1) * 32, :
                    ]

    for h in range(2):
        pass_axis(h, 0)
    for h in range(2):
        pass_y(h, False)
        put_axis(h, ALONG[h][1])
    for h in range(2):
        put_y(h, True)
    for h in range(2):
        end_axis(h, 0)
        grad(h, 0, 0)
    for h in range(2):
        end_y(h, early_half[h])
        put_far(h, early_half[h])
    for h in range(2):
        pass_y(h, True)
        put_whole(h, 1)
        share(h, WHOLE[h], 0)
    for h in range(2):
        grad(h, 0, 1)
    for h in range(2):
        pass_axis(h, ALONG[h][1])
    for h in range(2):
        end_y(h, 1 - early_half[h])
        put_far(h, 1 - early_half[h])
        put_whole(h, 3, 2)
    for h in range(2):
        end_axis(h, ALONG[h][1])
        grad(h, ALONG[h][1], 0)
    for h in range(2):
        grad(h, ALONG[h][1], 1)
    for h in range(2):
        pass_far(h)
    for h in range(2):
        finish(h, 0, 0)
        finish(h, 0, 1)
    for h in range(2):
        end_far(h)
        grad(h, 3, 0)
    for h in range(2):
        grad(h, 3, 1)
    for h in range(2):
        for o in range(2):
            finish(h, ALONG[h][1], o)
    dpr[pl.ds(d, 1), 0:8, :] = mxp[0:1]
    dpr[pl.ds(d, 1), 8:16, :] = mxp[1:2]
    for j in range(1, 16):
        send(f"n{j}", dpr.at[d], dpr.at[d], {"tp": t, "dp": (d + j) % 16})
    for h in range(2):
        end_whole(h)
        grad(h, WHOLE[h], 0)
    for h in range(2):
        grad(h, WHOLE[h], 1)
    settle(*(name for name in tuple(sent) if name[0] != "g"))
    for h in range(2):
        for o in range(2):
            finish(h, 3, o)
    for h in range(2):
        for o in range(2):
            finish(h, WHOLE[h], o)

    dpl[pl.ds(d, 1), 0:8, :] = mxp[2:3]
    dpl[pl.ds(d, 1), 8:16, :] = mxp[3:4]
    for j in range(1, 16):
        send(f"o{j}", dpl.at[d], dpl.at[d], {"tp": t, "dp": (d + j) % 16})
    for j in range(1, 16):
        got(f"n{j}", dpr.at[(d + 16 - j) % 16])
    over_dp = [dpr[0, 0:8, :], dpr[0, 8:16, :]]
    for j in range(16):
        for k in range(2):
            over_dp[k] = jnp.maximum(over_dp[k], dpr[j, k * 8 : (k + 1) * 8, :])
        sprd[j * 8 : (j + 1) * 8, :] = dpr[j, 16:24, :]
    for j in range(1, 16):
        got(f"o{j}", dpl.at[(d + 16 - j) % 16])
    over_dp += [dpl[0, 0:8, :], dpl[0, 8:16, :]]
    for j in range(1, 16):
        for k in range(2):
            over_dp[2 + k] = jnp.maximum(over_dp[2 + k], dpl[j, k * 8 : (k + 1) * 8, :])
    for p in range(4):
        for h in range(2):
            for o in range(2):
                first_row = block_of(turns[h][p], o) * 4 + h * 2
                for k in range(2):
                    row = h * 4 + o * 2 + k
                    mx[pl.ds(first_row + k, 1), :] = over_dp[p][row : row + 1, :]
    for j in range(1, 8):
        send(f"m{j}", mx, mxr.at[j - 1], {"tp": (t + j) % 8, "dp": d})
    settle(*(name for name in tuple(sent) if name[0] != "m"))
    most = mx[...]
    for j in range(1, 8):
        got(f"m{j}", mxr.at[j - 1])
        most = jnp.maximum(most, mxr[j - 1])
    small_ref[0:32, :] = most + 1e-06
    lanes = iota((REQS, REQS), 1) == d * 8 + (iota((REQS, REQS), 0) & 7)
    mine = jnp.sum(jnp.where(lanes, sprd[...], 0.0), axis=1, keepdims=True)
    loss = jnp.sum(jnp.where(eye, mine, 0.0), axis=0, keepdims=True)
    small_ref[32:40, :] = jnp.broadcast_to(loss, (8, 128))
    settle()


def scaled(upd, small, loss_ref, serve_ref, scale_ref):
    scale_ref[...] = small[0:32, :]
    loss_ref[...] = small[32:33, :]
    for k in range(OUT // 128):
        cols = slice(k * 128, (k + 1) * 128)
        serve_ref[:, :, cols] = (upd[:, :, cols] / small[k : k + 1, :][None]).astype(BF16)


def shards(hidden_rows, target_rows, row_counts, seq_slot, joining_weight, norm_gain):
    any_spec = pl.BlockSpec(memory_space=pl.ANY)
    vmem = pl.BlockSpec(memory_space=pltpu.VMEM)
    n = len(IDS)
    upd, small = pl.pallas_call(
        kernel,
        out_shape=(
            jax.ShapeDtypeStruct((3, 32, OUT), F32),
            jax.ShapeDtypeStruct((40, 128), F32),
        ),
        in_specs=[any_spec, any_spec, vmem, vmem, any_spec, vmem],
        out_specs=(vmem, vmem),
        scratch_shapes=[
            pltpu.VMEM((3, SLOTS, BLOCK), BF16),
            pltpu.VMEM((SLOTS, BLOCK), BF16),
            pltpu.VMEM((4 * FEATS, OUT), BF16),
            pltpu.VMEM((LIVE, SLOTS), BF16),
            pltpu.VMEM((BLOCK, BLOCK), BF16),
            pltpu.VMEM((LIVE, 4 * FEATS), BF16),
            pltpu.VMEM((LIVE, 4 * FEATS), BF16),
            pltpu.VMEM((LIVE, BLOCK), BF16),
            pltpu.VMEM((4, LIVE, BLOCK), BF16),
            pltpu.VMEM((3, LIVE, BLOCK), F32),
            pltpu.VMEM((2, HALF, BLOCK), BF16),
            pltpu.VMEM((2, LIVE, BLOCK), BF16),
            pltpu.VMEM((2, ALL, FEATS), BF16),
            pltpu.VMEM((2, FEATS, ALL), BF16),
            pltpu.VMEM((2, 8, ALL, PART), BF16),
            pltpu.VMEM((2, FEATS, 8 * PART), BF16),
            pltpu.VMEM((2, 3, ROWS_OUT, 8 * PART), BF16),
            pltpu.VMEM((LIVE, REQS), F32),
            pltpu.VMEM((PAD, 128), F32),
            pltpu.VMEM((128, PAD), F32),
            pltpu.VMEM((8, 8, PAD), F32),
            pltpu.VMEM((4, 8, 128), F32),
            pltpu.VMEM((32, 128), F32),
            pltpu.VMEM((7, 32, 128), F32),
            pltpu.VMEM((16, 24, 128), F32),
            pltpu.VMEM((16, 16, 128), F32),
            pltpu.VMEM((REQS, 128), F32),
            pltpu.SemaphoreType.DMA((18,)),
            pltpu.SemaphoreType.DMA((n,)),
            pltpu.SemaphoreType.DMA((n,)),
        ],
        compiler_params=pltpu.CompilerParams(
            collective_id=0, has_side_effects=True, vmem_limit_bytes=64 * 2**20 - 2**18
        ),
        name="joining_step",
    )(
        jnp.transpose(hidden_rows, (1, 0, 2)),
        target_rows,
        row_counts.reshape(1, REQS),
        seq_slot.reshape(1, REQS),
        joining_weight,
        norm_gain.reshape(32, 128),
    )
    loss, serve, scale = pl.pallas_call(
        scaled,
        out_shape=(
            jax.ShapeDtypeStruct((1, REQS), F32),
            jax.ShapeDtypeStruct((3, 32, OUT), BF16),
            jax.ShapeDtypeStruct((32, 128), F32),
        ),
        in_specs=[vmem, vmem],
        out_specs=(vmem, vmem, vmem),
        name="scaled",
    )(upd, small)
    return loss.reshape(REQS), serve, scale.reshape(OUT)


def solution(mesh):
    placed = (P("dp", None, "tp"), P("dp", "tp"), P("dp"), P("dp"), P(None, "tp", None), P())
    return jax.shard_map(
        shards,
        mesh=mesh,
        in_specs=placed,
        out_specs=(P("dp"), P(None, ("tp", "dp"), None), P()),
        check_vma=False,
    )
```

```python
import jax
import jax.numpy as jnp
from jax import lax
from jax.experimental import pallas as pl
from jax.experimental.pallas import tpu as pltpu
from jax.sharding import PartitionSpec as P

learn_rate = 1.0

F32, BF16, I32 = jnp.float32, jnp.bfloat16, jnp.int32
EXACT = lax.Precision.HIGHEST
REQS, MOST, SLOTS, LIVE = 128, 8, 1024, 544
HALF = LIVE // 2
PAD = 640
ALL = 4 * LIVE
BLOCK, PART = 512, 256
FEATS = 384
OUT = 4096
ROWS_OUT = 96
CHUNK = 32


def iota(shape, dim):
    return lax.broadcasted_iota(I32, shape, dim)


def names():
    out = [f"x{h}{j}" for h in range(2) for j in (1, 2, 3)] + [f"c{i}" for i in range(4)]
    out += ["c0b", "h+", "h-", "f+a", "f+b", "f-a", "f-b"] + [f"s{j}" for j in range(1, 8)]
    for h in range(2):
        out += [f"{k}{h}{s}" for k in ("y", "yf", "e") for s in "+-"]
        out += [f"{k}{h}{b}{s}" for k in ("a", "af") for b in range(4) for s in "+-"]
        out += [f"v{h}{j}" for j in (1, 2, 3)] + [f"d{h}{b}{k}" for b in range(4) for k in range(4)]
        out += [f"g{h}{b}{o}{j}" for b in range(4) for o in range(2) for j in (1, 2, 3)]
    out += [f"m{j}" for j in range(1, 8)] + [f"n{j}" for j in range(1, 16)]
    return {name: i for i, name in enumerate(out)}


IDS = names()
STEP = (0, 3, 1, 2)
ALONG = ((0, 2, 3), (0, 1, 3))
WHOLE = (1, 2)
TURN = (1, 3)


def kernel(
    hid_hbm, tgt_hbm, counts_ref, slots_ref, w_hbm, gain_ref,
    upd, small_ref,
    hid, tgt, wv, pick, perm, xc, xcb, wanted, crecv, part, hrecv, frecv, xg, xgt, df, gs, gr,
    owner, stc, str_, stat, mx, mxr, dpr, sprd, lsem, ss, rs,
):
    t = lax.axis_index("tp")
    d = lax.axis_index("dp")
    y, c = t // 2, t % 2
    z, x = d // 4, d % 4
    sent = {}

    def at(y=y, c=c, z=z, x=x):
        return {"tp": (y % 4) * 2 + c, "dp": (z % 4) * 4 + x % 4}

    sibling = at(c=1 - c)

    def send(name, src, dst, device):
        i = IDS[name]
        copy = pltpu.make_async_remote_copy(
            src_ref=src, dst_ref=dst, send_sem=ss.at[i], recv_sem=rs.at[i],
            device_id=device, device_id_type=pl.DeviceIdType.MESH,
        )
        copy.start()
        sent[name] = copy

    def settle(*which):
        for name in which or tuple(sent):
            sent.pop(name).wait_send()

    def got(name, ref):
        i = IDS[name]
        pltpu.make_async_remote_copy(
            src_ref=ref, dst_ref=ref, send_sem=ss.at[i], recv_sem=rs.at[i],
            device_id=sibling, device_id_type=pl.DeviceIdType.MESH,
        ).wait_recv()

    loads = [pltpu.make_async_copy(hid_hbm.at[l], hid.at[l], lsem.at[l]) for l in range(3)]
    loads.append(pltpu.make_async_copy(tgt_hbm, tgt, lsem.at[3]))
    weights = [[] for _ in range(4)]
    for g, step in enumerate((2, 1, 3, 0)):
        cols = pl.ds(pl.multiple_of(((y + step) % 4) * 2 * BLOCK, 2 * BLOCK), 2 * BLOCK)
        for zz in range(4):
            for l in range(3):
                weights[g].append(
                    pltpu.make_async_copy(
                        w_hbm.at[l, pl.ds(zz * 128, 128), cols],
                        wv.at[pl.ds(zz * FEATS + l * 128, 128), cols],
                        lsem.at[4 + g * 12 + zz * 3 + l],
                    )
                )
    for load in loads[:3]:
        load.start()
    barrier = pltpu.get_barrier_semaphore()
    for j in range(1, 8):
        pl.semaphore_signal(
            barrier, inc=1, device_id={"tp": (t + j) % 8, "dp": d}, device_id_type=pl.DeviceIdType.MESH
        )
    for j in range(1, 16):
        pl.semaphore_signal(
            barrier, inc=1, device_id={"tp": t, "dp": (d + j) % 16}, device_id_type=pl.DeviceIdType.MESH
        )

    counts = counts_ref[...].astype(F32)
    counts8 = jnp.broadcast_to(counts, (8, REQS))
    expand = (iota((REQS, SLOTS), 1) >> 3 == iota((REQS, SLOTS), 0)).astype(F32)
    before = (iota((REQS, REQS), 0) < iota((REQS, REQS), 1)).astype(F32)
    start8 = jnp.dot(counts8, before, precision=EXACT, preferred_element_type=F32)
    count_slot = jnp.dot(counts8, expand, precision=EXACT, preferred_element_type=F32)
    start_slot = jnp.dot(start8, expand, precision=EXACT, preferred_element_type=F32)
    inside = iota((8, SLOTS), 1) & 7
    rank8 = (start_slot + 0.5).astype(I32) + inside
    rank8 = jnp.where(inside < (count_slot + 0.5).astype(I32), rank8, -1)
    rank = rank8[0:1, :]

    @pl.loop(0, LIVE // 272)
    def _(i):
        rows = pl.ds(pl.multiple_of(i * 272, 16), 272)
        hit = iota((272, SLOTS), 0) + i * 272 == rank
        pick[rows, :] = jnp.where(hit, 1.0, 0.0).astype(BF16)

    for load in loads[:3]:
        load.wait()
    loads[3].start()
    for load in weights[0]:
        load.start()

    @pl.loop(0, LIVE // 272)
    def _(i):
        rows = pl.ds(pl.multiple_of(i * 272, 16), 272)
        chosen = pick[rows, :]
        for l in range(3):
            got_rows = jnp.dot(chosen, hid[l], preferred_element_type=F32).astype(BF16)
            for q in range(4):
                cols = slice(q * FEATS + l * 128, q * FEATS + (l + 1) * 128)
                xc[rows, cols] = got_rows[:, q * 128 : (q + 1) * 128]

    for group in weights[1:]:
        for load in group:
            load.start()
    pl.semaphore_wait(barrier, 22)

    def feats(q):
        return pl.ds(pl.multiple_of((q % 4) * FEATS, 128), FEATS)

    def rows_of(q):
        return pl.ds(pl.multiple_of((q % 4) * LIVE, 16), LIVE)

    me = (z, x)

    def axis(h, step):
        return at(z=z + step) if h == 0 else at(x=x + step)

    own_copies = []

    def exchange(h, kept):
        for j in (1, 2, 3):
            send(f"x{h}{j}", kept.at[:, feats(me[h] + j)], xg.at[h, rows_of(me[h]), :], axis(h, j))
        own_copies.append(
            pltpu.make_async_copy(kept.at[:, feats(me[h])], xg.at[h, rows_of(me[h]), :], lsem.at[52 + h])
        )
        own_copies[h].start()

    exchange(0, xc)
    for load in weights[0]:
        load.wait()

    def forward(yy, core, dst, rows=slice(None)):
        column = ((yy % 4) * 2 + core) * BLOCK

        @pl.loop(0, 2)
        def _(i):
            cols = pl.ds(pl.multiple_of(column + i * PART, PART), PART)
            dst[rows, pl.ds(pl.multiple_of(i * PART, PART), PART)] = jnp.dot(
                xc[rows, :], wv[:, cols], preferred_element_type=F32
            ).astype(dst.dtype)

    csend = [xcb.at[:, i * BLOCK : (i + 1) * BLOCK] for i in range(3)] + [hid.at[2, pl.ds(0, LIVE)]]
    ysend = [hid.at[i, pl.ds(0, LIVE)] for i in range(2)]
    yhalf = [hid.at[i, pl.ds(LIVE, HALF)] for i in range(2)]

    def to_sibling(i, step):
        forward(y + step, 1 - c, csend[i])
        send(f"c{i}", csend[i], crecv.at[i], sibling)

    up, down = at(y=y + 1), at(y=y + 3)
    top, low = pl.ds(0, HALF), pl.ds(HALF, HALF)
    for rows, name in ((top, "c0"), (low, "c0b")):
        forward(y + 2, 1 - c, csend[0], rows)
        send(name, csend[0].at[rows], crecv.at[0, rows], sibling)
        forward(y + 2, c, part.at[0], rows)
    for k, (rows, name, there, device) in enumerate(((top, "c0", "h+", up), (low, "c0b", "h-", down))):
        got(name, crecv.at[0, rows])
        yhalf[k][...] = (part[0, rows, :] + crecv[0, rows, :].astype(F32)).astype(BF16)
        send(there, yhalf[k], hrecv.at[k], device)
    for load in weights[1]:
        load.wait()
    to_sibling(1, 1)
    forward(y + 1, c, part.at[1])
    got("c1", crecv.at[1])
    ysend[0][low, :] = (part[1, low, :] + crecv[1, low, :].astype(F32)).astype(BF16)
    send("f+a", ysend[0].at[low], frecv.at[0, low], up)
    for load in weights[2]:
        load.wait()
    to_sibling(2, 3)
    forward(y + 3, c, part.at[2])
    got("c2", crecv.at[2])
    ysend[1][top, :] = (part[2, top, :] + crecv[2, top, :].astype(F32)).astype(BF16)
    send("f-a", ysend[1].at[top], frecv.at[1, top], down)

    place = iota((BLOCK, BLOCK), 1)
    source = ((place >> 5) & 3) * 128 + (place >> 7) * 32 + (place & 31)
    perm[...] = (iota((BLOCK, BLOCK), 0) == source).astype(F32).astype(BF16)

    settle("c0", "c0b", "c1", "c2")

    @pl.loop(0, LIVE // 272)
    def _(i):
        rows = pl.ds(pl.multiple_of(i * 272, 16), 272)
        for l in range(3):
            whole_rows = jnp.concatenate(
                [xc[rows, q * FEATS + l * 128 : q * FEATS + (l + 1) * 128] for q in range(4)], axis=1
            )
            swapped = jnp.dot(whole_rows, perm[...], preferred_element_type=F32).astype(BF16)
            for q in range(4):
                xcb[rows, q * FEATS + l * 128 : q * FEATS + (l + 1) * 128] = swapped[:, q * 128 : (q + 1) * 128]

    exchange(1, xcb)
    got("h+", hrecv.at[0])
    ysend[0][top, :] = (part[1, top, :] + crecv[1, top, :].astype(F32) + hrecv[0].astype(F32)).astype(BF16)
    send("f+b", ysend[0].at[top], frecv.at[0, top], up)
    got("h-", hrecv.at[1])
    ysend[1][low, :] = (part[2, low, :] + crecv[2, low, :].astype(F32) + hrecv[1].astype(F32)).astype(BF16)
    send("f-b", ysend[1].at[low], frecv.at[1, low], down)
    for load in weights[3]:
        load.wait()
    to_sibling(3, 0)
    forward(y, c, part.at[0])
    turned_expand = (iota((SLOTS, REQS), 0) >> 3 == iota((SLOTS, REQS), 1)).astype(F32).astype(BF16)
    loads[3].wait()

    @pl.loop(0, LIVE // 272)
    def _(i):
        rows = pl.ds(pl.multiple_of(i * 272, 16), 272)
        chosen = pick[rows, :]
        wanted[rows, :] = jnp.dot(chosen, tgt[...], preferred_element_type=F32).astype(BF16)
        owner[rows, :] = jnp.dot(chosen, turned_expand, preferred_element_type=F32)


    got("c3", crecv.at[3])
    stc[...] = jnp.zeros_like(stc)
    lane = iota((CHUNK, 128), 1)

    @pl.loop(0, LIVE // CHUNK)
    def _(i):
        rows = pl.ds(pl.multiple_of(i * CHUNK, CHUNK), CHUNK)
        part[0, rows, :] = part[0, rows, :] + crecv[3, rows, :].astype(F32)
        goal = wanted[rows, :].astype(F32)
        row = jnp.where(lane == 3, jnp.sum(goal * goal, axis=1, keepdims=True), 0.0)
        count = jnp.sum(owner[rows, :] * counts, axis=1, keepdims=True)
        stc[rows, :] = jnp.where(lane == 4, count, row)

    got("f+a", frecv.at[0, low])
    got("f-a", frecv.at[1, top])
    got("f+b", frecv.at[0, top])
    got("f-b", frecv.at[1, low])
    gains = gain_ref[pl.ds(t * 4, 4), :]
    gain = jnp.concatenate([gains[k : k + 1, :] for k in range(4)], axis=1)

    @pl.loop(0, LIVE // CHUNK)
    def _(i):
        rows = pl.ds(pl.multiple_of(i * CHUNK, CHUNK), CHUNK)
        joined = part[0, rows, :] + (frecv[0, rows, :].astype(F32) + frecv[1, rows, :].astype(F32))
        part[0, rows, :] = joined
        goal = wanted[rows, :].astype(F32)
        scaled = joined * gain
        sums = [joined * joined, scaled * scaled, scaled * goal]
        row = stc[rows, :]
        for k, term in enumerate(sums):
            row = jnp.where(lane == k, jnp.sum(term, axis=1, keepdims=True), row)
        stc[rows, :] = row

    turned = stc[...].T
    count_row = jnp.maximum(turned[4:5, :], 1.0)
    stat[pl.ds(t, 1)] = turned[None, 0:8, :]
    for j in range(1, 8):
        send(f"s{j}", stat.at[t], stat.at[t], {"tp": (t + j) % 8, "dp": d})
    for j in range(1, 8):
        got(f"s{j}", stat.at[(t + 8 - j) % 8])
    total = stat[0]
    for j in range(1, 8):
        total = total + stat[j]
    inv_rms = lax.rsqrt(total[0:1] / OUT + 1e-05)
    weight_row = 2.0 / (OUT * count_row)
    row_loss = (inv_rms * inv_rms * total[1:2] - 2.0 * inv_rms * total[2:3] + total[3:4]) / OUT
    inner = weight_row * (inv_rms * total[1:2] - total[2:3])
    str_[...] = jnp.zeros_like(str_)
    str_[0:1, :] = inv_rms
    str_[1:2, :] = inv_rms * weight_row
    str_[2:3, :] = inv_rms * inv_rms * inv_rms * inner / OUT
    str_[3:4, :] = row_loss
    stc[...] = str_[...].T

    def gradient(h):
        cols = slice(h * PART, (h + 1) * PART)

        @pl.loop(0, LIVE // CHUNK)
        def _(i):
            rows = pl.ds(pl.multiple_of(i * CHUNK, CHUNK), CHUNK)
            there = pl.ds(pl.multiple_of(me[h] * LIVE + i * CHUNK, CHUNK), CHUNK)
            joined = part[0, rows, cols]
            stats = stc[rows, :]
            err = joined * stats[:, 0:1] * gain[:, cols] - wanted[rows, cols].astype(F32)
            value = stats[:, 1:2] * gain[:, cols] * err - joined * stats[:, 2:3]
            df[h, t, there, :] = value.astype(BF16)

    def block(h, yy, place, half=None):
        start, size = (0, LIVE) if half is None else (half * HALF, HALF)
        rows = pl.ds(pl.multiple_of((place % 4) * LIVE + start, 16), size)
        return df.at[h, (yy % 4) * 2 + c, rows, :]

    def put(name, ref, device):
        send(name, ref, ref, device)

    up_first = (False, True)
    early_half = (1, 0)

    def put_y(h, second):
        if up_first[h] != second:
            put(f"y{h}+", block(h, y, me[h]), up)
        else:
            put(f"y{h}-", block(h, y, me[h]), down)

    def pass_y(h, second):
        if up_first[h] != second:
            got(f"y{h}+", block(h, y + 3, me[h]))
            put(f"yf{h}+", block(h, y + 3, me[h], 0), up)
        else:
            got(f"y{h}-", block(h, y + 1, me[h]))
            put(f"yf{h}-", block(h, y + 1, me[h], 1), down)

    def end_y(h, half):
        got(f"yf{h}" + "+-"[half], block(h, y + 2, me[h], half))

    def put_far(h, half):
        name = "e" if half == early_half[h] else "a"
        last = "" if name == "e" else "3"
        put(f"{name}{h}{last}+", block(h, y + 2, me[h], half), axis(h, 1))
        put(f"{name}{h}{last}-", block(h, y + 2, me[h], half), axis(h, 3))

    def pass_far(h):
        half = early_half[h]
        got(f"e{h}+", block(h, y + 2, me[h] + 3, half))
        put(f"af{h}3+", block(h, y + 2, me[h] + 3, half), axis(h, 1))
        got(f"e{h}-", block(h, y + 2, me[h] + 1, half))
        half = 1 - half
        got(f"a{h}3-", block(h, y + 2, me[h] + 1, half))
        put(f"af{h}3-", block(h, y + 2, me[h] + 1, half), axis(h, 3))
        got(f"a{h}3+", block(h, y + 2, me[h] + 3, half))
        share(h, 3, 0, 1, 3)

    def end_far(h):
        got(f"af{h}3+", block(h, y + 2, me[h] + 2, early_half[h]))
        got(f"af{h}3-", block(h, y + 2, me[h] + 2, 1 - early_half[h]))
        share(h, 3, 2)

    def put_axis(h, b):
        put(f"a{h}{b}+", block(h, y + STEP[b], me[h]), axis(h, 1))
        put(f"a{h}{b}-", block(h, y + STEP[b], me[h]), axis(h, 3))

    def pass_axis(h, b):
        got(f"a{h}{b}+", block(h, y + STEP[b], me[h] + 3))
        put(f"af{h}{b}+", block(h, y + STEP[b], me[h] + 3, 0), axis(h, 1))
        got(f"a{h}{b}-", block(h, y + STEP[b], me[h] + 1))
        put(f"af{h}{b}-", block(h, y + STEP[b], me[h] + 1, 1), axis(h, 3))

        share(h, b, 0, 1, 3)

    def end_axis(h, b):
        got(f"af{h}{b}+", block(h, y + STEP[b], me[h] + 2, 0))
        got(f"af{h}{b}-", block(h, y + STEP[b], me[h] + 2, 1))
        share(h, b, 2)

    def put_whole(h, *steps):
        for j in steps:
            put(f"v{h}{j}", block(h, y, me[h] + j), at(y=y + TURN[h]))

    def end_whole(h):
        for j in (1, 3, 2):
            got(f"v{h}{j}", block(h, y + 4 - TURN[h], me[h] + j))
            share(h, WHOLE[h], j)

    def share(h, b, *steps):
        for k in steps:
            put(f"d{h}{b}{k}", block(h, y + STEP[b], me[h] + k), sibling)

    def shared(h, b):
        for k in range(4):
            rows = rows_of(me[h] + k)
            got(f"d{h}{b}{k}", df.at[h, block_of(b, 1), rows, :])

    def block_of(b, o):
        return ((y + STEP[b]) % 4) * 2 + (c if o == 0 else 1 - c)

    def across(h, step):
        return axis(1 - h, step)

    def grad(h, b, o):
        if o == 1:
            shared(h, b)
        cols = pl.ds(pl.multiple_of(block_of(b, o) * PART, PART), PART)
        gs[h, :, cols] = jnp.dot(xgt[h], df[h, block_of(b, o)], preferred_element_type=F32).astype(BF16)
        for j in (2, 1, 3):
            rows = pl.ds(pl.multiple_of(((me[1 - h] + j) % 4) * ROWS_OUT, 32), ROWS_OUT)
            send(f"g{h}{b}{o}{j}", gs.at[h, rows, cols], gr.at[h, j - 1, :, cols], across(h, j))

    def finish(h, b, o):
        column = block_of(b, o) * BLOCK + h * PART
        cols = pl.ds(pl.multiple_of(block_of(b, o) * PART, PART), PART)
        wide = pl.ds(pl.multiple_of(column, PART), PART)
        for j in (1, 2, 3):
            got(f"g{h}{b}{o}{j}", gr.at[h, j - 1, :, cols])
        largest = jnp.zeros((1, PART), F32)
        for l in range(3):
            mine = pl.ds(pl.multiple_of(me[1 - h] * ROWS_OUT + l * 32, 32), 32)
            there = pl.ds(pl.multiple_of(z * FEATS + l * 128 + x * 32, 32), 32)
            here = pl.ds(l * 32, 32)
            total = gs[h, mine, cols].astype(F32)
            for j in range(3):
                total = total + gr[h, j, here, cols].astype(F32)
            new = wv[there, wide].astype(F32) - learn_rate * total
            upd[l, :, wide] = new
            largest = jnp.maximum(largest, jnp.max(jnp.abs(new), axis=0, keepdims=True))
        for k in range(PART // 128):
            mx[pl.ds(column // 128 + k, 1), :] = largest[:, k * 128 : (k + 1) * 128]

    early = tuple(sent)
    for h in range(2):
        gradient(h)
        put_y(h, False)
        put_axis(h, 0)

    loss_rows = stc[0:LIVE, 3:4] * owner[...]
    request_loss = jnp.sum(loss_rows, axis=0, keepdims=True) / counts
    slots = slots_ref[...]
    places = (slots >> 7) * 8 + (slots & 127) - d * 8
    hit = places == iota((REQS, REQS), 0)
    by_place = jnp.sum(jnp.where(hit, request_loss, 0.0), axis=1, keepdims=True)
    eye = iota((REQS, REQS), 0) == iota((REQS, REQS), 1)
    by_place = jnp.sum(jnp.where(eye, by_place, 0.0), axis=0, keepdims=True)
    dpr[pl.ds(d, 1), 32:40, :] = jnp.broadcast_to(by_place[None], (1, 8, 128))

    settle(*early)
    for h in range(2):
        own_copies[h].wait()
        for j in (1, 2, 3):
            got(f"x{h}{j}", xg.at[h, rows_of(me[h] + 4 - j), :])

        @pl.loop(0, ALL // 128)
        def _(k):
            places = pl.ds(pl.multiple_of(k * 128, 128), 128)
            turned = xg[h, places, :].T
            for q in range(4):
                for l in range(3):
                    xgt[h, q * ROWS_OUT + l * 32 : q * ROWS_OUT + (l + 1) * 32, places] = turned[
                        l * 128 + q * 32 : l * 128 + (q + 1) * 32, :
                    ]

    for h in range(2):
        pass_axis(h, 0)
    for h in range(2):
        pass_y(h, False)
        put_axis(h, ALONG[h][1])
    for h in range(2):
        put_y(h, True)
    for h in range(2):
        end_axis(h, 0)
        grad(h, 0, 0)
    for h in range(2):
        end_y(h, early_half[h])
        put_far(h, early_half[h])
    for h in range(2):
        pass_y(h, True)
        put_whole(h, 1)
        share(h, WHOLE[h], 0)
    for h in range(2):
        grad(h, 0, 1)
    for h in range(2):
        pass_axis(h, ALONG[h][1])
    for h in range(2):
        end_y(h, 1 - early_half[h])
        put_far(h, 1 - early_half[h])
        put_whole(h, 3, 2)
    for h in range(2):
        end_axis(h, ALONG[h][1])
        grad(h, ALONG[h][1], 0)
    for h in range(2):
        grad(h, ALONG[h][1], 1)
    for h in range(2):
        pass_far(h)
    for h in range(2):
        finish(h, 0, 0)
        finish(h, 0, 1)
    for h in range(2):
        end_far(h)
        grad(h, 3, 0)
    for h in range(2):
        grad(h, 3, 1)
    for h in range(2):
        for o in range(2):
            finish(h, ALONG[h][1], o)
    for h in range(2):
        end_whole(h)
        grad(h, WHOLE[h], 0)
    for h in range(2):
        grad(h, WHOLE[h], 1)
    settle(*(name for name in tuple(sent) if name[0] != "g"))
    for h in range(2):
        for o in range(2):
            finish(h, 3, o)
    for h in range(2):
        for o in range(2):
            finish(h, WHOLE[h], o)

    for j in range(1, 8):
        send(f"m{j}", mx, mxr.at[j - 1], {"tp": (t + j) % 8, "dp": d})
    settle(*(name for name in tuple(sent) if name[0] == "g"))
    most = mx[...]
    for j in range(1, 8):
        got(f"m{j}", mxr.at[j - 1])
        most = jnp.maximum(most, mxr[j - 1])
    dpr[pl.ds(d, 1), 0:32, :] = most[None]
    for j in range(1, 16):
        send(f"n{j}", dpr.at[d], dpr.at[d], {"tp": t, "dp": (d + j) % 16})
    for j in range(1, 16):
        got(f"n{j}", dpr.at[(d + 16 - j) % 16])
    for j in range(16):
        most = jnp.maximum(most, dpr[j, 0:32, :])
        sprd[j * 8 : (j + 1) * 8, :] = dpr[j, 32:40, :]
    small_ref[0:32, :] = most + 1e-06
    lanes = iota((REQS, REQS), 1) == d * 8 + (iota((REQS, REQS), 0) & 7)
    mine = jnp.sum(jnp.where(lanes, sprd[...], 0.0), axis=1, keepdims=True)
    loss = jnp.sum(jnp.where(eye, mine, 0.0), axis=0, keepdims=True)
    small_ref[32:40, :] = jnp.broadcast_to(loss, (8, 128))
    settle()


def scaled(upd, small, loss_ref, serve_ref, scale_ref):
    scale_ref[...] = small[0:32, :]
    loss_ref[...] = small[32:33, :]
    for k in range(OUT // 128):
        cols = slice(k * 128, (k + 1) * 128)
        serve_ref[:, :, cols] = (upd[:, :, cols] / small[k : k + 1, :][None]).astype(BF16)


def shards(hidden_rows, target_rows, row_counts, seq_slot, joining_weight, norm_gain):
    any_spec = pl.BlockSpec(memory_space=pl.ANY)
    vmem = pl.BlockSpec(memory_space=pltpu.VMEM)
    n = len(IDS)
    upd, small = pl.pallas_call(
        kernel,
        out_shape=(
            jax.ShapeDtypeStruct((3, 32, OUT), F32),
            jax.ShapeDtypeStruct((40, 128), F32),
        ),
        in_specs=[any_spec, any_spec, vmem, vmem, any_spec, vmem],
        out_specs=(vmem, vmem),
        scratch_shapes=[
            pltpu.VMEM((3, SLOTS, BLOCK), BF16),
            pltpu.VMEM((SLOTS, BLOCK), BF16),
            pltpu.VMEM((4 * FEATS, OUT), BF16),
            pltpu.VMEM((LIVE, SLOTS), BF16),
            pltpu.VMEM((BLOCK, BLOCK), BF16),
            pltpu.VMEM((LIVE, 4 * FEATS), BF16),
            pltpu.VMEM((LIVE, 4 * FEATS), BF16),
            pltpu.VMEM((LIVE, BLOCK), BF16),
            pltpu.VMEM((4, LIVE, BLOCK), BF16),
            pltpu.VMEM((3, LIVE, BLOCK), F32),
            pltpu.VMEM((2, HALF, BLOCK), BF16),
            pltpu.VMEM((2, LIVE, BLOCK), BF16),
            pltpu.VMEM((2, ALL, FEATS), BF16),
            pltpu.VMEM((2, FEATS, ALL), BF16),
            pltpu.VMEM((2, 8, ALL, PART), BF16),
            pltpu.VMEM((2, FEATS, 8 * PART), BF16),
            pltpu.VMEM((2, 3, ROWS_OUT, 8 * PART), BF16),
            pltpu.VMEM((LIVE, REQS), F32),
            pltpu.VMEM((PAD, 128), F32),
            pltpu.VMEM((128, PAD), F32),
            pltpu.VMEM((8, 8, PAD), F32),
            pltpu.VMEM((32, 128), F32),
            pltpu.VMEM((7, 32, 128), F32),
            pltpu.VMEM((16, 40, 128), F32),
            pltpu.VMEM((REQS, 128), F32),
            pltpu.SemaphoreType.DMA((54,)),
            pltpu.SemaphoreType.DMA((n,)),
            pltpu.SemaphoreType.DMA((n,)),
        ],
        compiler_params=pltpu.CompilerParams(
            collective_id=0, has_side_effects=True, vmem_limit_bytes=64 * 2**20 - 2**18
        ),
        name="joining_step",
    )(
        jnp.transpose(hidden_rows, (1, 0, 2)),
        target_rows,
        row_counts.reshape(1, REQS),
        seq_slot.reshape(1, REQS),
        joining_weight,
        norm_gain.reshape(32, 128),
    )
    loss, serve, scale = pl.pallas_call(
        scaled,
        out_shape=(
            jax.ShapeDtypeStruct((1, REQS), F32),
            jax.ShapeDtypeStruct((3, 32, OUT), BF16),
            jax.ShapeDtypeStruct((32, 128), F32),
        ),
        in_specs=[vmem, vmem],
        out_specs=(vmem, vmem, vmem),
        name="scaled",
    )(upd, small)
    return loss.reshape(REQS), serve, scale.reshape(OUT)


def solution(mesh):
    placed = (P("dp", None, "tp"), P("dp", "tp"), P("dp"), P("dp"), P(None, "tp", None), P())
    return jax.shard_map(
        shards,
        mesh=mesh,
        in_specs=placed,
        out_specs=(P("dp"), P(None, ("tp", "dp"), None), P()),
        check_vma=False,
    )
```

```python
import jax
import jax.numpy as jnp
from jax import lax
from jax.experimental import pallas as pl
from jax.experimental.pallas import tpu as pltpu
from jax.sharding import PartitionSpec as P

learn_rate = 1.0

F32, BF16, I32 = jnp.float32, jnp.bfloat16, jnp.int32
EXACT = lax.Precision.HIGHEST
REQS, MOST, SLOTS, LIVE = 128, 8, 1024, 544
HALF = LIVE // 2
PAD = 640
ALL = 4 * LIVE
BLOCK, PART = 512, 256
FEATS = 384
OUT = 4096
ROWS_OUT = 96
CHUNK = 32


def iota(shape, dim):
    return lax.broadcasted_iota(I32, shape, dim)


def names():
    out = [f"x{h}{j}" for h in range(2) for j in (1, 2, 3)] + [f"c{i}" for i in range(4)]
    out += ["c0b", "h+", "h-", "f+a", "f+b", "f-a", "f-b"] + [f"s{j}" for j in range(1, 8)]
    for h in range(2):
        out += [f"{k}{h}{s}" for k in ("y", "yf", "e") for s in "+-"]
        out += [f"{k}{h}{b}{s}" for k in ("a", "af") for b in range(4) for s in "+-"]
        out += [f"v{h}{j}" for j in (1, 2, 3)] + [f"d{h}{b}{k}" for b in range(4) for k in range(4)]
        out += [f"g{h}{b}{o}{j}" for b in range(4) for o in range(2) for j in (1, 2, 3)]
    out += [f"m{j}" for j in range(1, 8)] + [f"n{j}" for j in range(1, 16)]
    return {name: i for i, name in enumerate(out)}


IDS = names()
STEP = (0, 3, 1, 2)
ALONG = ((0, 2, 3), (0, 1, 3))
WHOLE = (1, 2)
TURN = (1, 3)


def kernel(
    hid_hbm, tgt_hbm, counts_ref, slots_ref, w_hbm, gain_ref,
    upd, small_ref,
    hid, tgt, wv, pick, perm, xc, xcb, wanted, crecv, part, hrecv, frecv, xg, xgt, df, gs, gr,
    owner, stc, str_, stat, mx, mxr, dpr, sprd, lsem, ss, rs,
):
    t = lax.axis_index("tp")
    d = lax.axis_index("dp")
    y, c = t // 2, t % 2
    z, x = d // 4, d % 4
    sent = {}

    def at(y=y, c=c, z=z, x=x):
        return {"tp": (y % 4) * 2 + c, "dp": (z % 4) * 4 + x % 4}

    sibling = at(c=1 - c)

    def send(name, src, dst, device):
        i = IDS[name]
        copy = pltpu.make_async_remote_copy(
            src_ref=src, dst_ref=dst, send_sem=ss.at[i], recv_sem=rs.at[i],
            device_id=device, device_id_type=pl.DeviceIdType.MESH,
        )
        copy.start()
        sent[name] = copy

    def settle(*which):
        for name in which or tuple(sent):
            sent.pop(name).wait_send()

    def got(name, ref):
        i = IDS[name]
        pltpu.make_async_remote_copy(
            src_ref=ref, dst_ref=ref, send_sem=ss.at[i], recv_sem=rs.at[i],
            device_id=sibling, device_id_type=pl.DeviceIdType.MESH,
        ).wait_recv()

    loads = [pltpu.make_async_copy(hid_hbm.at[l], hid.at[l], lsem.at[l]) for l in range(3)]
    loads.append(pltpu.make_async_copy(tgt_hbm, tgt, lsem.at[3]))
    weights = [[] for _ in range(4)]
    for g, step in enumerate((2, 1, 3, 0)):
        cols = pl.ds(pl.multiple_of(((y + step) % 4) * 2 * BLOCK, 2 * BLOCK), 2 * BLOCK)
        for zz in range(4):
            weights[g].append(
                pltpu.make_async_copy(
                    w_hbm.at[:, pl.ds(zz * 128, 128), cols], wv.at[zz, :, :, cols], lsem.at[4 + g * 4 + zz]
                )
            )
    for load in loads[:3]:
        load.start()
    barrier = pltpu.get_barrier_semaphore()
    for j in range(1, 8):
        pl.semaphore_signal(
            barrier, inc=1, device_id={"tp": (t + j) % 8, "dp": d}, device_id_type=pl.DeviceIdType.MESH
        )
    for j in range(1, 16):
        pl.semaphore_signal(
            barrier, inc=1, device_id={"tp": t, "dp": (d + j) % 16}, device_id_type=pl.DeviceIdType.MESH
        )

    counts = counts_ref[...].astype(F32)
    counts8 = jnp.broadcast_to(counts, (8, REQS))
    expand = (iota((REQS, SLOTS), 1) >> 3 == iota((REQS, SLOTS), 0)).astype(F32)
    before = (iota((REQS, REQS), 0) < iota((REQS, REQS), 1)).astype(F32)
    start8 = jnp.dot(counts8, before, precision=EXACT, preferred_element_type=F32)
    count_slot = jnp.dot(counts8, expand, precision=EXACT, preferred_element_type=F32)
    start_slot = jnp.dot(start8, expand, precision=EXACT, preferred_element_type=F32)
    inside = iota((8, SLOTS), 1) & 7
    rank8 = (start_slot + 0.5).astype(I32) + inside
    rank8 = jnp.where(inside < (count_slot + 0.5).astype(I32), rank8, -1)
    rank = rank8[0:1, :]

    @pl.loop(0, LIVE // 272)
    def _(i):
        rows = pl.ds(pl.multiple_of(i * 272, 16), 272)
        hit = iota((272, SLOTS), 0) + i * 272 == rank
        pick[rows, :] = jnp.where(hit, 1.0, 0.0).astype(BF16)

    for load in loads[:3]:
        load.wait()
    loads[3].start()
    for load in weights[0]:
        load.start()

    @pl.loop(0, LIVE // 272)
    def _(i):
        rows = pl.ds(pl.multiple_of(i * 272, 16), 272)
        chosen = pick[rows, :]
        for l in range(3):
            got_rows = jnp.dot(chosen, hid[l], preferred_element_type=F32).astype(BF16)
            for q in range(4):
                cols = slice(q * FEATS + l * 128, q * FEATS + (l + 1) * 128)
                xc[rows, cols] = got_rows[:, q * 128 : (q + 1) * 128]

    for group in weights[1:]:
        for load in group:
            load.start()
    pl.semaphore_wait(barrier, 22)

    def feats(q):
        return pl.ds(pl.multiple_of((q % 4) * FEATS, 128), FEATS)

    def rows_of(q):
        return pl.ds(pl.multiple_of((q % 4) * LIVE, 16), LIVE)

    me = (z, x)

    def axis(h, step):
        return at(z=z + step) if h == 0 else at(x=x + step)

    own_copies = []

    def exchange(h, kept):
        for j in (1, 2, 3):
            send(f"x{h}{j}", kept.at[:, feats(me[h] + j)], xg.at[h, rows_of(me[h]), :], axis(h, j))
        own_copies.append(
            pltpu.make_async_copy(kept.at[:, feats(me[h])], xg.at[h, rows_of(me[h]), :], lsem.at[20 + h])
        )
        own_copies[h].start()

    exchange(0, xc)
    for load in weights[0]:
        load.wait()

    def forward(yy, core, dst, rows=slice(None)):
        column = ((yy % 4) * 2 + core) * BLOCK

        @pl.loop(0, 2)
        def _(i):
            cols = pl.ds(pl.multiple_of(column + i * PART, PART), PART)
            dst[rows, pl.ds(pl.multiple_of(i * PART, PART), PART)] = jnp.dot(
                xc[rows, :], wv[:, :, :, cols].reshape(4 * FEATS, PART), preferred_element_type=F32
            ).astype(dst.dtype)

    csend = [xcb.at[:, i * BLOCK : (i + 1) * BLOCK] for i in range(3)] + [hid.at[2, pl.ds(0, LIVE)]]
    ysend = [hid.at[i, pl.ds(0, LIVE)] for i in range(2)]
    yhalf = [hid.at[i, pl.ds(LIVE, HALF)] for i in range(2)]

    def to_sibling(i, step):
        forward(y + step, 1 - c, csend[i])
        send(f"c{i}", csend[i], crecv.at[i], sibling)

    up, down = at(y=y + 1), at(y=y + 3)
    top, low = pl.ds(0, HALF), pl.ds(HALF, HALF)
    for rows, name in ((top, "c0"), (low, "c0b")):
        forward(y + 2, 1 - c, csend[0], rows)
        send(name, csend[0].at[rows], crecv.at[0, rows], sibling)
        forward(y + 2, c, part.at[0], rows)
    for k, (rows, name, there, device) in enumerate(((top, "c0", "h+", up), (low, "c0b", "h-", down))):
        got(name, crecv.at[0, rows])
        yhalf[k][...] = (part[0, rows, :] + crecv[0, rows, :].astype(F32)).astype(BF16)
        send(there, yhalf[k], hrecv.at[k], device)
    for load in weights[1]:
        load.wait()
    to_sibling(1, 1)
    forward(y + 1, c, part.at[1])
    got("c1", crecv.at[1])
    ysend[0][low, :] = (part[1, low, :] + crecv[1, low, :].astype(F32)).astype(BF16)
    send("f+a", ysend[0].at[low], frecv.at[0, low], up)
    for load in weights[2]:
        load.wait()
    to_sibling(2, 3)
    forward(y + 3, c, part.at[2])
    got("c2", crecv.at[2])
    ysend[1][top, :] = (part[2, top, :] + crecv[2, top, :].astype(F32)).astype(BF16)
    send("f-a", ysend[1].at[top], frecv.at[1, top], down)

    place = iota((BLOCK, BLOCK), 1)
    source = ((place >> 5) & 3) * 128 + (place >> 7) * 32 + (place & 31)
    perm[...] = (iota((BLOCK, BLOCK), 0) == source).astype(F32).astype(BF16)

    settle("c0", "c0b", "c1", "c2")

    @pl.loop(0, LIVE // 272)
    def _(i):
        rows = pl.ds(pl.multiple_of(i * 272, 16), 272)
        for l in range(3):
            whole_rows = jnp.concatenate(
                [xc[rows, q * FEATS + l * 128 : q * FEATS + (l + 1) * 128] for q in range(4)], axis=1
            )
            swapped = jnp.dot(whole_rows, perm[...], preferred_element_type=F32).astype(BF16)
            for q in range(4):
                xcb[rows, q * FEATS + l * 128 : q * FEATS + (l + 1) * 128] = swapped[:, q * 128 : (q + 1) * 128]

    exchange(1, xcb)
    got("h+", hrecv.at[0])
    ysend[0][top, :] = (part[1, top, :] + crecv[1, top, :].astype(F32) + hrecv[0].astype(F32)).astype(BF16)
    send("f+b", ysend[0].at[top], frecv.at[0, top], up)
    got("h-", hrecv.at[1])
    ysend[1][low, :] = (part[2, low, :] + crecv[2, low, :].astype(F32) + hrecv[1].astype(F32)).astype(BF16)
    send("f-b", ysend[1].at[low], frecv.at[1, low], down)
    for load in weights[3]:
        load.wait()
    to_sibling(3, 0)
    forward(y, c, part.at[0])
    turned_expand = (iota((SLOTS, REQS), 0) >> 3 == iota((SLOTS, REQS), 1)).astype(F32).astype(BF16)
    loads[3].wait()

    @pl.loop(0, LIVE // 272)
    def _(i):
        rows = pl.ds(pl.multiple_of(i * 272, 16), 272)
        chosen = pick[rows, :]
        wanted[rows, :] = jnp.dot(chosen, tgt[...], preferred_element_type=F32).astype(BF16)
        owner[rows, :] = jnp.dot(chosen, turned_expand, preferred_element_type=F32)


    got("c3", crecv.at[3])
    stc[...] = jnp.zeros_like(stc)
    lane = iota((CHUNK, 128), 1)

    @pl.loop(0, LIVE // CHUNK)
    def _(i):
        rows = pl.ds(pl.multiple_of(i * CHUNK, CHUNK), CHUNK)
        part[0, rows, :] = part[0, rows, :] + crecv[3, rows, :].astype(F32)
        goal = wanted[rows, :].astype(F32)
        row = jnp.where(lane == 3, jnp.sum(goal * goal, axis=1, keepdims=True), 0.0)
        count = jnp.sum(owner[rows, :] * counts, axis=1, keepdims=True)
        stc[rows, :] = jnp.where(lane == 4, count, row)

    got("f+a", frecv.at[0, low])
    got("f-a", frecv.at[1, top])
    got("f+b", frecv.at[0, top])
    got("f-b", frecv.at[1, low])
    gains = gain_ref[pl.ds(t * 4, 4), :]
    gain = jnp.concatenate([gains[k : k + 1, :] for k in range(4)], axis=1)

    @pl.loop(0, LIVE // CHUNK)
    def _(i):
        rows = pl.ds(pl.multiple_of(i * CHUNK, CHUNK), CHUNK)
        joined = part[0, rows, :] + (frecv[0, rows, :].astype(F32) + frecv[1, rows, :].astype(F32))
        part[0, rows, :] = joined
        goal = wanted[rows, :].astype(F32)
        scaled = joined * gain
        sums = [joined * joined, scaled * scaled, scaled * goal]
        row = stc[rows, :]
        for k, term in enumerate(sums):
            row = jnp.where(lane == k, jnp.sum(term, axis=1, keepdims=True), row)
        stc[rows, :] = row

    turned = stc[...].T
    count_row = jnp.maximum(turned[4:5, :], 1.0)
    stat[pl.ds(t, 1)] = turned[None, 0:8, :]
    for j in range(1, 8):
        send(f"s{j}", stat.at[t], stat.at[t], {"tp": (t + j) % 8, "dp": d})
    for j in range(1, 8):
        got(f"s{j}", stat.at[(t + 8 - j) % 8])
    total = stat[0]
    for j in range(1, 8):
        total = total + stat[j]
    inv_rms = lax.rsqrt(total[0:1] / OUT + 1e-05)
    weight_row = 2.0 / (OUT * count_row)
    row_loss = (inv_rms * inv_rms * total[1:2] - 2.0 * inv_rms * total[2:3] + total[3:4]) / OUT
    inner = weight_row * (inv_rms * total[1:2] - total[2:3])
    str_[...] = jnp.zeros_like(str_)
    str_[0:1, :] = inv_rms
    str_[1:2, :] = inv_rms * weight_row
    str_[2:3, :] = inv_rms * inv_rms * inv_rms * inner / OUT
    str_[3:4, :] = row_loss
    stc[...] = str_[...].T

    def gradient(h):
        cols = slice(h * PART, (h + 1) * PART)

        @pl.loop(0, LIVE // CHUNK)
        def _(i):
            rows = pl.ds(pl.multiple_of(i * CHUNK, CHUNK), CHUNK)
            there = pl.ds(pl.multiple_of(me[h] * LIVE + i * CHUNK, CHUNK), CHUNK)
            joined = part[0, rows, cols]
            stats = stc[rows, :]
            err = joined * stats[:, 0:1] * gain[:, cols] - wanted[rows, cols].astype(F32)
            value = stats[:, 1:2] * gain[:, cols] * err - joined * stats[:, 2:3]
            df[h, t, there, :] = value.astype(BF16)

    def block(h, yy, place, half=None):
        start, size = (0, LIVE) if half is None else (half * HALF, HALF)
        rows = pl.ds(pl.multiple_of((place % 4) * LIVE + start, 16), size)
        return df.at[h, (yy % 4) * 2 + c, rows, :]

    def put(name, ref, device):
        send(name, ref, ref, device)

    up_first = (False, True)
    early_half = (1, 0)

    def put_y(h, second):
        if up_first[h] != second:
            put(f"y{h}+", block(h, y, me[h]), up)
        else:
            put(f"y{h}-", block(h, y, me[h]), down)

    def pass_y(h, second):
        if up_first[h] != second:
            got(f"y{h}+", block(h, y + 3, me[h]))
            put(f"yf{h}+", block(h, y + 3, me[h], 0), up)
        else:
            got(f"y{h}-", block(h, y + 1, me[h]))
            put(f"yf{h}-", block(h, y + 1, me[h], 1), down)

    def end_y(h, half):
        got(f"yf{h}" + "+-"[half], block(h, y + 2, me[h], half))

    def put_far(h, half):
        name = "e" if half == early_half[h] else "a"
        last = "" if name == "e" else "3"
        put(f"{name}{h}{last}+", block(h, y + 2, me[h], half), axis(h, 1))
        put(f"{name}{h}{last}-", block(h, y + 2, me[h], half), axis(h, 3))

    def pass_far(h):
        half = early_half[h]
        got(f"e{h}+", block(h, y + 2, me[h] + 3, half))
        put(f"af{h}3+", block(h, y + 2, me[h] + 3, half), axis(h, 1))
        got(f"e{h}-", block(h, y + 2, me[h] + 1, half))
        half = 1 - half
        got(f"a{h}3-", block(h, y + 2, me[h] + 1, half))
        put(f"af{h}3-", block(h, y + 2, me[h] + 1, half), axis(h, 3))
        got(f"a{h}3+", block(h, y + 2, me[h] + 3, half))
        share(h, 3, 0, 1, 3)

    def end_far(h):
        got(f"af{h}3+", block(h, y + 2, me[h] + 2, early_half[h]))
        got(f"af{h}3-", block(h, y + 2, me[h] + 2, 1 - early_half[h]))
        share(h, 3, 2)

    def put_axis(h, b):
        put(f"a{h}{b}+", block(h, y + STEP[b], me[h]), axis(h, 1))
        put(f"a{h}{b}-", block(h, y + STEP[b], me[h]), axis(h, 3))

    def pass_axis(h, b):
        got(f"a{h}{b}+", block(h, y + STEP[b], me[h] + 3))
        put(f"af{h}{b}+", block(h, y + STEP[b], me[h] + 3, 0), axis(h, 1))
        got(f"a{h}{b}-", block(h, y + STEP[b], me[h] + 1))
        put(f"af{h}{b}-", block(h, y + STEP[b], me[h] + 1, 1), axis(h, 3))

        share(h, b, 0, 1, 3)

    def end_axis(h, b):
        got(f"af{h}{b}+", block(h, y + STEP[b], me[h] + 2, 0))
        got(f"af{h}{b}-", block(h, y + STEP[b], me[h] + 2, 1))
        share(h, b, 2)

    def put_whole(h, *steps):
        for j in steps:
            put(f"v{h}{j}", block(h, y, me[h] + j), at(y=y + TURN[h]))

    def end_whole(h):
        for j in (1, 3, 2):
            got(f"v{h}{j}", block(h, y + 4 - TURN[h], me[h] + j))
            share(h, WHOLE[h], j)

    def share(h, b, *steps):
        for k in steps:
            put(f"d{h}{b}{k}", block(h, y + STEP[b], me[h] + k), sibling)

    def shared(h, b):
        for k in range(4):
            rows = rows_of(me[h] + k)
            got(f"d{h}{b}{k}", df.at[h, block_of(b, 1), rows, :])

    def block_of(b, o):
        return ((y + STEP[b]) % 4) * 2 + (c if o == 0 else 1 - c)

    def across(h, step):
        return axis(1 - h, step)

    def grad(h, b, o):
        if o == 1:
            shared(h, b)
        cols = pl.ds(pl.multiple_of(block_of(b, o) * PART, PART), PART)
        gs[h, :, cols] = jnp.dot(xgt[h], df[h, block_of(b, o)], preferred_element_type=F32).astype(BF16)
        for j in (2, 1, 3):
            rows = pl.ds(pl.multiple_of(((me[1 - h] + j) % 4) * ROWS_OUT, 32), ROWS_OUT)
            send(f"g{h}{b}{o}{j}", gs.at[h, rows, cols], gr.at[h, j - 1, :, cols], across(h, j))

    def finish(h, b, o):
        column = block_of(b, o) * BLOCK + h * PART
        cols = pl.ds(pl.multiple_of(block_of(b, o) * PART, PART), PART)
        wide = pl.ds(pl.multiple_of(column, PART), PART)
        for j in (1, 2, 3):
            got(f"g{h}{b}{o}{j}", gr.at[h, j - 1, :, cols])
        largest = jnp.zeros((1, PART), F32)
        for l in range(3):
            mine = pl.ds(pl.multiple_of(me[1 - h] * ROWS_OUT + l * 32, 32), 32)
            there = pl.ds(pl.multiple_of(x * 32, 32), 32)
            here = pl.ds(l * 32, 32)
            total = gs[h, mine, cols].astype(F32)
            for j in range(3):
                total = total + gr[h, j, here, cols].astype(F32)
            new = wv[z, l, there, wide].astype(F32) - learn_rate * total
            upd[l, :, wide] = new
            largest = jnp.maximum(largest, jnp.max(jnp.abs(new), axis=0, keepdims=True))
        for k in range(PART // 128):
            mx[pl.ds(column // 128 + k, 1), :] = largest[:, k * 128 : (k + 1) * 128]

    early = tuple(sent)
    for h in range(2):
        gradient(h)
        put_y(h, False)
        put_axis(h, 0)

    loss_rows = stc[0:LIVE, 3:4] * owner[...]
    request_loss = jnp.sum(loss_rows, axis=0, keepdims=True) / counts
    slots = slots_ref[...]
    places = (slots >> 7) * 8 + (slots & 127) - d * 8
    hit = places == iota((REQS, REQS), 0)
    by_place = jnp.sum(jnp.where(hit, request_loss, 0.0), axis=1, keepdims=True)
    eye = iota((REQS, REQS), 0) == iota((REQS, REQS), 1)
    by_place = jnp.sum(jnp.where(eye, by_place, 0.0), axis=0, keepdims=True)
    dpr[pl.ds(d, 1), 32:40, :] = jnp.broadcast_to(by_place[None], (1, 8, 128))

    settle(*early)
    for h in range(2):
        own_copies[h].wait()
        for j in (1, 2, 3):
            got(f"x{h}{j}", xg.at[h, rows_of(me[h] + 4 - j), :])

        @pl.loop(0, ALL // 128)
        def _(k):
            places = pl.ds(pl.multiple_of(k * 128, 128), 128)
            turned = xg[h, places, :].T
            for q in range(4):
                for l in range(3):
                    xgt[h, q * ROWS_OUT + l * 32 : q * ROWS_OUT + (l + 1) * 32, places] = turned[
                        l * 128 + q * 32 : l * 128 + (q + 1) * 32, :
                    ]

    for h in range(2):
        pass_axis(h, 0)
    for h in range(2):
        pass_y(h, False)
        put_axis(h, ALONG[h][1])
    for h in range(2):
        put_y(h, True)
    for h in range(2):
        end_axis(h, 0)
        grad(h, 0, 0)
    for h in range(2):
        end_y(h, early_half[h])
        put_far(h, early_half[h])
    for h in range(2):
        pass_y(h, True)
        put_whole(h, 1)
        share(h, WHOLE[h], 0)
    for h in range(2):
        grad(h, 0, 1)
    for h in range(2):
        pass_axis(h, ALONG[h][1])
    for h in range(2):
        end_y(h, 1 - early_half[h])
        put_far(h, 1 - early_half[h])
        put_whole(h, 3, 2)
    for h in range(2):
        end_axis(h, ALONG[h][1])
        grad(h, ALONG[h][1], 0)
    for h in range(2):
        grad(h, ALONG[h][1], 1)
    for h in range(2):
        pass_far(h)
    for h in range(2):
        finish(h, 0, 0)
        finish(h, 0, 1)
    for h in range(2):
        end_far(h)
        grad(h, 3, 0)
    for h in range(2):
        grad(h, 3, 1)
    for h in range(2):
        for o in range(2):
            finish(h, ALONG[h][1], o)
    for h in range(2):
        end_whole(h)
        grad(h, WHOLE[h], 0)
    for h in range(2):
        grad(h, WHOLE[h], 1)
    settle(*(name for name in tuple(sent) if name[0] != "g"))
    for h in range(2):
        for o in range(2):
            finish(h, 3, o)
    for h in range(2):
        for o in range(2):
            finish(h, WHOLE[h], o)

    for j in range(1, 8):
        send(f"m{j}", mx, mxr.at[j - 1], {"tp": (t + j) % 8, "dp": d})
    settle(*(name for name in tuple(sent) if name[0] == "g"))
    most = mx[...]
    for j in range(1, 8):
        got(f"m{j}", mxr.at[j - 1])
        most = jnp.maximum(most, mxr[j - 1])
    dpr[pl.ds(d, 1), 0:32, :] = most[None]
    for j in range(1, 16):
        send(f"n{j}", dpr.at[d], dpr.at[d], {"tp": t, "dp": (d + j) % 16})
    for j in range(1, 16):
        got(f"n{j}", dpr.at[(d + 16 - j) % 16])
    for j in range(16):
        most = jnp.maximum(most, dpr[j, 0:32, :])
        sprd[j * 8 : (j + 1) * 8, :] = dpr[j, 32:40, :]
    small_ref[0:32, :] = most + 1e-06
    lanes = iota((REQS, REQS), 1) == d * 8 + (iota((REQS, REQS), 0) & 7)
    mine = jnp.sum(jnp.where(lanes, sprd[...], 0.0), axis=1, keepdims=True)
    loss = jnp.sum(jnp.where(eye, mine, 0.0), axis=0, keepdims=True)
    small_ref[32:40, :] = jnp.broadcast_to(loss, (8, 128))
    settle()


def scaled(upd, small, loss_ref, serve_ref, scale_ref):
    scale_ref[...] = small[0:32, :]
    loss_ref[...] = small[32:33, :]
    for k in range(OUT // 128):
        cols = slice(k * 128, (k + 1) * 128)
        serve_ref[:, :, cols] = (upd[:, :, cols] / small[k : k + 1, :][None]).astype(BF16)


def shards(hidden_rows, target_rows, row_counts, seq_slot, joining_weight, norm_gain):
    any_spec = pl.BlockSpec(memory_space=pl.ANY)
    vmem = pl.BlockSpec(memory_space=pltpu.VMEM)
    n = len(IDS)
    upd, small = pl.pallas_call(
        kernel,
        out_shape=(
            jax.ShapeDtypeStruct((3, 32, OUT), F32),
            jax.ShapeDtypeStruct((40, 128), F32),
        ),
        in_specs=[any_spec, any_spec, vmem, vmem, any_spec, vmem],
        out_specs=(vmem, vmem),
        scratch_shapes=[
            pltpu.VMEM((3, SLOTS, BLOCK), BF16),
            pltpu.VMEM((SLOTS, BLOCK), BF16),
            pltpu.VMEM((4, 3, 128, OUT), BF16),
            pltpu.VMEM((LIVE, SLOTS), BF16),
            pltpu.VMEM((BLOCK, BLOCK), BF16),
            pltpu.VMEM((LIVE, 4 * FEATS), BF16),
            pltpu.VMEM((LIVE, 4 * FEATS), BF16),
            pltpu.VMEM((LIVE, BLOCK), BF16),
            pltpu.VMEM((4, LIVE, BLOCK), BF16),
            pltpu.VMEM((3, LIVE, BLOCK), F32),
            pltpu.VMEM((2, HALF, BLOCK), BF16),
            pltpu.VMEM((2, LIVE, BLOCK), BF16),
            pltpu.VMEM((2, ALL, FEATS), BF16),
            pltpu.VMEM((2, FEATS, ALL), BF16),
            pltpu.VMEM((2, 8, ALL, PART), BF16),
            pltpu.VMEM((2, FEATS, 8 * PART), BF16),
            pltpu.VMEM((2, 3, ROWS_OUT, 8 * PART), BF16),
            pltpu.VMEM((LIVE, REQS), F32),
            pltpu.VMEM((PAD, 128), F32),
            pltpu.VMEM((128, PAD), F32),
            pltpu.VMEM((8, 8, PAD), F32),
            pltpu.VMEM((32, 128), F32),
            pltpu.VMEM((7, 32, 128), F32),
            pltpu.VMEM((16, 40, 128), F32),
            pltpu.VMEM((REQS, 128), F32),
            pltpu.SemaphoreType.DMA((22,)),
            pltpu.SemaphoreType.DMA((n,)),
            pltpu.SemaphoreType.DMA((n,)),
        ],
        compiler_params=pltpu.CompilerParams(
            collective_id=0, has_side_effects=True, vmem_limit_bytes=64 * 2**20 - 2**18
        ),
        name="joining_step",
    )(
        jnp.transpose(hidden_rows, (1, 0, 2)),
        target_rows,
        row_counts.reshape(1, REQS),
        seq_slot.reshape(1, REQS),
        joining_weight,
        norm_gain.reshape(32, 128),
    )
    loss, serve, scale = pl.pallas_call(
        scaled,
        out_shape=(
            jax.ShapeDtypeStruct((1, REQS), F32),
            jax.ShapeDtypeStruct((3, 32, OUT), BF16),
            jax.ShapeDtypeStruct((32, 128), F32),
        ),
        in_specs=[vmem, vmem],
        out_specs=(vmem, vmem, vmem),
        name="scaled",
    )(upd, small)
    return loss.reshape(REQS), serve, scale.reshape(OUT)


def solution(mesh):
    placed = (P("dp", None, "tp"), P("dp", "tp"), P("dp"), P("dp"), P(None, "tp", None), P())
    return jax.shard_map(
        shards,
        mesh=mesh,
        in_specs=placed,
        out_specs=(P("dp"), P(None, ("tp", "dp"), None), P()),
        check_vma=False,
    )
```

```python
import jax
import jax.numpy as jnp
from jax import lax
from jax.experimental import pallas as pl
from jax.experimental.pallas import tpu as pltpu
from jax.sharding import PartitionSpec as P

learn_rate = 1.0

F32, BF16, I32 = jnp.float32, jnp.bfloat16, jnp.int32
EXACT = lax.Precision.HIGHEST
REQS, MOST, SLOTS, LIVE = 128, 8, 1024, 544
HALF = LIVE // 2
PAD = 640
ALL = 4 * LIVE
BLOCK, PART = 512, 256
FEATS = 384
OUT = 4096
ROWS_OUT = 96
CHUNK = 32


def iota(shape, dim):
    return lax.broadcasted_iota(I32, shape, dim)


def names():
    out = [f"x{h}{j}" for h in range(2) for j in (1, 2, 3)] + [f"c{i}" for i in range(4)]
    out += ["c0b", "h+", "h-", "f+a", "f+b", "f-a", "f-b"] + [f"s{j}" for j in range(1, 8)]
    for h in range(2):
        out += [f"{k}{h}{s}" for k in ("y", "yf", "e") for s in "+-"]
        out += [f"{k}{h}{b}{s}" for k in ("a", "af") for b in range(4) for s in "+-"]
        out += [f"v{h}{j}" for j in (1, 2, 3)] + [f"d{h}{b}{k}" for b in range(4) for k in range(4)]
        out += [f"g{h}{b}{o}{j}" for b in range(4) for o in range(2) for j in (1, 2, 3)]
    out += [f"m{j}" for j in range(1, 8)] + [f"n{j}" for j in range(1, 16)]
    return {name: i for i, name in enumerate(out)}


IDS = names()
STEP = (0, 3, 1, 2)
ALONG = ((0, 2, 3), (0, 1, 3))
WHOLE = (1, 2)
TURN = (1, 3)


def kernel(
    hid_hbm, tgt_hbm, counts_ref, slots_ref, w_hbm, gain_ref,
    upd, small_ref,
    hid, tgt, wv, pick, perm, xc, xcb, wanted, crecv, part, hrecv, frecv, xg, xgt, df, gs, gr,
    owner, stc, str_, stat, mx, mxr, dpr, sprd, lsem, ss, rs,
):
    t = lax.axis_index("tp")
    d = lax.axis_index("dp")
    y, c = t // 2, t % 2
    z, x = d // 4, d % 4
    sent = {}

    def at(y=y, c=c, z=z, x=x):
        return {"tp": (y % 4) * 2 + c, "dp": (z % 4) * 4 + x % 4}

    sibling = at(c=1 - c)

    def send(name, src, dst, device):
        i = IDS[name]
        copy = pltpu.make_async_remote_copy(
            src_ref=src, dst_ref=dst, send_sem=ss.at[i], recv_sem=rs.at[i],
            device_id=device, device_id_type=pl.DeviceIdType.MESH,
        )
        copy.start()
        sent[name] = copy

    def settle(*which):
        for name in which or tuple(sent):
            sent.pop(name).wait_send()

    def got(name, ref):
        i = IDS[name]
        pltpu.make_async_remote_copy(
            src_ref=ref, dst_ref=ref, send_sem=ss.at[i], recv_sem=rs.at[i],
            device_id=sibling, device_id_type=pl.DeviceIdType.MESH,
        ).wait_recv()

    loads = [pltpu.make_async_copy(hid_hbm.at[l], hid.at[l], lsem.at[l]) for l in range(3)]
    loads.append(pltpu.make_async_copy(tgt_hbm, tgt, lsem.at[3]))
    weights = [[] for _ in range(4)]
    for g, step in enumerate((2, 1, 3, 0)):
        cols = pl.ds(pl.multiple_of(((y + step) % 4) * 2 * BLOCK, 2 * BLOCK), 2 * BLOCK)
        for zz in range(4):
            for l in range(3):
                weights[g].append(
                    pltpu.make_async_copy(
                        w_hbm.at[l, pl.ds(zz * 128, 128), cols],
                        wv.at[pl.ds(zz * FEATS + l * 128, 128), cols],
                        lsem.at[4 + g * 12 + zz * 3 + l],
                    )
                )
    for load in loads[:3]:
        load.start()
    barrier = pltpu.get_barrier_semaphore()
    for j in range(1, 8):
        pl.semaphore_signal(
            barrier, inc=1, device_id={"tp": (t + j) % 8, "dp": d}, device_id_type=pl.DeviceIdType.MESH
        )
    for j in range(1, 16):
        pl.semaphore_signal(
            barrier, inc=1, device_id={"tp": t, "dp": (d + j) % 16}, device_id_type=pl.DeviceIdType.MESH
        )

    counts = counts_ref[...].astype(F32)
    counts8 = jnp.broadcast_to(counts, (8, REQS))
    expand = (iota((REQS, SLOTS), 1) >> 3 == iota((REQS, SLOTS), 0)).astype(F32)
    before = (iota((REQS, REQS), 0) < iota((REQS, REQS), 1)).astype(F32)
    start8 = jnp.dot(counts8, before, precision=EXACT, preferred_element_type=F32)
    count_slot = jnp.dot(counts8, expand, precision=EXACT, preferred_element_type=F32)
    start_slot = jnp.dot(start8, expand, precision=EXACT, preferred_element_type=F32)
    inside = iota((8, SLOTS), 1) & 7
    rank8 = (start_slot + 0.5).astype(I32) + inside
    rank8 = jnp.where(inside < (count_slot + 0.5).astype(I32), rank8, -1)
    rank = rank8[0:1, :]

    @pl.loop(0, LIVE // 272)
    def _(i):
        rows = pl.ds(pl.multiple_of(i * 272, 16), 272)
        hit = iota((272, SLOTS), 0) + i * 272 == rank
        pick[rows, :] = jnp.where(hit, 1.0, 0.0).astype(BF16)

    for load in loads[:3]:
        load.wait()
    loads[3].start()
    for load in weights[0]:
        load.start()

    @pl.loop(0, LIVE // 272)
    def _(i):
        rows = pl.ds(pl.multiple_of(i * 272, 16), 272)
        chosen = pick[rows, :]
        for l in range(3):
            got_rows = jnp.dot(chosen, hid[l], preferred_element_type=F32).astype(BF16)
            for q in range(4):
                cols = slice(q * FEATS + l * 128, q * FEATS + (l + 1) * 128)
                xc[rows, cols] = got_rows[:, q * 128 : (q + 1) * 128]

    for group in weights[1:]:
        for load in group:
            load.start()
    pl.semaphore_wait(barrier, 22)

    def feats(q):
        return pl.ds(pl.multiple_of((q % 4) * FEATS, 128), FEATS)

    def rows_of(q):
        return pl.ds(pl.multiple_of((q % 4) * LIVE, 16), LIVE)

    me = (z, x)

    def axis(h, step):
        return at(z=z + step) if h == 0 else at(x=x + step)

    own_copies = []

    def exchange(h, kept):
        for j in (1, 2, 3):
            send(f"x{h}{j}", kept.at[:, feats(me[h] + j)], xg.at[h, rows_of(me[h]), :], axis(h, j))
        own_copies.append(
            pltpu.make_async_copy(kept.at[:, feats(me[h])], xg.at[h, rows_of(me[h]), :], lsem.at[52 + h])
        )
        own_copies[h].start()

    for load in weights[0]:
        load.wait()

    def forward(yy, core, dst, rows=slice(None)):
        column = ((yy % 4) * 2 + core) * BLOCK

        @pl.loop(0, 2)
        def _(i):
            cols = pl.ds(pl.multiple_of(column + i * PART, PART), PART)
            dst[rows, pl.ds(pl.multiple_of(i * PART, PART), PART)] = jnp.dot(
                xc[rows, :], wv[:, cols], preferred_element_type=F32
            ).astype(dst.dtype)

    csend = [xcb.at[:, i * BLOCK : (i + 1) * BLOCK] for i in range(3)] + [hid.at[2, pl.ds(0, LIVE)]]
    ysend = [hid.at[i, pl.ds(0, LIVE)] for i in range(2)]
    yhalf = [hid.at[i, pl.ds(LIVE, HALF)] for i in range(2)]

    def to_sibling(i, step):
        forward(y + step, 1 - c, csend[i])
        send(f"c{i}", csend[i], crecv.at[i], sibling)

    up, down = at(y=y + 1), at(y=y + 3)
    top, low = pl.ds(0, HALF), pl.ds(HALF, HALF)
    for rows, name in ((top, "c0"), (low, "c0b")):
        forward(y + 2, 1 - c, csend[0], rows)
        send(name, csend[0].at[rows], crecv.at[0, rows], sibling)
        forward(y + 2, c, part.at[0], rows)
    for k, (rows, name, there, device) in enumerate(((top, "c0", "h+", up), (low, "c0b", "h-", down))):
        got(name, crecv.at[0, rows])
        yhalf[k][...] = (part[0, rows, :] + crecv[0, rows, :].astype(F32)).astype(BF16)
        send(there, yhalf[k], hrecv.at[k], device)
    exchange(0, xc)
    for load in weights[1]:
        load.wait()
    to_sibling(1, 1)
    forward(y + 1, c, part.at[1])
    got("c1", crecv.at[1])
    ysend[0][low, :] = (part[1, low, :] + crecv[1, low, :].astype(F32)).astype(BF16)
    send("f+a", ysend[0].at[low], frecv.at[0, low], up)
    for load in weights[2]:
        load.wait()
    to_sibling(2, 3)
    forward(y + 3, c, part.at[2])
    got("c2", crecv.at[2])
    ysend[1][top, :] = (part[2, top, :] + crecv[2, top, :].astype(F32)).astype(BF16)
    send("f-a", ysend[1].at[top], frecv.at[1, top], down)

    place = iota((BLOCK, BLOCK), 1)
    source = ((place >> 5) & 3) * 128 + (place >> 7) * 32 + (place & 31)
    perm[...] = (iota((BLOCK, BLOCK), 0) == source).astype(F32).astype(BF16)

    settle("c0", "c0b", "c1", "c2")

    @pl.loop(0, LIVE // 272)
    def _(i):
        rows = pl.ds(pl.multiple_of(i * 272, 16), 272)
        for l in range(3):
            whole_rows = jnp.concatenate(
                [xc[rows, q * FEATS + l * 128 : q * FEATS + (l + 1) * 128] for q in range(4)], axis=1
            )
            swapped = jnp.dot(whole_rows, perm[...], preferred_element_type=F32).astype(BF16)
            for q in range(4):
                xcb[rows, q * FEATS + l * 128 : q * FEATS + (l + 1) * 128] = swapped[:, q * 128 : (q + 1) * 128]

    exchange(1, xcb)
    got("h+", hrecv.at[0])
    ysend[0][top, :] = (part[1, top, :] + crecv[1, top, :].astype(F32) + hrecv[0].astype(F32)).astype(BF16)
    send("f+b", ysend[0].at[top], frecv.at[0, top], up)
    got("h-", hrecv.at[1])
    ysend[1][low, :] = (part[2, low, :] + crecv[2, low, :].astype(F32) + hrecv[1].astype(F32)).astype(BF16)
    send("f-b", ysend[1].at[low], frecv.at[1, low], down)
    for load in weights[3]:
        load.wait()
    to_sibling(3, 0)
    forward(y, c, part.at[0])
    turned_expand = (iota((SLOTS, REQS), 0) >> 3 == iota((SLOTS, REQS), 1)).astype(F32).astype(BF16)
    loads[3].wait()

    @pl.loop(0, LIVE // 272)
    def _(i):
        rows = pl.ds(pl.multiple_of(i * 272, 16), 272)
        chosen = pick[rows, :]
        wanted[rows, :] = jnp.dot(chosen, tgt[...], preferred_element_type=F32).astype(BF16)
        owner[rows, :] = jnp.dot(chosen, turned_expand, preferred_element_type=F32)


    got("c3", crecv.at[3])
    stc[...] = jnp.zeros_like(stc)
    lane = iota((CHUNK, 128), 1)

    @pl.loop(0, LIVE // CHUNK)
    def _(i):
        rows = pl.ds(pl.multiple_of(i * CHUNK, CHUNK), CHUNK)
        part[0, rows, :] = part[0, rows, :] + crecv[3, rows, :].astype(F32)
        goal = wanted[rows, :].astype(F32)
        row = jnp.where(lane == 3, jnp.sum(goal * goal, axis=1, keepdims=True), 0.0)
        count = jnp.sum(owner[rows, :] * counts, axis=1, keepdims=True)
        stc[rows, :] = jnp.where(lane == 4, count, row)

    got("f+a", frecv.at[0, low])
    got("f-a", frecv.at[1, top])
    got("f+b", frecv.at[0, top])
    got("f-b", frecv.at[1, low])
    gains = gain_ref[pl.ds(t * 4, 4), :]
    gain = jnp.concatenate([gains[k : k + 1, :] for k in range(4)], axis=1)

    @pl.loop(0, LIVE // CHUNK)
    def _(i):
        rows = pl.ds(pl.multiple_of(i * CHUNK, CHUNK), CHUNK)
        joined = part[0, rows, :] + (frecv[0, rows, :].astype(F32) + frecv[1, rows, :].astype(F32))
        part[0, rows, :] = joined
        goal = wanted[rows, :].astype(F32)
        scaled = joined * gain
        sums = [joined * joined, scaled * scaled, scaled * goal]
        row = stc[rows, :]
        for k, term in enumerate(sums):
            row = jnp.where(lane == k, jnp.sum(term, axis=1, keepdims=True), row)
        stc[rows, :] = row

    turned = stc[...].T
    count_row = jnp.maximum(turned[4:5, :], 1.0)
    stat[pl.ds(t, 1)] = turned[None, 0:8, :]
    for j in range(1, 8):
        send(f"s{j}", stat.at[t], stat.at[t], {"tp": (t + j) % 8, "dp": d})
    for j in range(1, 8):
        got(f"s{j}", stat.at[(t + 8 - j) % 8])
    total = stat[0]
    for j in range(1, 8):
        total = total + stat[j]
    inv_rms = lax.rsqrt(total[0:1] / OUT + 1e-05)
    weight_row = 2.0 / (OUT * count_row)
    row_loss = (inv_rms * inv_rms * total[1:2] - 2.0 * inv_rms * total[2:3] + total[3:4]) / OUT
    inner = weight_row * (inv_rms * total[1:2] - total[2:3])
    str_[...] = jnp.zeros_like(str_)
    str_[0:1, :] = inv_rms
    str_[1:2, :] = inv_rms * weight_row
    str_[2:3, :] = inv_rms * inv_rms * inv_rms * inner / OUT
    str_[3:4, :] = row_loss
    stc[...] = str_[...].T

    def gradient(h):
        cols = slice(h * PART, (h + 1) * PART)

        @pl.loop(0, LIVE // CHUNK)
        def _(i):
            rows = pl.ds(pl.multiple_of(i * CHUNK, CHUNK), CHUNK)
            there = pl.ds(pl.multiple_of(me[h] * LIVE + i * CHUNK, CHUNK), CHUNK)
            joined = part[0, rows, cols]
            stats = stc[rows, :]
            err = joined * stats[:, 0:1] * gain[:, cols] - wanted[rows, cols].astype(F32)
            value = stats[:, 1:2] * gain[:, cols] * err - joined * stats[:, 2:3]
            df[h, t, there, :] = value.astype(BF16)

    def block(h, yy, place, half=None):
        start, size = (0, LIVE) if half is None else (half * HALF, HALF)
        rows = pl.ds(pl.multiple_of((place % 4) * LIVE + start, 16), size)
        return df.at[h, (yy % 4) * 2 + c, rows, :]

    def put(name, ref, device):
        send(name, ref, ref, device)

    up_first = (False, True)
    early_half = (1, 0)

    def put_y(h, second):
        if up_first[h] != second:
            put(f"y{h}+", block(h, y, me[h]), up)
        else:
            put(f"y{h}-", block(h, y, me[h]), down)

    def pass_y(h, second):
        if up_first[h] != second:
            got(f"y{h}+", block(h, y + 3, me[h]))
            put(f"yf{h}+", block(h, y + 3, me[h], 0), up)
        else:
            got(f"y{h}-", block(h, y + 1, me[h]))
            put(f"yf{h}-", block(h, y + 1, me[h], 1), down)

    def end_y(h, half):
        got(f"yf{h}" + "+-"[half], block(h, y + 2, me[h], half))

    def put_far(h, half):
        name = "e" if half == early_half[h] else "a"
        last = "" if name == "e" else "3"
        put(f"{name}{h}{last}+", block(h, y + 2, me[h], half), axis(h, 1))
        put(f"{name}{h}{last}-", block(h, y + 2, me[h], half), axis(h, 3))

    def pass_far(h):
        half = early_half[h]
        got(f"e{h}+", block(h, y + 2, me[h] + 3, half))
        put(f"af{h}3+", block(h, y + 2, me[h] + 3, half), axis(h, 1))
        got(f"e{h}-", block(h, y + 2, me[h] + 1, half))
        half = 1 - half
        got(f"a{h}3-", block(h, y + 2, me[h] + 1, half))
        put(f"af{h}3-", block(h, y + 2, me[h] + 1, half), axis(h, 3))
        got(f"a{h}3+", block(h, y + 2, me[h] + 3, half))
        share(h, 3, 0, 1, 3)

    def end_far(h):
        got(f"af{h}3+", block(h, y + 2, me[h] + 2, early_half[h]))
        got(f"af{h}3-", block(h, y + 2, me[h] + 2, 1 - early_half[h]))
        share(h, 3, 2)

    def put_axis(h, b):
        put(f"a{h}{b}+", block(h, y + STEP[b], me[h]), axis(h, 1))
        put(f"a{h}{b}-", block(h, y + STEP[b], me[h]), axis(h, 3))

    def pass_axis(h, b):
        got(f"a{h}{b}+", block(h, y + STEP[b], me[h] + 3))
        put(f"af{h}{b}+", block(h, y + STEP[b], me[h] + 3, 0), axis(h, 1))
        got(f"a{h}{b}-", block(h, y + STEP[b], me[h] + 1))
        put(f"af{h}{b}-", block(h, y + STEP[b], me[h] + 1, 1), axis(h, 3))

        share(h, b, 0, 1, 3)

    def end_axis(h, b):
        got(f"af{h}{b}+", block(h, y + STEP[b], me[h] + 2, 0))
        got(f"af{h}{b}-", block(h, y + STEP[b], me[h] + 2, 1))
        share(h, b, 2)

    def put_whole(h, *steps):
        for j in steps:
            put(f"v{h}{j}", block(h, y, me[h] + j), at(y=y + TURN[h]))

    def end_whole(h):
        for j in (1, 3, 2):
            got(f"v{h}{j}", block(h, y + 4 - TURN[h], me[h] + j))
            share(h, WHOLE[h], j)

    def share(h, b, *steps):
        for k in steps:
            put(f"d{h}{b}{k}", block(h, y + STEP[b], me[h] + k), sibling)

    def shared(h, b):
        for k in range(4):
            rows = rows_of(me[h] + k)
            got(f"d{h}{b}{k}", df.at[h, block_of(b, 1), rows, :])

    def block_of(b, o):
        return ((y + STEP[b]) % 4) * 2 + (c if o == 0 else 1 - c)

    def across(h, step):
        return axis(1 - h, step)

    def grad(h, b, o):
        if o == 1:
            shared(h, b)
        cols = pl.ds(pl.multiple_of(block_of(b, o) * PART, PART), PART)
        gs[h, :, cols] = jnp.dot(xgt[h], df[h, block_of(b, o)], preferred_element_type=F32).astype(BF16)
        for j in (2, 1, 3):
            rows = pl.ds(pl.multiple_of(((me[1 - h] + j) % 4) * ROWS_OUT, 32), ROWS_OUT)
            send(f"g{h}{b}{o}{j}", gs.at[h, rows, cols], gr.at[h, j - 1, :, cols], across(h, j))

    def finish(h, b, o):
        column = block_of(b, o) * BLOCK + h * PART
        cols = pl.ds(pl.multiple_of(block_of(b, o) * PART, PART), PART)
        wide = pl.ds(pl.multiple_of(column, PART), PART)
        for j in (1, 2, 3):
            got(f"g{h}{b}{o}{j}", gr.at[h, j - 1, :, cols])
        largest = jnp.zeros((1, PART), F32)
        for l in range(3):
            mine = pl.ds(pl.multiple_of(me[1 - h] * ROWS_OUT + l * 32, 32), 32)
            there = pl.ds(pl.multiple_of(z * FEATS + l * 128 + x * 32, 32), 32)
            here = pl.ds(l * 32, 32)
            total = gs[h, mine, cols].astype(F32)
            for j in range(3):
                total = total + gr[h, j, here, cols].astype(F32)
            new = wv[there, wide].astype(F32) - learn_rate * total
            upd[l, :, wide] = new
            largest = jnp.maximum(largest, jnp.max(jnp.abs(new), axis=0, keepdims=True))
        for k in range(PART // 128):
            mx[pl.ds(column // 128 + k, 1), :] = largest[:, k * 128 : (k + 1) * 128]

    early = tuple(sent)
    for h in range(2):
        gradient(h)
        put_y(h, False)
        put_axis(h, 0)

    loss_rows = stc[0:LIVE, 3:4] * owner[...]
    request_loss = jnp.sum(loss_rows, axis=0, keepdims=True) / counts
    slots = slots_ref[...]
    places = (slots >> 7) * 8 + (slots & 127) - d * 8
    hit = places == iota((REQS, REQS), 0)
    by_place = jnp.sum(jnp.where(hit, request_loss, 0.0), axis=1, keepdims=True)
    eye = iota((REQS, REQS), 0) == iota((REQS, REQS), 1)
    by_place = jnp.sum(jnp.where(eye, by_place, 0.0), axis=0, keepdims=True)
    dpr[pl.ds(d, 1), 32:40, :] = jnp.broadcast_to(by_place[None], (1, 8, 128))

    settle(*early)
    for h in range(2):
        own_copies[h].wait()
        for j in (1, 2, 3):
            got(f"x{h}{j}", xg.at[h, rows_of(me[h] + 4 - j), :])

        @pl.loop(0, ALL // 128)
        def _(k):
            places = pl.ds(pl.multiple_of(k * 128, 128), 128)
            turned = xg[h, places, :].T
            for q in range(4):
                for l in range(3):
                    xgt[h, q * ROWS_OUT + l * 32 : q * ROWS_OUT + (l + 1) * 32, places] = turned[
                        l * 128 + q * 32 : l * 128 + (q + 1) * 32, :
                    ]

    for h in range(2):
        pass_axis(h, 0)
    for h in range(2):
        pass_y(h, False)
        put_axis(h, ALONG[h][1])
    for h in range(2):
        put_y(h, True)
    for h in range(2):
        end_axis(h, 0)
        grad(h, 0, 0)
    for h in range(2):
        end_y(h, early_half[h])
        put_far(h, early_half[h])
    for h in range(2):
        pass_y(h, True)
        put_whole(h, 1)
        share(h, WHOLE[h], 0)
    for h in range(2):
        grad(h, 0, 1)
    for h in range(2):
        pass_axis(h, ALONG[h][1])
    for h in range(2):
        end_y(h, 1 - early_half[h])
        put_far(h, 1 - early_half[h])
        put_whole(h, 3, 2)
    for h in range(2):
        end_axis(h, ALONG[h][1])
        grad(h, ALONG[h][1], 0)
    for h in range(2):
        grad(h, ALONG[h][1], 1)
    for h in range(2):
        pass_far(h)
    for h in range(2):
        finish(h, 0, 0)
        finish(h, 0, 1)
    for h in range(2):
        end_far(h)
        grad(h, 3, 0)
    for h in range(2):
        grad(h, 3, 1)
    for h in range(2):
        for o in range(2):
            finish(h, ALONG[h][1], o)
    for h in range(2):
        end_whole(h)
        grad(h, WHOLE[h], 0)
    for h in range(2):
        grad(h, WHOLE[h], 1)
    settle(*(name for name in tuple(sent) if name[0] != "g"))
    for h in range(2):
        for o in range(2):
            finish(h, 3, o)
    for h in range(2):
        for o in range(2):
            finish(h, WHOLE[h], o)

    for j in range(1, 8):
        send(f"m{j}", mx, mxr.at[j - 1], {"tp": (t + j) % 8, "dp": d})
    settle(*(name for name in tuple(sent) if name[0] == "g"))
    most = mx[...]
    for j in range(1, 8):
        got(f"m{j}", mxr.at[j - 1])
        most = jnp.maximum(most, mxr[j - 1])
    dpr[pl.ds(d, 1), 0:32, :] = most[None]
    for j in range(1, 16):
        send(f"n{j}", dpr.at[d], dpr.at[d], {"tp": t, "dp": (d + j) % 16})
    for j in range(1, 16):
        got(f"n{j}", dpr.at[(d + 16 - j) % 16])
    for j in range(16):
        most = jnp.maximum(most, dpr[j, 0:32, :])
        sprd[j * 8 : (j + 1) * 8, :] = dpr[j, 32:40, :]
    small_ref[0:32, :] = most + 1e-06
    lanes = iota((REQS, REQS), 1) == d * 8 + (iota((REQS, REQS), 0) & 7)
    mine = jnp.sum(jnp.where(lanes, sprd[...], 0.0), axis=1, keepdims=True)
    loss = jnp.sum(jnp.where(eye, mine, 0.0), axis=0, keepdims=True)
    small_ref[32:40, :] = jnp.broadcast_to(loss, (8, 128))
    settle()


def scaled(upd, small, loss_ref, serve_ref, scale_ref):
    scale_ref[...] = small[0:32, :]
    loss_ref[...] = small[32:33, :]
    for k in range(OUT // 128):
        cols = slice(k * 128, (k + 1) * 128)
        serve_ref[:, :, cols] = (upd[:, :, cols] / small[k : k + 1, :][None]).astype(BF16)


def shards(hidden_rows, target_rows, row_counts, seq_slot, joining_weight, norm_gain):
    any_spec = pl.BlockSpec(memory_space=pl.ANY)
    vmem = pl.BlockSpec(memory_space=pltpu.VMEM)
    n = len(IDS)
    upd, small = pl.pallas_call(
        kernel,
        out_shape=(
            jax.ShapeDtypeStruct((3, 32, OUT), F32),
            jax.ShapeDtypeStruct((40, 128), F32),
        ),
        in_specs=[any_spec, any_spec, vmem, vmem, any_spec, vmem],
        out_specs=(vmem, vmem),
        scratch_shapes=[
            pltpu.VMEM((3, SLOTS, BLOCK), BF16),
            pltpu.VMEM((SLOTS, BLOCK), BF16),
            pltpu.VMEM((4 * FEATS, OUT), BF16),
            pltpu.VMEM((LIVE, SLOTS), BF16),
            pltpu.VMEM((BLOCK, BLOCK), BF16),
            pltpu.VMEM((LIVE, 4 * FEATS), BF16),
            pltpu.VMEM((LIVE, 4 * FEATS), BF16),
            pltpu.VMEM((LIVE, BLOCK), BF16),
            pltpu.VMEM((4, LIVE, BLOCK), BF16),
            pltpu.VMEM((3, LIVE, BLOCK), F32),
            pltpu.VMEM((2, HALF, BLOCK), BF16),
            pltpu.VMEM((2, LIVE, BLOCK), BF16),
            pltpu.VMEM((2, ALL, FEATS), BF16),
            pltpu.VMEM((2, FEATS, ALL), BF16),
            pltpu.VMEM((2, 8, ALL, PART), BF16),
            pltpu.VMEM((2, FEATS, 8 * PART), BF16),
            pltpu.VMEM((2, 3, ROWS_OUT, 8 * PART), BF16),
            pltpu.VMEM((LIVE, REQS), F32),
            pltpu.VMEM((PAD, 128), F32),
            pltpu.VMEM((128, PAD), F32),
            pltpu.VMEM((8, 8, PAD), F32),
            pltpu.VMEM((32, 128), F32),
            pltpu.VMEM((7, 32, 128), F32),
            pltpu.VMEM((16, 40, 128), F32),
            pltpu.VMEM((REQS, 128), F32),
            pltpu.SemaphoreType.DMA((54,)),
            pltpu.SemaphoreType.DMA((n,)),
            pltpu.SemaphoreType.DMA((n,)),
        ],
        compiler_params=pltpu.CompilerParams(
            collective_id=0, has_side_effects=True, vmem_limit_bytes=64 * 2**20 - 2**18
        ),
        name="joining_step",
    )(
        jnp.transpose(hidden_rows, (1, 0, 2)),
        target_rows,
        row_counts.reshape(1, REQS),
        seq_slot.reshape(1, REQS),
        joining_weight,
        norm_gain.reshape(32, 128),
    )
    loss, serve, scale = pl.pallas_call(
        scaled,
        out_shape=(
            jax.ShapeDtypeStruct((1, REQS), F32),
            jax.ShapeDtypeStruct((3, 32, OUT), BF16),
            jax.ShapeDtypeStruct((32, 128), F32),
        ),
        in_specs=[vmem, vmem],
        out_specs=(vmem, vmem, vmem),
        name="scaled",
    )(upd, small)
    return loss.reshape(REQS), serve, scale.reshape(OUT)


def solution(mesh):
    placed = (P("dp", None, "tp"), P("dp", "tp"), P("dp"), P("dp"), P(None, "tp", None), P())
    return jax.shard_map(
        shards,
        mesh=mesh,
        in_specs=placed,
        out_specs=(P("dp"), P(None, ("tp", "dp"), None), P()),
        check_vma=False,
    )
```
